128 devices in a mesh: tile: 32 (over y, z, core), tm: 4 (over x).
Axes of the slice: x: 4, y: 4, z: 4, core: 2. Of those that a mesh axis runs over, the one named last changes fastest.
Arguments:
- features: bfloat16 [128, 128, 128, 128], P('tm', 'tile'), may hold values from -6 to 6
- norm_gain: float32 [128], replicated, may hold values from 0.5 to 2
- conv_weight: bfloat16 [128, 81], replicated, may hold values from -0.109375 to 0.109375
- colour_bias: float32 [3], replicated, may hold values from -3 to 3
- observed_frames: int32 [4, 32, 3], P('tm'), may hold values from 0 to 31, as said below
- observed_counts: int32 [4, 32], P('tm'), may hold values from 0 to 3, as said below
- key_rows: int32 [128, 17], P('tm'), may hold values from 0 to 31
- key_columns: int32 [128, 17], P('tm'), may hold values from 0 to 31
- key_visible: int32 [128, 17], P('tm'), may hold values 0 or 1
- position_table: bfloat16 [64, 1280], replicated, may hold values from -6 to 6
- patch_weight: bfloat16 [768, 1280], replicated, may hold values from -0.21875 to 0.21875
- layer_gain: float32 [1280], replicated, may hold values from 0.5 to 2
- up_weight: bfloat16 [1280, 2560], replicated, may hold values from -0.15625 to 0.15625
- down_weight: bfloat16 [2560, 1280], replicated, may hold values from -0.125 to 0.125
- head_weight: bfloat16 [1280, 272], replicated, may hold values from -0.15625 to 0.15625
Outputs:
- feature_grad: bfloat16 [128, 128, 128, 128], P('tm', 'tile')
The draws below stay inside these ranges and needn't reach their ends.
Inputs may be any that keep to these rules, and one draw needn't show every extreme that they name: `observed_frames`: slot j of pose device d in block g is used when j < observed_counts[g, d]; the used slots of one block name 32 different frames; unused slots hold 0. `observed_counts`: the counts of one block sum to 32; in every block some device holds 3.
All inputs are finite; a program needn't handle non-finite values. No bound on the sum of `key_visible` on one device may be relied on, other than what follows from the above.
Results may differ from the reference program's by a relative error of at most 0.015.
Values may be sent and summed in bfloat16 or wider, within the bound.
No kernel may reach another device: no remote copies, remote signals or barrier semaphores. Data moves between devices by JAX's collectives and lax.ppermute only.
A program may use at most 128 MiB of HBM per device.

```python
import math
import jax
import jax.numpy as jnp
from jax import lax

CH = 128
DP = 1280
HID = 2560
PATCH = 16
KP = 17
OBS_MOST = 3
FR_DEV = 32
COLS = 128
FRAMES = 128
HEIGHT = 128
NTOK = 64
SUB = 4
N_TILE = 32
N_TM = 4


def observation_plan(key):
    heavy_count = N_TILE // 4
    role_counts = jnp.concatenate((jnp.full((heavy_count,), OBS_MOST, jnp.int32), jnp.zeros((heavy_count * (OBS_MOST - 1),), jnp.int32), jnp.ones((N_TILE - heavy_count * OBS_MOST,), jnp.int32)))
    listings = []
    tallies = []
    for group in range(N_TM):
        group_key = jax.random.fold_in(jax.random.fold_in(key, 4242), group)
        first_key, second_key, third_key = jax.random.split(group_key, 3)
        group_counts = jax.random.permutation(first_key, role_counts).astype(jnp.int32)
        others = jax.random.permutation(second_key, FR_DEV - 1).astype(jnp.int32)
        chosen = jnp.concatenate((jnp.full((1,), FR_DEV - 1, jnp.int32), others[:N_TILE - 1]))
        frame_order = jax.random.permutation(third_key, chosen).astype(jnp.int32)
        starts = jnp.cumsum(group_counts) - group_counts
        slot_ids = jnp.arange(OBS_MOST, dtype=jnp.int32)
        places = jnp.minimum(starts[:, None] + slot_ids[None, :], N_TILE - 1)
        in_use = slot_ids[None, :] < group_counts[:, None]
        listings.append(jnp.where(in_use, frame_order[places], 0))
        tallies.append(group_counts)
    return (jnp.stack(listings).astype(jnp.int32), jnp.stack(tallies).astype(jnp.int32))


def draw_observed_frames(key, part):
    return observation_plan(key)[0]


def draw_observed_counts(key, part):
    return observation_plan(key)[1]


def set_ends(values, own_key, low, high):
    index_at = [jax.random.randint(jax.random.fold_in(own_key, axis), (), 0, length) for axis, length in enumerate(values.shape)]
    main_axis = values.shape.index(max(values.shape))
    beside = index_at[:main_axis] + [(index_at[main_axis] + 1) % values.shape[main_axis]] + index_at[main_axis + 1:]
    return values.at[tuple(index_at)].set(low).at[tuple(beside)].set(high)


def shard_levels(key, dims, cuts, smallest, high):
    def one(dim, blocks):
        steps = jax.random.uniform(jax.random.fold_in(jax.random.fold_in(key, 6), dim), (blocks,), jnp.float32, smallest / len(cuts), high / len(cuts))
        return jnp.repeat(jnp.exp(steps), dims[dim] // blocks).reshape((-1,) + (1,) * (len(dims) - dim - 1))

    factor_of = one(*cuts[0])
    for cut in cuts[1:]:
        factor_of = factor_of * one(*cut)
    return factor_of


def noise(stream_key, dims, scale, bound, cuts=(), kind=jnp.bfloat16):
    gain = shard_levels(stream_key, dims, cuts, -0.22, 0.18) if cuts else 1.0
    entries = jax.random.normal(stream_key, dims, jnp.float32) * scale * gain
    return jnp.minimum(jnp.maximum(entries, -bound), bound).astype(kind)


def setup_inputs(seed: int = 0) -> dict:
    streams_of = jax.random.split(jax.random.key(seed), 16)
    return {
        "features": noise(streams_of[0], (FRAMES, HEIGHT, COLS, CH), 1.0, 6.0, ((0, 4), (1, 32))),
        "norm_gain": jnp.clip(jnp.exp(jax.random.uniform(streams_of[1], (CH,), jnp.float32, math.log(0.5), math.log(2.0))), 0.5, 2.0),
        "conv_weight": noise(streams_of[2], (CH, 81), (27 * CH) ** -0.5, 0.109375),
        "colour_bias": noise(streams_of[3], (3,), 0.5, 3.0, (), jnp.float32),
        "observed_frames": draw_observed_frames(jax.random.fold_in(streams_of[15], 71), 0),
        "observed_counts": draw_observed_counts(jax.random.fold_in(streams_of[15], 71), 0),
        "key_rows": set_ends(jax.random.randint(streams_of[6], (FRAMES, KP), 0, HEIGHT // 4), jax.random.fold_in(streams_of[6], 1), 0, (HEIGHT // 4) - 1).astype(jnp.int32),
        "key_columns": set_ends(jax.random.randint(streams_of[7], (FRAMES, KP), 0, COLS // 4), jax.random.fold_in(streams_of[7], 1), 0, (COLS // 4) - 1).astype(jnp.int32),
        "key_visible": set_ends((jax.random.randint(streams_of[8], (FRAMES, KP), 0, 4) < 3).astype(jnp.int32), jax.random.fold_in(streams_of[8], 1), 0, 1),
        "position_table": noise(streams_of[9], (NTOK, DP), 1.0, 6.0),
        "patch_weight": noise(streams_of[10], (PATCH * PATCH * 3, DP), (PATCH * PATCH * 3) ** -0.5, 0.21875),
        "layer_gain": jnp.clip(jnp.exp(jax.random.uniform(streams_of[11], (DP,), jnp.float32, math.log(0.5), math.log(2.0))), 0.5, 2.0),
        "up_weight": noise(streams_of[12], (DP, HID), DP ** -0.5, 0.15625),
        "down_weight": noise(streams_of[13], (HID, DP), HID ** -0.5, 0.125),
        "head_weight": noise(streams_of[14], (DP, SUB * SUB * KP), DP ** -0.5, 0.15625),
    }


norm_eps = 1e-06
spread_sq = 8.0

def decoder_norm(features, norm_gain):
    widened = features.astype(jnp.float32)
    rescale = lax.rsqrt(lax.optimization_barrier(jnp.mean(widened * widened, axis=-1, keepdims=True)) + norm_eps)
    normed = widened * rescale
    return (normed, rescale, normed * norm_gain)

def silu_slope(preact):
    sigmoid = jax.nn.sigmoid(preact)
    return sigmoid * (1.0 + preact * (1.0 - sigmoid))

def gelu_slope(preact):
    return 0.5 * (1.0 + lax.erf(preact * 0.7071067811865476)) + preact * jnp.exp(-0.5 * preact * preact) * 0.3989422804014327

def tap_sum(partial_value, frame_count, row_count, column_count):
    summed = jnp.zeros((frame_count, row_count, column_count, 3), jnp.float32)
    for t_shift in range(3):
        for r_shift in range(3):
            for c_shift in range(3):
                tap_index = (t_shift * 3 + r_shift) * 3 + c_shift
                summed = summed + partial_value[t_shift:t_shift + frame_count, r_shift:r_shift + row_count, c_shift:c_shift + column_count, 3 * tap_index:3 * tap_index + 3]
    return summed

def tap_columns(padded, frame_count, row_count, column_count):
    pieces = []
    for t_shift in range(3):
        for r_shift in range(3):
            for c_shift in range(3):
                pieces.append(padded[2 - t_shift:2 - t_shift + frame_count, 2 - r_shift:2 - r_shift + row_count, 2 - c_shift:2 - c_shift + column_count, :])
    return jnp.concatenate(pieces, axis=-1)

def norm_back(features, norm_gain, activated_grad):
    normed, rescale, preact = decoder_norm(features, norm_gain)
    scaled = activated_grad * silu_slope(preact) * norm_gain
    return (rescale * (scaled - normed * lax.optimization_barrier(jnp.mean(scaled * normed, axis=-1, keepdims=True)))).astype(jnp.bfloat16)

def pose_grad(images, key_rows, key_columns, key_visible, weight, position_table, patch_weight, layer_gain, up_weight, down_weight, head_weight):
    frame_total, height, width, _ = images.shape
    grid_rows = height // PATCH
    grid_cols = width // PATCH
    token_total = grid_rows * grid_cols
    sub_size = PATCH // 4
    key_total = key_rows.shape[1]
    head_total = head_weight.shape[1]
    model_width = patch_weight.shape[1]
    patches = images.reshape(frame_total, grid_rows, PATCH, grid_cols, PATCH, 3).transpose(0, 1, 3, 2, 4, 5).reshape(frame_total * token_total, PATCH * PATCH * 3)
    embedded = jnp.dot(patches, patch_weight, preferred_element_type=jnp.float32).reshape(frame_total, token_total, model_width) + position_table.astype(jnp.float32)
    centred = embedded - lax.optimization_barrier(jnp.mean(embedded, axis=-1, keepdims=True))
    inverse = lax.rsqrt(lax.optimization_barrier(jnp.mean(centred * centred, axis=-1, keepdims=True)) + norm_eps)
    unit_rows = centred * inverse
    normed_tokens = (unit_rows * layer_gain).astype(jnp.bfloat16).reshape(-1, model_width)
    hidden_pre = jnp.dot(normed_tokens, up_weight, preferred_element_type=jnp.float32)
    hidden = jax.nn.gelu(hidden_pre, approximate=False).astype(jnp.bfloat16)
    block_out = embedded.reshape(-1, model_width) + jnp.dot(hidden, down_weight, preferred_element_type=jnp.float32)
    heatmap = jnp.dot(block_out.astype(jnp.bfloat16), head_weight, preferred_element_type=jnp.float32).reshape(frame_total, token_total, head_total)
    token_ids = jnp.arange(token_total, dtype=jnp.int32)
    column_ids = jnp.arange(head_total, dtype=jnp.int32)
    keypoint_ids = column_ids % key_total
    pixel_rows = ((token_ids // grid_cols)[:, None] * sub_size + (column_ids // (sub_size * key_total))[None, :]).astype(jnp.float32)
    pixel_cols = ((token_ids % grid_cols)[:, None] * sub_size + (column_ids // key_total % sub_size)[None, :]).astype(jnp.float32)
    row_goal = jnp.take(key_rows, keypoint_ids, axis=1).astype(jnp.float32)
    col_goal = jnp.take(key_columns, keypoint_ids, axis=1).astype(jnp.float32)
    row_gap = pixel_rows[None, :, :] - row_goal[:, None, :]
    col_gap = pixel_cols[None, :, :] - col_goal[:, None, :]
    target = jnp.exp(-(row_gap * row_gap + col_gap * col_gap) / spread_sq)
    loss_mask = jnp.take(key_visible, keypoint_ids, axis=1).astype(jnp.float32) * weight[:, None]
    heat_grad = ((heatmap - target) * loss_mask[:, None, :]).astype(jnp.bfloat16).reshape(-1, head_total)
    out_grad = jnp.dot(heat_grad, head_weight.T, preferred_element_type=jnp.float32)
    hidden_grad = jnp.dot(out_grad.astype(jnp.bfloat16), down_weight.T, preferred_element_type=jnp.float32)
    pre_grad = (hidden_grad * gelu_slope(hidden_pre)).astype(jnp.bfloat16)
    normed_grad = jnp.dot(pre_grad, up_weight.T, preferred_element_type=jnp.float32).reshape(frame_total, token_total, model_width)
    unit_grad = normed_grad * layer_gain
    embed_grad = out_grad.reshape(frame_total, token_total, model_width) + inverse * (unit_grad - lax.optimization_barrier(jnp.mean(unit_grad, axis=-1, keepdims=True)) - unit_rows * lax.optimization_barrier(jnp.mean(unit_grad * unit_rows, axis=-1, keepdims=True)))
    colour_grad = jnp.dot(embed_grad.astype(jnp.bfloat16).reshape(-1, model_width), patch_weight.T, preferred_element_type=jnp.float32).astype(jnp.bfloat16)
    return colour_grad.reshape(frame_total, grid_rows, grid_cols, PATCH, PATCH, 3).transpose(0, 1, 3, 2, 4, 5).reshape(frame_total, height, width, 3)

def reference(features, norm_gain, conv_weight, colour_bias, observed_frames, observed_counts, key_rows, key_columns, key_visible, position_table, patch_weight, layer_gain, up_weight, down_weight, head_weight):
    frames, height, width, channels = features.shape
    normed, rescale, preact = decoder_norm(features, norm_gain)
    activated = jax.nn.silu(preact).astype(jnp.bfloat16)
    partial_value = jnp.dot(activated.reshape(-1, channels), conv_weight, preferred_element_type=jnp.float32).reshape(frames, height, width, 81)
    partial_value = jnp.pad(partial_value, ((2, 0), (1, 1), (1, 1), (0, 0)))
    colours = (tap_sum(partial_value, frames, height, width) + colour_bias).astype(jnp.bfloat16)
    slot_ids = jnp.arange(observed_frames.shape[2], dtype=jnp.int32)
    in_use = slot_ids[None, None, :] < observed_counts[:, :, None]
    local_ids = jnp.arange(FR_DEV, dtype=jnp.int32)
    flags = jnp.any((observed_frames[:, :, :, None] == local_ids) & in_use[:, :, :, None], axis=(1, 2))
    weight = flags.reshape(-1).astype(jnp.float32)
    colour_grad = pose_grad(colours, key_rows, key_columns, key_visible, weight, position_table, patch_weight, layer_gain, up_weight, down_weight, head_weight)
    padded = jnp.pad(colour_grad, ((0, 2), (1, 1), (1, 1), (0, 0)))
    columns = tap_columns(padded, frames, height, width).reshape(-1, 81)
    activated_grad = jnp.dot(columns, conv_weight.T, preferred_element_type=jnp.float32).reshape(frames, height, width, channels)
    return norm_back(features, norm_gain, activated_grad)
```

```python
import functools

import jax
import jax.numpy as jnp
import ml_dtypes
import numpy as np
from jax import lax
from jax.experimental import pallas as pl
from jax.experimental.pallas import tpu as pltpu
from jax.sharding import PartitionSpec as P

CH = 128
DP = 1280
HID = 2560
PATCH = 16
KP = 17
HEAD = 272
COLS = 128
ROWS = 4
NORM_EPS = 1e-06
F32 = jnp.float32
BF16 = jnp.bfloat16


def slot_of(c, o, k):
    group = 3 * c + o
    if group < 8:
        return 8 * group + k
    return 8 * (k // 2) + 6 + k % 2


def make_selector():
    table = np.zeros((81, 2, ROWS, 256), np.float32)
    for tau in range(2):
        for r in range(ROWS):
            for f in range(4):
                a = tau + 2 - f
                if not 0 <= a <= 2:
                    continue
                for k in range(6):
                    b = r + 2 - k
                    if not 0 <= b <= 2:
                        continue
                    for c in range(3):
                        for o in range(3):
                            table[3 * (9 * a + 3 * b + c) + o, tau, r, 64 * f + slot_of(c, o, k)] = 1
    return table.reshape(81, 2048)


def make_pixel_order():
    table = np.zeros((768, 768), np.float32)
    for o in range(3):
        for pixel in range(256):
            table[256 * o + pixel, 3 * pixel + o] = 1
    return table


def make_key_spread():
    table = np.zeros((KP, HEAD), np.float32)
    table[np.arange(HEAD) % KP, np.arange(HEAD)] = 1
    return table


SELECTOR = make_selector().astype(ml_dtypes.bfloat16)
SELECTOR_T = np.ascontiguousarray(make_selector().T).astype(ml_dtypes.bfloat16)
PIXEL_ORDER = make_pixel_order().astype(ml_dtypes.bfloat16)
PIXEL_ORDER_T = np.ascontiguousarray(make_pixel_order().T).astype(ml_dtypes.bfloat16)
KEY_SPREAD = make_key_spread().astype(ml_dtypes.bfloat16)
MEAN_PAIR = (np.kron(np.eye(2), np.ones((CH, CH))) / CH).astype(ml_dtypes.bfloat16)


def dot(a, b):
    return jnp.dot(a, b, preferred_element_type=F32)


def dot_nt(a, b):
    return lax.dot_general(a, b, (((1,), (1,)), ((), ())), preferred_element_type=F32)


def roll(x, shift, axis):
    shift %= x.shape[axis]
    return pltpu.roll(x, shift, axis) if shift else x


def channel_mean(first, second, mean_pair):
    both = jnp.concatenate([first.astype(BF16), second.astype(BF16)], axis=1)
    means = dot(both, mean_pair)
    return means[:, :CH], means[:, CH:]


def lanes_of(shape):
    return lax.broadcasted_iota(jnp.int32, shape, len(shape) - 1)


def sublanes_of(shape):
    return lax.broadcasted_iota(jnp.int32, shape, len(shape) - 2)


def from_left(x):
    return jnp.where(lanes_of(x.shape) >= 1, roll(x, 1, x.ndim - 1), 0.0)


def from_right(x):
    return jnp.where(lanes_of(x.shape) < COLS - 1, roll(x, -1, x.ndim - 1), 0.0)


def activated_rows(feat_ref, frame, half_gain, mean_pair):
    acts = []
    for pair in range(ROWS // 2):
        xs = [feat_ref[frame, 2 * pair + i].astype(F32) for i in range(2)]
        means = channel_mean(xs[0] * xs[0], xs[1] * xs[1], mean_pair)
        for x, mean in zip(xs, means):
            half = x * lax.rsqrt(mean + NORM_EPS) * half_gain
            acts.append((half + half * jnp.tanh(half)).astype(BF16))
    return acts


def frame_sums(taps, out_ref, frame):
    groups = [taps[8 * g : 8 * g + 8] for g in range(8)]
    row = sublanes_of((8, COLS))
    groups.append(
        jnp.where(
            row < 2,
            roll(groups[0], 2, 0),
            jnp.where(row < 4, roll(groups[1], 4, 0), roll(groups[2], 6, 0)),
        )
    )
    for o in range(3):
        out_ref[frame, o] = from_left(groups[o]) + groups[3 + o] + from_right(groups[6 + o])


def spread_weights(conv_ref, sel_ref, weight_scr):
    conv = conv_ref[...]
    for block in range(8):
        weight_scr[CH * block : CH * block + CH, :] = dot(
            conv, sel_ref[:, 256 * block : 256 * block + 256]
        ).astype(BF16)


def conv_kernel(feat_ref, gain_ref, mean_ref, conv_ref, sel_ref, out_ref, weight_scr, carry):
    @pl.when(pl.program_id(0) == 0)
    def _():
        spread_weights(conv_ref, sel_ref, weight_scr)
        carry[...] = jnp.zeros_like(carry)

    half_gain = 0.5 * gain_ref[...]
    mean_pair = mean_ref[...]
    for pair in range(feat_ref.shape[0] // 2):
        acts = []
        for tau in range(2):
            acts += activated_rows(feat_ref, 2 * pair + tau, half_gain, mean_pair)
        sums = dot(jnp.concatenate(acts, axis=1), weight_scr[...])
        taps = (sums[:, :128] + carry[...]).T
        carry[...] = sums[:, 128:]
        for f in range(2):
            frame_sums(taps[64 * f : 64 * f + 64], out_ref, 2 * pair + f)


def tail_kernel(feat_ref, gain_ref, mean_ref, conv_ref, sel_ref, out_ref, weight_scr):
    spread_weights(conv_ref, sel_ref, weight_scr)
    half_gain = 0.5 * gain_ref[...]
    mean_pair = mean_ref[...]
    acts = []
    for tau in range(2):
        acts += activated_rows(feat_ref, tau, half_gain, mean_pair)
    taps = dot(jnp.concatenate(acts, axis=1), weight_scr[:, 128:]).T
    for f in range(2):
        frame_sums(taps[64 * f : 64 * f + 64], out_ref, f)


def whole(shape):
    return pl.BlockSpec(shape, lambda *_: (0,) * len(shape))


def conv_forward(features, gain, conv_weight, block):
    frames = features.shape[0]
    common = [whole((1, CH)), whole((256, 256)), whole((CH, 81)), whole((81, 2048))]
    consts = (gain, jnp.asarray(MEAN_PAIR), conv_weight, jnp.asarray(SELECTOR))
    tail = pl.pallas_call(
        tail_kernel,
        grid=(1,),
        in_specs=[pl.BlockSpec((2, ROWS, COLS, CH), lambda i: (frames // 2 - 1, 0, 0, 0))] + common,
        out_specs=whole((2, 3, 8, COLS)),
        out_shape=jax.ShapeDtypeStruct((2, 3, 8, COLS), F32),
        scratch_shapes=[pltpu.VMEM((1024, 256), BF16)],
        name="conv_tail",
    )(features, *consts)
    main = pl.pallas_call(
        conv_kernel,
        grid=(frames // block,),
        in_specs=[pl.BlockSpec((block, ROWS, COLS, CH), lambda i: (i, 0, 0, 0))] + common,
        out_specs=pl.BlockSpec((block, 3, 8, COLS), lambda i: (i, 0, 0, 0)),
        out_shape=jax.ShapeDtypeStruct((frames, 3, 8, COLS), F32),
        scratch_shapes=[pltpu.VMEM((1024, 256), BF16), pltpu.VMEM((COLS, 128), F32)],
        compiler_params=pltpu.CompilerParams(vmem_limit_bytes=32 * 1024 * 1024),
        cost_estimate=pl.CostEstimate(
            flops=2 * 16384 * 1024, bytes_accessed=5 * 1024 * 1024, transcendentals=2 * 2097152
        ),
        name="conv_main",
    )(features, *consts)
    return tail, main


def swap_blocks(x):
    row, group = sublanes_of(x.shape), lanes_of(x.shape) // 16
    for bit in (4, 2, 1):
        low = (row & bit) == 0
        same = low == ((group & bit) == 0)
        moved = jnp.where(
            low,
            roll(roll(x, -bit, 1), 16 * bit, 2),
            roll(roll(x, bit, 1), -16 * bit, 2),
        )
        x = jnp.where(same, x, moved)
    return x


def gather_patches(x_ref, bias_ref):
    row = sublanes_of((16, 8, COLS))
    zero = jnp.zeros((1, 8, COLS), F32)
    pieces = []
    for o in range(3):
        strips = x_ref[:, o].reshape(16, 2, 8, COLS)
        even = roll(strips[:, 0], -1, 1)
        odd = roll(strips[:, 1], 3, 1)
        even_next = jnp.concatenate([even[1:], zero], axis=0)
        odd_prior = jnp.concatenate([zero, odd[:-1]], axis=0)
        total = (
            jnp.where(row <= 4, even, jnp.where(row == 7, even_next, 0.0))
            + jnp.where(row >= 3, odd, jnp.where(row == 0, odd_prior, 0.0))
            + bias_ref[o]
        )
        blocks = swap_blocks(total).reshape(8, 2, 8, 128)
        for half in range(2):
            pieces.append(blocks[:, half].reshape(64, 128).astype(BF16))
    return jnp.concatenate(pieces, axis=1)


def scatter_patches(grad, out_ref):
    row = sublanes_of((16, 8, COLS))
    zero = jnp.zeros((1, 8, COLS), F32)
    for o in range(3):
        halves = [
            grad[:, 256 * o + 128 * half : 256 * o + 128 * half + 128].reshape(8, 1, 8, 128)
            for half in range(2)
        ]
        rows = swap_blocks(jnp.concatenate(halves, axis=1).reshape(16, 8, 128))
        down = roll(rows, 1, 1)
        up = roll(rows, -3, 1)
        down_prior = jnp.concatenate([zero, down[:-1]], axis=0)
        up_next = jnp.concatenate([up[1:], zero], axis=0)
        even = jnp.where(row == 0, down_prior, down)
        odd = jnp.where(row == 5, up_next, up)
        out_ref[:, o] = jnp.concatenate([even[:, None], odd[:, None]], axis=1).reshape(32, 8, COLS)


def normal_cdf(x):
    return 0.5 * (1.0 + lax.erf(x * 0.7071067811865476))


def pose_kernel(
    own_ref,
    bias_ref,
    x_ref,
    frames_ref,
    counts_ref,
    key_rows_ref,
    key_cols_ref,
    key_vis_ref,
    key_spread_ref,
    gain_ref,
    order_hbm,
    order_t_hbm,
    position_hbm,
    patch_hbm,
    up_hbm,
    down_hbm,
    head_hbm,
    out_ref,
    order,
    order_t,
    position,
    patch,
    up,
    down,
    head,
    hidden_pre,
    hidden,
    pre_grad,
    sems,
):
    pairs = [
        (order_hbm, order),
        (patch_hbm, patch),
        (position_hbm, position),
        (up_hbm, up),
        (down_hbm, down),
        (head_hbm, head),
        (order_t_hbm, order_t),
    ]
    copies = [pltpu.make_async_copy(src, dst, sems.at[i]) for i, (src, dst) in enumerate(pairs)]
    for copy in copies:
        copy.start()
    own = own_ref[0]

    slot = lanes_of((32, 3))
    diagonal = sublanes_of((32, 32)) == lanes_of((32, 32))
    counts = jnp.sum(jnp.where(diagonal, counts_ref[...], 0), axis=1, keepdims=True)
    hit = jnp.where((frames_ref[...] == own) & (slot < counts), 1.0, 0.0)
    weight = jnp.max(jnp.max(hit, axis=1, keepdims=True), axis=0, keepdims=True)
    mine = sublanes_of((32, HEAD)) == own
    spread = key_spread_ref[...]

    def own_keys(ref):
        table = dot(ref[...].astype(F32).astype(BF16), spread)
        return jnp.sum(jnp.where(mine, table, 0.0), axis=0, keepdims=True)

    token = sublanes_of((64, HEAD))
    column = lanes_of((64, HEAD))
    pixel_row = (token // 8) * 4 + column // (4 * KP)
    pixel_col = (token % 8) * 4 + (column // KP) % 4
    row_gap = pixel_row.astype(F32) - own_keys(key_rows_ref)
    col_gap = pixel_col.astype(F32) - own_keys(key_cols_ref)
    target = jnp.exp((row_gap * row_gap + col_gap * col_gap) * -0.125)
    mask = own_keys(key_vis_ref) * weight

    raw = gather_patches(x_ref, bias_ref)
    copies[0].wait()
    patches = dot(raw, order[...]).astype(BF16)
    copies[1].wait()
    copies[2].wait()
    embedded = dot(patches, patch[...]) + position[...].astype(F32)
    centred = embedded - jnp.mean(embedded, axis=-1, keepdims=True)
    inverse = lax.rsqrt(jnp.mean(centred * centred, axis=-1, keepdims=True) + NORM_EPS)
    unit_rows = centred * inverse
    gain = gain_ref[...]
    normed_tokens = (unit_rows * gain).astype(BF16)
    copies[3].wait()

    @pl.loop(0, HID // 256)
    def _(i):
        at = pl.ds(pl.multiple_of(i * 256, 256), 256)
        value = dot(normed_tokens, up[:, at])
        hidden_pre[:, at] = value
        hidden[:, at] = (value * normal_cdf(value)).astype(BF16)

    copies[4].wait()
    block = dot(hidden[...], down[...])
    block_round = (embedded + block).astype(BF16)
    copies[5].wait()
    heatmap = dot(block_round, head[...])
    heat_grad = ((heatmap - target) * mask).astype(BF16)
    out_grad = dot_nt(heat_grad, head[...])
    out_round = out_grad.astype(BF16)

    @pl.loop(0, HID // 256)
    def _(i):
        at = pl.ds(pl.multiple_of(i * 256, 256), 256)
        grad = dot_nt(out_round, down[at, :])
        pre = hidden_pre[:, at]
        slope = normal_cdf(pre) + pre * jnp.exp(-0.5 * pre * pre) * 0.3989422804014327
        pre_grad[:, at] = (grad * slope).astype(BF16)

    normed_grad = dot_nt(pre_grad[...], up[...])
    unit_grad = normed_grad * gain
    embed_grad = out_grad + inverse * (
        unit_grad
        - jnp.mean(unit_grad, axis=-1, keepdims=True)
        - unit_rows * jnp.mean(unit_grad * unit_rows, axis=-1, keepdims=True)
    )
    colour_grad = dot_nt(embed_grad.astype(BF16), patch[...]).astype(BF16)
    copies[6].wait()
    scatter_patches(dot(colour_grad, order_t[...]), out_ref)


def pose(own, bias, x, frames, counts, key_rows, key_cols, key_vis, gain, position, patch, up, down, head):
    smem = pl.BlockSpec(memory_space=pltpu.SMEM)
    vmem = pl.BlockSpec(memory_space=pltpu.VMEM)
    anywhere = pl.BlockSpec(memory_space=pl.ANY)
    return pl.pallas_call(
        pose_kernel,
        in_specs=[smem] * 2 + [vmem] * 8 + [anywhere] * 7,
        out_specs=vmem,
        out_shape=jax.ShapeDtypeStruct((32, 3, 8, COLS), F32),
        scratch_shapes=[
            pltpu.VMEM((768, 768), BF16),
            pltpu.VMEM((768, 768), BF16),
            pltpu.VMEM((64, DP), BF16),
            pltpu.VMEM((768, DP), BF16),
            pltpu.VMEM((DP, HID), BF16),
            pltpu.VMEM((HID, DP), BF16),
            pltpu.VMEM((DP, HEAD), BF16),
            pltpu.VMEM((64, HID), F32),
            pltpu.VMEM((64, HID), BF16),
            pltpu.VMEM((64, HID), BF16),
            pltpu.SemaphoreType.DMA((7,)),
        ],
        compiler_params=pltpu.CompilerParams(vmem_limit_bytes=48 * 1024 * 1024),
        cost_estimate=pl.CostEstimate(
            flops=2 * 64 * 15800000, bytes_accessed=17 * 1024 * 1024, transcendentals=64 * HID * 3
        ),
        name="pose",
    )(
        own,
        bias,
        x,
        frames,
        counts,
        key_rows,
        key_cols,
        key_vis,
        jnp.asarray(KEY_SPREAD),
        gain,
        jnp.asarray(PIXEL_ORDER),
        jnp.asarray(PIXEL_ORDER_T),
        position,
        patch,
        up,
        down,
        head,
    )


def frame_taps(groups):
    row = sublanes_of((8, COLS))
    taps = [from_right(g) for g in groups] + list(groups) + [from_left(g) for g in groups]
    last = taps.pop()
    for i in range(3):
        taps[i] = jnp.where(row >= 6, roll(last, 6 - 2 * i, 0), taps[i])
    return taps


def pair_taps(ref, frame):
    rows = []
    for f in range(2):
        rows += frame_taps([ref[frame + f, o] for o in range(3)])
    return jnp.concatenate(rows, axis=0).T


def back_kernel(
    feat_ref, grad_ref, next_ref, gain_ref, mean_ref, conv_ref, sel_ref, out_ref, weight_scr, carry
):
    step = pl.program_id(0)
    block = feat_ref.shape[0]

    @pl.when(step == 0)
    def _():
        conv = conv_ref[...]
        for i in range(8):
            weight_scr[:, CH * i : CH * i + CH] = dot_nt(
                sel_ref[256 * i : 256 * i + 256, :], conv
            ).astype(BF16)
        carry[...] = pair_taps(grad_ref, 0)

    gain = gain_ref[...]
    half_gain = 0.5 * gain
    mean_pair = mean_ref[...]
    for pair in range(block // 2):
        now = carry[...]
        if pair < block // 2 - 1:
            carry[...] = pair_taps(grad_ref, step * block + 2 * pair + 2)
        else:

            @pl.when(step < pl.num_programs(0) - 1)
            def _():
                carry[...] = pair_taps(grad_ref, (step + 1) * block)

            @pl.when(step == pl.num_programs(0) - 1)
            def _():
                carry[...] = pair_taps(next_ref, 0)

        taps = jnp.concatenate([now, carry[...]], axis=1).astype(BF16)
        grads = dot(taps, weight_scr[...])
        for tau in range(2):
            frame = 2 * pair + tau
            for half in range(ROWS // 2):
                rows = [2 * half, 2 * half + 1]
                xs = [feat_ref[frame, r].astype(F32) for r in rows]
                means = channel_mean(xs[0] * xs[0], xs[1] * xs[1], mean_pair)
                kept = []
                for x, mean, r in zip(xs, means, rows):
                    rescale = lax.rsqrt(mean + NORM_EPS)
                    normed = x * rescale
                    half_pre = normed * half_gain
                    sigma = 0.5 + 0.5 * jnp.tanh(half_pre)
                    slope = sigma * (1.0 + (half_pre + half_pre) * (1.0 - sigma)) * gain
                    at = CH * (ROWS * tau + r)
                    kept.append((rescale, normed, grads[:, at : at + CH] * slope))
                dots = channel_mean(kept[0][2] * kept[0][1], kept[1][2] * kept[1][1], mean_pair)
                for (rescale, normed, scaled), along, r in zip(kept, dots, rows):
                    out_ref[frame, r] = (rescale * (scaled - normed * along)).astype(BF16)


def conv_backward(features, grads, later, gain, conv_weight, block):
    frames = features.shape[0]
    return pl.pallas_call(
        back_kernel,
        grid=(frames // block,),
        in_specs=[
            pl.BlockSpec((block, ROWS, COLS, CH), lambda i: (i, 0, 0, 0)),
            whole((frames, 3, 8, COLS)),
            whole((2, 3, 8, COLS)),
            whole((1, CH)),
            whole((256, 256)),
            whole((CH, 81)),
            whole((2048, 81)),
        ],
        out_specs=pl.BlockSpec((block, ROWS, COLS, CH), lambda i: (i, 0, 0, 0)),
        out_shape=jax.ShapeDtypeStruct((frames, ROWS, COLS, CH), BF16),
        scratch_shapes=[pltpu.VMEM((256, 1024), BF16), pltpu.VMEM((COLS, 128), F32)],
        compiler_params=pltpu.CompilerParams(vmem_limit_bytes=32 * 1024 * 1024),
        cost_estimate=pl.CostEstimate(
            flops=2 * 16384 * 1024, bytes_accessed=9 * 1024 * 1024, transcendentals=2 * 2097152
        ),
        name="conv_back",
    )(features, grads, later, gain, jnp.asarray(MEAN_PAIR), conv_weight, jnp.asarray(SELECTOR_T))


def per_device(
    features,
    norm_gain,
    conv_weight,
    colour_bias,
    observed_frames,
    observed_counts,
    key_rows,
    key_columns,
    key_visible,
    position_table,
    patch_weight,
    layer_gain,
    up_weight,
    down_weight,
    head_weight,
):
    tm_count = lax.axis_size("tm")
    own = lax.axis_index("tile").reshape(1)
    gain = norm_gain.reshape(1, CH)
    tail, sums = conv_forward(features, gain, conv_weight, 8)
    prior = lax.ppermute(tail, "tm", [(i, i + 1) for i in range(tm_count - 1)])
    sums = sums.at[:2].add(prior)
    strips = lax.all_to_all(sums, "tile", 0, 0, tiled=True)
    colour_grad = pose(
        own,
        colour_bias,
        strips,
        observed_frames[0],
        observed_counts,
        key_rows,
        key_columns,
        key_visible,
        layer_gain.reshape(1, DP),
        position_table,
        patch_weight,
        up_weight,
        down_weight,
        head_weight,
    )
    grads = lax.all_to_all(colour_grad, "tile", 0, 0, tiled=True)
    later = lax.ppermute(grads[:2], "tm", [(i + 1, i) for i in range(tm_count - 1)])
    return conv_backward(features, grads, later, gain, conv_weight, 8)


def solution(mesh):
    in_specs = (
        P("tm", "tile", None, None),
        P(),
        P(),
        P(),
        P("tm", None, None),
        P("tm", None),
        P("tm", None),
        P("tm", None),
        P("tm", None),
        P(),
        P(),
        P(),
        P(),
        P(),
        P(),
    )
    return jax.shard_map(
        per_device,
        mesh=mesh,
        in_specs=in_specs,
        out_specs=P("tm", "tile", None, None),
        check_vma=False,
    )
```

```python
import jax
import jax.numpy as jnp
import ml_dtypes
import numpy as np
from jax import lax
from jax.experimental import pallas as pl
from jax.experimental.pallas import tpu as pltpu
from jax.sharding import PartitionSpec as P

CH = 128
DP = 1280
HID = 2560
PATCH = 16
KP = 17
HEAD = 272
COLS = 128
ROWS = 4
GROUP = 4
FORWARD_FRAMES = 8
BACK_FRAMES = 10
BACK_ROWS = 4
NORM_EPS = 1e-06
F32 = jnp.float32
BF16 = jnp.bfloat16


def slot_of(c, o, k):
    group = 3 * c + o
    if group < 8:
        return 8 * group + k
    return 8 * (k // 2) + 6 + k % 2


def make_selector():
    table = np.zeros((81, 2, ROWS, 256), np.float32)
    for tau in range(2):
        for r in range(ROWS):
            for f in range(4):
                a = tau + 2 - f
                if not 0 <= a <= 2:
                    continue
                for k in range(6):
                    b = r + 2 - k
                    if not 0 <= b <= 2:
                        continue
                    for c in range(3):
                        for o in range(3):
                            table[3 * (9 * a + 3 * b + c) + o, tau, r, 64 * f + slot_of(c, o, k)] = 1
    return table.reshape(81, 2048)


def make_pixel_order():
    table = np.zeros((768, 768), np.float32)
    for o in range(3):
        for pixel in range(256):
            table[256 * o + pixel, 3 * pixel + o] = 1
    return table


def make_key_spread():
    table = np.zeros((KP, HEAD), np.float32)
    table[np.arange(HEAD) % KP, np.arange(HEAD)] = 1
    return table


SELECTOR = make_selector().astype(ml_dtypes.bfloat16)
SELECTOR_T = np.ascontiguousarray(make_selector().T).astype(ml_dtypes.bfloat16)
PIXEL_ORDER = make_pixel_order().astype(ml_dtypes.bfloat16)
KEY_SPREAD = make_key_spread().astype(ml_dtypes.bfloat16)
MEAN_PAIR = (np.kron(np.eye(2), np.ones((CH, CH))) / CH).astype(ml_dtypes.bfloat16)


def dot(a, b):
    return jnp.dot(a, b, preferred_element_type=F32)


def dot_tn(a, b):
    return lax.dot_general(a, b, (((0,), (0,)), ((), ())), preferred_element_type=F32)


def dot_nt(a, b):
    return lax.dot_general(a, b, (((1,), (1,)), ((), ())), preferred_element_type=F32)


def roll(x, shift, axis):
    shift %= x.shape[axis]
    return pltpu.roll(x, shift, axis) if shift else x


def channel_means(values, mean_pair):
    rounded = [value.astype(BF16) for value in values]
    pairs = [jnp.concatenate(rounded[i : i + 2], axis=1) for i in range(0, len(values), 2)]
    means = dot(jnp.concatenate(pairs, axis=0), mean_pair)
    out = []
    for i in range(len(pairs)):
        rows = slice(COLS * i, COLS * i + COLS)
        out += [means[rows, :CH], means[rows, CH:]]
    return out


def lanes_of(shape):
    return lax.broadcasted_iota(jnp.int32, shape, len(shape) - 1)


def sublanes_of(shape):
    return lax.broadcasted_iota(jnp.int32, shape, len(shape) - 2)


def from_left(x):
    return jnp.where(lanes_of(x.shape) >= 1, roll(x, 1, x.ndim - 1), 0.0)


def from_right(x):
    return jnp.where(lanes_of(x.shape) < COLS - 1, roll(x, -1, x.ndim - 1), 0.0)


def activated_rows(feat_ref, frame, half_gain, mean_pair):
    xs = [feat_ref[frame, r].astype(F32) for r in range(ROWS)]
    acts = []
    for x, mean in zip(xs, channel_means([x * x for x in xs], mean_pair)):
        half = x * lax.rsqrt(mean + NORM_EPS) * half_gain
        acts.append((half + half * jnp.tanh(half)).astype(BF16))
    return acts


def frame_sums(taps, out_ref, frame):
    groups = [taps[8 * g : 8 * g + 8] for g in range(8)]
    row = sublanes_of((8, COLS))
    groups.append(
        jnp.where(
            row < 2,
            roll(groups[0], 2, 0),
            jnp.where(row < 4, roll(groups[1], 4, 0), roll(groups[2], 6, 0)),
        )
    )
    for o in range(3):
        out_ref[frame, o] = from_left(groups[o]) + groups[3 + o] + from_right(groups[6 + o])


def pair_sums(feat_ref, frame, half_gain, mean_pair, weight):
    acts = []
    for tau in range(2):
        acts += activated_rows(feat_ref, frame + tau, half_gain, mean_pair)
    return dot(jnp.concatenate(acts, axis=1), weight)


def tail_kernel(
    feat_hbm, gain_ref, mean_ref, conv_ref, sel_ref, sel_t_ref,
    out_ref, feat_ref, weight_ref, weight_t_ref, sems,
):
    frames = feat_hbm.shape[0]
    last = pltpu.make_async_copy(feat_hbm.at[frames - 2 :], feat_ref.at[frames - 2 :], sems.at[0])
    rest = pltpu.make_async_copy(feat_hbm.at[: frames - 2], feat_ref.at[: frames - 2], sems.at[1])
    last.start()
    rest.start()
    conv = conv_ref[...]
    for i in range(8):
        at = slice(CH * i, CH * i + CH)
        wide = slice(256 * i, 256 * i + 256)
        weight_ref[at, :] = dot_tn(conv, sel_ref[:, wide]).astype(BF16)
        weight_t_ref[:, at] = dot(sel_t_ref[wide, :], conv).astype(BF16)
    last.wait()
    sums = pair_sums(feat_ref, frames - 2, 0.5 * gain_ref[...], mean_ref[...], weight_ref[:, 128:])
    taps = sums.T
    for f in range(2):
        frame_sums(taps[64 * f : 64 * f + 64], out_ref, f)
    rest.wait()


def conv_kernel(
    feat_ref, gain_ref, mean_ref, weight_ref, up_hbm, down_hbm, out_ref, up_ref, down_ref, carry, sems
):
    copies = [
        pltpu.make_async_copy(up_hbm, up_ref, sems.at[0]),
        pltpu.make_async_copy(down_hbm, down_ref, sems.at[1]),
    ]
    for copy in copies:
        copy.start()
    carry[...] = jnp.zeros_like(carry)
    half_gain = 0.5 * gain_ref[...]
    mean_pair = mean_ref[...]

    @pl.loop(0, feat_ref.shape[0] // FORWARD_FRAMES)
    def _(step):
        for pair in range(FORWARD_FRAMES // 2):
            frame = step * FORWARD_FRAMES + 2 * pair
            sums = pair_sums(feat_ref, frame, half_gain, mean_pair, weight_ref[...])
            taps = (sums[:, :128] + carry[...]).T
            carry[...] = sums[:, 128:]
            for f in range(2):
                frame_sums(taps[64 * f : 64 * f + 64], out_ref, frame + f)

    for copy in copies:
        copy.wait()


VMEM = pl.BlockSpec(memory_space=pltpu.VMEM)
ANYWHERE = pl.BlockSpec(memory_space=pl.ANY)


def megabytes(count):
    return pltpu.CompilerParams(vmem_limit_bytes=count * 1024 * 1024)


def conv_tail(features, gain, conv_weight):
    return pl.pallas_call(
        tail_kernel,
        in_specs=[ANYWHERE] + [VMEM] * 5,
        out_specs=[VMEM] * 4,
        out_shape=[
            jax.ShapeDtypeStruct((2, 3, 8, COLS), F32),
            pltpu.VMEM(features.shape, BF16),
            pltpu.VMEM((1024, 256), BF16),
            pltpu.VMEM((256, 1024), BF16),
        ],
        scratch_shapes=[pltpu.SemaphoreType.DMA((2,))],
        compiler_params=megabytes(8),
        name="conv_tail",
    )(
        features,
        gain,
        jnp.asarray(MEAN_PAIR),
        conv_weight,
        jnp.asarray(SELECTOR),
        jnp.asarray(SELECTOR_T),
    )


def conv_main(features, gain, weight, up, down):
    return pl.pallas_call(
        conv_kernel,
        in_specs=[VMEM] * 4 + [ANYWHERE] * 2,
        out_specs=[VMEM, ANYWHERE, ANYWHERE],
        out_shape=[
            jax.ShapeDtypeStruct((features.shape[0], 3, 8, COLS), F32),
            pltpu.VMEM(up.shape, BF16),
            pltpu.VMEM(down.shape, BF16),
        ],
        scratch_shapes=[pltpu.VMEM((COLS, 128), F32), pltpu.SemaphoreType.DMA((2,))],
        compiler_params=megabytes(12),
        cost_estimate=pl.CostEstimate(
            flops=2 * 16384 * 1024, bytes_accessed=20 * 1024 * 1024, transcendentals=2 * 2097152
        ),
        name="conv_main",
    )(features, gain, jnp.asarray(MEAN_PAIR), weight, up, down)


def lay_rows(groups):
    row = sublanes_of(groups[0].shape)
    both = jnp.where(row < 4, groups[0], roll(groups[1], 4, 1))
    return jnp.concatenate([both, groups[2]], axis=1)


def rim_kernel(sums_ref, prior_ref, up_ref, down_ref):
    for o in range(3):
        for k, out_ref in ((0, up_ref), (5, down_ref)):
            out_ref[o] = sums_ref[:, o, k, :]
            out_ref[o, 0:2] = sums_ref[0:2, o, k, :] + prior_ref[:, o, k, :]


def rims(sums, prior):
    shape = jax.ShapeDtypeStruct((3, sums.shape[0], COLS), F32)
    return pl.pallas_call(
        rim_kernel,
        in_specs=[VMEM] * 2,
        out_specs=[VMEM] * 2,
        out_shape=[shape] * 2,
        compiler_params=megabytes(4),
        name="rims",
    )(sums, prior)


def colour_kernel(own_ref, bias_ref, sums_ref, prior_ref, above_ref, below_ref, *rest):
    out_refs, total = rest[:GROUP], rest[GROUP]
    total[...] = sums_ref[...]
    total[0:2] = sums_ref[0:2] + prior_ref[...]
    row = sublanes_of((8, 8, COLS))
    me = lax.rem(own_ref[0], GROUP)
    for turn in range(GROUP):
        frames = pl.ds(pl.multiple_of(lax.rem(me + turn, GROUP) * 8, 8), 8)
        groups = []
        for o in range(3):
            value = total[frames, o]
            value += jnp.where(row == 1, above_ref[o, frames, :][:, None, :], 0.0)
            value += jnp.where(row == 4, below_ref[o, frames, :][:, None, :], 0.0)
            groups.append(roll(value, -1, 1) + bias_ref[o])
        out_refs[turn][...] = lay_rows(groups).astype(BF16)


def colours(own, bias, sums, prior, above, below):
    smem = pl.BlockSpec(memory_space=pltpu.SMEM)
    shape = jax.ShapeDtypeStruct((8, 16, COLS), BF16)
    return pl.pallas_call(
        colour_kernel,
        in_specs=[smem] * 2 + [VMEM] * 4,
        out_specs=[VMEM] * GROUP,
        out_shape=[shape] * GROUP,
        scratch_shapes=[pltpu.VMEM(sums.shape, F32)],
        compiler_params=megabytes(4),
        name="colours",
    )(own, bias, sums, prior, above, below)


def swap_turns(parts):
    count = lax.axis_size("tile")
    out = [parts[0]]
    for turn in range(1, GROUP):
        pairs = [(i, i - i % GROUP + (i + turn) % GROUP) for i in range(count)]
        out.append(lax.ppermute(parts[turn], "tile", pairs))
    return out


def to_neighbours(up, down):
    count = lax.axis_size("tile")
    above = lax.ppermute(down, "tile", [(i, i + 1) for i in range(count - 1)])
    below = lax.ppermute(up, "tile", [(i + 1, i) for i in range(count - 1)])
    return above, below


def swap_blocks(x):
    row, group = sublanes_of(x.shape), lanes_of(x.shape) // 16
    for bit in (4, 2, 1):
        low = (row & bit) == 0
        same = low == ((group & bit) == 0)
        moved = jnp.where(
            low,
            roll(roll(x, -bit, 1), 16 * bit, 2),
            roll(roll(x, bit, 1), -16 * bit, 2),
        )
        x = jnp.where(same, x, moved)
    return x


def gather_patches(me, x_refs, strips):
    for turn in range(GROUP):
        strips[lax.rem(me + GROUP - turn, GROUP)] = x_refs[turn][...].astype(F32)
    first = sublanes_of((8, 8, COLS)) < 4
    pieces = [[], [], []]
    for half in range(2):
        even, odd = strips[2 * half], strips[2 * half + 1]
        pieces[0].append(jnp.where(first, even[:, :8], roll(odd[:, :8], 4, 1)))
        pieces[1].append(jnp.where(first, roll(even[:, :8], 4, 1), odd[:, :8]))
        pieces[2].append(jnp.where(first, even[:, 8:], roll(odd[:, 8:], 4, 1)))
    ordered = [swap_blocks(piece).reshape(64, 128) for group in pieces for piece in group]
    return jnp.concatenate(ordered, axis=1).astype(BF16)


def scatter_patches(me, grad, strips, out_refs):
    rows = [swap_blocks(grad[:, 128 * i : 128 * i + 128].reshape(8, 8, 128)) for i in range(6)]
    for half in range(2):
        groups = [rows[2 * o + half] for o in range(3)]
        strips[2 * half] = lay_rows(groups)
        strips[2 * half + 1] = lay_rows([roll(group, 4, 1) for group in groups])
    for turn in range(GROUP):
        out_refs[turn][...] = strips[lax.rem(me + turn, GROUP)].astype(BF16)


def normal_cdf(x):
    return 0.5 * (1.0 + lax.erf(x * 0.7071067811865476))


def pose_kernel(
    own_ref,
    x0_ref,
    x1_ref,
    x2_ref,
    x3_ref,
    frames_ref,
    counts_ref,
    key_rows_ref,
    key_cols_ref,
    key_vis_ref,
    key_spread_ref,
    gain_ref,
    up,
    down,
    order_hbm,
    patch_hbm,
    head_hbm,
    position_hbm,
    out0_ref,
    out1_ref,
    out2_ref,
    out3_ref,
    order,
    patch,
    head,
    position,
    strips,
    key_table,
    hidden_pre,
    hidden,
    pre_grad,
    sems,
):
    pairs = [(order_hbm, order), (patch_hbm, patch), (position_hbm, position), (head_hbm, head)]
    copies = [pltpu.make_async_copy(src, dst, sems.at[i]) for i, (src, dst) in enumerate(pairs)]
    for copy in copies:
        copy.start()
    token_row = own_ref[0] // GROUP
    me = lax.rem(own_ref[0], GROUP)
    first_frame = pl.multiple_of(me * 8, 8)

    frame = sublanes_of((8, 32)) + first_frame
    hit = jnp.zeros((8, 32), F32)
    for slot in range(3):
        used = frames_ref[slot] == frame
        hit = jnp.maximum(hit, jnp.where(used & (counts_ref[...] > slot), 1.0, 0.0))
    weight = jnp.max(hit, axis=1, keepdims=True)
    spread = key_spread_ref[...]

    def own_keys(ref):
        key_table[...] = dot_tn(ref[...].astype(F32).astype(BF16), spread)
        return key_table[pl.ds(first_frame, 8), :]

    def by_token(value):
        return jnp.broadcast_to(value[:, None, :], (8, 8, HEAD)).reshape(64, HEAD)

    token_column = sublanes_of((64, HEAD)) % 8
    column = lanes_of((64, HEAD))
    pixel_row = token_row * 4 + column // (4 * KP)
    pixel_col = token_column * 4 + (column // KP) % 4
    row_gap = pixel_row.astype(F32) - by_token(own_keys(key_rows_ref))
    col_gap = pixel_col.astype(F32) - by_token(own_keys(key_cols_ref))
    target = jnp.exp((row_gap * row_gap + col_gap * col_gap) * -0.125)
    mask = by_token(own_keys(key_vis_ref) * weight)

    raw = gather_patches(me, (x0_ref, x1_ref, x2_ref, x3_ref), strips)
    copies[0].wait()
    patches = dot(raw, order[...]).astype(BF16)
    copies[1].wait()
    copies[2].wait()
    pair_rows = pl.ds(pl.multiple_of(token_row // 2 * 16, 16), 16)
    two = position[pair_rows, :].astype(F32)
    places = jnp.where(lax.rem(token_row, 2) == 0, two[:8], two[8:])
    places = jnp.broadcast_to(places[None], (8, 8, DP)).reshape(64, DP)
    embedded = dot(patches, patch[...]) + places
    centred = embedded - jnp.mean(embedded, axis=-1, keepdims=True)
    inverse = lax.rsqrt(jnp.mean(centred * centred, axis=-1, keepdims=True) + NORM_EPS)
    unit_rows = centred * inverse
    gain = gain_ref[...]
    normed_tokens = (unit_rows * gain).astype(BF16)

    for i in range(HID // 256):
        at = slice(256 * i, 256 * i + 256)
        value = dot(normed_tokens, up[:, at])
        hidden_pre[:, at] = value
        hidden[:, at] = (value * normal_cdf(value)).astype(BF16)

    block = dot(hidden[...], down[...])
    block_round = (embedded + block).astype(BF16)
    copies[3].wait()
    heatmap = dot_nt(block_round, head[...])
    heat_grad = ((heatmap - target) * mask).astype(BF16)
    out_grad = dot(heat_grad, head[...])
    out_round = out_grad.astype(BF16)

    for i in range(HID // 256):
        at = slice(256 * i, 256 * i + 256)
        grad = dot_nt(out_round, down[at, :])
        pre = hidden_pre[:, at]
        slope = normal_cdf(pre) + pre * jnp.exp(-0.5 * pre * pre) * 0.3989422804014327
        pre_grad[:, at] = (grad * slope).astype(BF16)

    normed_grad = dot_nt(pre_grad[...], up[...])
    unit_grad = normed_grad * gain
    embed_grad = out_grad + inverse * (
        unit_grad
        - jnp.mean(unit_grad, axis=-1, keepdims=True)
        - unit_rows * jnp.mean(unit_grad * unit_rows, axis=-1, keepdims=True)
    )
    colour_grad = dot_nt(embed_grad.astype(BF16), patch[...]).astype(BF16)
    outs = (out0_ref, out1_ref, out2_ref, out3_ref)
    scatter_patches(me, dot_nt(colour_grad, order[...]), strips, outs)


def pose(own, parts, frames, counts, key_rows, key_cols, key_vis, gain, up, down, patch, head, position):
    smem = pl.BlockSpec(memory_space=pltpu.SMEM)
    return pl.pallas_call(
        pose_kernel,
        in_specs=[smem] + [VMEM] * 13 + [ANYWHERE] * 4,
        out_specs=[VMEM] * GROUP,
        out_shape=[jax.ShapeDtypeStruct((8, 16, COLS), BF16)] * GROUP,
        scratch_shapes=[
            pltpu.VMEM((768, 768), BF16),
            pltpu.VMEM((768, DP), BF16),
            pltpu.VMEM((HEAD, DP), BF16),
            pltpu.VMEM((64, DP), BF16),
            pltpu.VMEM((GROUP, 8, 16, COLS), F32),
            pltpu.VMEM((32, HEAD), F32),
            pltpu.VMEM((64, HID), F32),
            pltpu.VMEM((64, HID), BF16),
            pltpu.VMEM((64, HID), BF16),
            pltpu.SemaphoreType.DMA((4,)),
        ],
        compiler_params=megabytes(20),
        cost_estimate=pl.CostEstimate(
            flops=2 * 64 * 15800000, bytes_accessed=17 * 1024 * 1024, transcendentals=64 * HID * 3
        ),
        name="pose",
    )(
        own,
        *parts,
        frames,
        counts,
        key_rows,
        key_cols,
        key_vis,
        jnp.asarray(KEY_SPREAD),
        gain,
        up,
        down,
        jnp.asarray(PIXEL_ORDER),
        patch,
        head,
        position,
    )


def strip_kernel(own_ref, x0_ref, x1_ref, x2_ref, x3_ref, out_ref, first_ref, last_ref):
    me = lax.rem(own_ref[0], GROUP)
    first = sublanes_of((8, 8, COLS)) < 4
    for turn, ref in enumerate((x0_ref, x1_ref, x2_ref, x3_ref)):
        frames = pl.ds(pl.multiple_of(lax.rem(me + GROUP - turn, GROUP) * 8, 8), 8)
        value = ref[...].astype(F32)
        groups = [value[:, :8], roll(value[:, :8], 4, 1), value[:, 8:]]
        for o in range(3):
            out_ref[frames, o] = roll(jnp.where(first, groups[o], 0.0), 1, 1)
    for o in range(3):
        first_ref[o] = out_ref[:, o, 1, :]
        last_ref[o] = out_ref[:, o, 4, :]


def strip_grads(own, parts):
    rim = jax.ShapeDtypeStruct((3, 32, COLS), F32)
    return pl.pallas_call(
        strip_kernel,
        in_specs=[pl.BlockSpec(memory_space=pltpu.SMEM)] + [VMEM] * GROUP,
        out_specs=[VMEM] * 3,
        out_shape=[jax.ShapeDtypeStruct((32, 3, 8, COLS), F32), rim, rim],
        compiler_params=megabytes(4),
        name="strip_grads",
    )(own, *parts)


def whole_kernel(x_ref, above_ref, below_ref, out_ref, first_ref):
    row = sublanes_of((32, 8, COLS))
    for o in range(3):
        value = jnp.where(row == 0, above_ref[o][:, None, :], x_ref[:, o])
        value = jnp.where(row == 5, below_ref[o][:, None, :], value)
        out_ref[:, o] = value
        first_ref[:, o] = value[:2]


def whole_grads(x, above, below):
    return pl.pallas_call(
        whole_kernel,
        in_specs=[VMEM] * 3,
        out_specs=[VMEM] * 2,
        out_shape=[
            jax.ShapeDtypeStruct(x.shape, F32),
            jax.ShapeDtypeStruct((2, 3, 8, COLS), F32),
        ],
        compiler_params=megabytes(4),
        name="whole_grads",
    )(x, above, below)


def frame_taps(groups):
    row = sublanes_of((8, COLS))
    taps = [from_right(g) for g in groups] + list(groups) + [from_left(g) for g in groups]
    last = taps.pop()
    for i in range(3):
        taps[i] = jnp.where(row >= 6, roll(last, 6 - 2 * i, 0), taps[i])
    return taps


def pair_taps(ref, frame):
    rows = []
    for f in range(2):
        rows += frame_taps([ref[frame + f, o] for o in range(3)])
    return jnp.concatenate(rows, axis=0).T


def back_pair(feat_ref, frame, taps, weight, half_gain, mean_pair, store):
    grads = dot(taps, weight)
    places = [(tau, r) for tau in range(2) for r in range(ROWS)]
    for part in range(0, len(places), BACK_ROWS):
        group = places[part : part + BACK_ROWS]
        xs = [feat_ref[frame + tau, r].astype(F32) for tau, r in group]
        means = channel_means([x * x for x in xs], mean_pair)
        kept = []
        for x, mean, (tau, r) in zip(xs, means, group):
            rescale = lax.rsqrt(mean + NORM_EPS)
            normed = x * rescale
            half_pre = normed * half_gain
            tanh = jnp.tanh(half_pre)
            slope = (1.0 + tanh) * (1.0 + half_pre * (1.0 - tanh)) * half_gain
            at = CH * (ROWS * tau + r)
            kept.append((rescale, normed, grads[:, at : at + CH] * slope))
        along = channel_means([scaled * normed for _, normed, scaled in kept], mean_pair)
        for (rescale, normed, scaled), mean, (tau, r) in zip(kept, along, group):
            store(tau, r, (rescale * (scaled - normed * mean)).astype(BF16))


def back_kernel(
    feat_ref, grad_ref, gain_ref, mean_ref, weight_ref, out_hbm, buffer, carry, sems
):
    half_gain = 0.5 * gain_ref[...]
    mean_pair = mean_ref[...]
    carry[...] = pair_taps(grad_ref, 0)
    steps = (feat_ref.shape[0] - 2) // BACK_FRAMES

    def copy_of(step, slot):
        rows = pl.ds(step * BACK_FRAMES, BACK_FRAMES)
        return pltpu.make_async_copy(buffer.at[slot], out_hbm.at[rows], sems.at[slot])

    @pl.loop(0, steps)
    def _(step):
        slot = lax.rem(step, 2)

        @pl.when(step >= 2)
        def _():
            copy_of(step - 2, slot).wait()

        for pair in range(BACK_FRAMES // 2):
            frame = step * BACK_FRAMES + 2 * pair
            now = carry[...]
            later = pair_taps(grad_ref, frame + 2)
            carry[...] = later
            taps = jnp.concatenate([now, later], axis=1).astype(BF16)

            def store(tau, r, value):
                buffer[slot, 2 * pair + tau, r] = value

            back_pair(feat_ref, frame, taps, weight_ref[...], half_gain, mean_pair, store)
        copy_of(step, slot).start()

    for step in range(max(steps - 2, 0), steps):
        copy_of(step, step % 2).wait()


def last_kernel(
    feat_ref, grad_ref, next_ref, gain_ref, mean_ref, weight_ref, prior_hbm, out_hbm, buffer, sem
):
    del prior_hbm
    frame = feat_ref.shape[0] - 2
    taps = jnp.concatenate([pair_taps(grad_ref, frame), pair_taps(next_ref, 0)], axis=1).astype(BF16)

    def store(tau, r, value):
        buffer[tau, r] = value

    back_pair(feat_ref, frame, taps, weight_ref[...], 0.5 * gain_ref[...], mean_ref[...], store)
    copy = pltpu.make_async_copy(buffer, out_hbm.at[frame:], sem)
    copy.start()
    copy.wait()


def conv_backward(features, grads, later, gain, weight):
    mean_pair = jnp.asarray(MEAN_PAIR)
    out_shape = jax.ShapeDtypeStruct(features.shape, BF16)
    part = pl.pallas_call(
        back_kernel,
        in_specs=[VMEM] * 5,
        out_specs=ANYWHERE,
        out_shape=out_shape,
        scratch_shapes=[
            pltpu.VMEM((2, BACK_FRAMES, ROWS, COLS, CH), BF16),
            pltpu.VMEM((COLS, 128), F32),
            pltpu.SemaphoreType.DMA((2,)),
        ],
        compiler_params=megabytes(16),
        cost_estimate=pl.CostEstimate(
            flops=2 * 16384 * 1024, bytes_accessed=9 * 1024 * 1024, transcendentals=2 * 2097152
        ),
        name="conv_back",
    )(features, grads, gain, mean_pair, weight)
    return pl.pallas_call(
        last_kernel,
        in_specs=[VMEM] * 6 + [ANYWHERE],
        out_specs=ANYWHERE,
        out_shape=out_shape,
        input_output_aliases={6: 0},
        scratch_shapes=[pltpu.VMEM((2, ROWS, COLS, CH), BF16), pltpu.SemaphoreType.DMA],
        compiler_params=megabytes(12),
        name="conv_last",
    )(features, grads, later, gain, mean_pair, weight, part)


def per_device(
    features,
    norm_gain,
    conv_weight,
    colour_bias,
    observed_frames,
    observed_counts,
    key_rows,
    key_columns,
    key_visible,
    position_table,
    patch_weight,
    layer_gain,
    up_weight,
    down_weight,
    head_weight,
):
    tm_count = lax.axis_size("tm")
    own = lax.axis_index("tile").reshape(1)
    gain = norm_gain.reshape(1, CH)
    features, layer_gain, own = lax.optimization_barrier(
        (features, layer_gain.reshape(1, DP), own)
    )
    features = pltpu.with_memory_space_constraint(features, pltpu.HBM)
    up_weight = pltpu.with_memory_space_constraint(up_weight, pltpu.HBM)
    down_weight = pltpu.with_memory_space_constraint(down_weight, pltpu.HBM)
    tail, features, weight, weight_t = conv_tail(features, gain, conv_weight.T)
    prior = lax.ppermute(tail, "tm", [(i, i + 1) for i in range(tm_count - 1)])
    sums, up, down = conv_main(features, gain, weight, up_weight, down_weight)
    above, below = to_neighbours(*rims(sums, prior))
    parts = swap_turns(colours(own, colour_bias, sums, prior, above, below))
    parts = pose(
        own,
        parts,
        observed_frames.transpose(2, 0, 1),
        observed_counts,
        key_rows.T,
        key_columns.T,
        key_visible.T,
        layer_gain,
        up,
        down,
        patch_weight,
        head_weight.T,
        position_table,
    )
    grads, first, last = strip_grads(own, swap_turns(parts))
    above, below = to_neighbours(first, last)
    grads, first = whole_grads(grads, above, below)
    later = lax.ppermute(first, "tm", [(i + 1, i) for i in range(tm_count - 1)])
    return conv_backward(features, grads, later, gain, weight_t)


def solution(mesh):
    in_specs = (
        P("tm", "tile", None, None),
        P(),
        P(),
        P(),
        P("tm", None, None),
        P("tm", None),
        P("tm", None),
        P("tm", None),
        P("tm", None),
        P(),
        P(),
        P(),
        P(),
        P(),
        P(),
    )
    return jax.shard_map(
        per_device,
        mesh=mesh,
        in_specs=in_specs,
        out_specs=P("tm", "tile", None, None),
        check_vma=False,
    )
```

```python
import jax
import jax.numpy as jnp
import ml_dtypes
import numpy as np
from jax import lax
from jax.experimental import pallas as pl
from jax.experimental.pallas import tpu as pltpu
from jax.sharding import PartitionSpec as P

CH = 128
DP = 1280
HID = 2560
PATCH = 16
KP = 17
HEAD = 272
COLS = 128
ROWS = 4
GROUP = 4
FORWARD_FRAMES = 8
BACK_FRAMES = 10
BACK_ROWS = 4
NORM_EPS = 1e-06
F32 = jnp.float32
BF16 = jnp.bfloat16


def slot_of(c, o, k):
    group = 3 * c + o
    if group < 8:
        return 8 * group + k
    return 8 * (k // 2) + 6 + k % 2


def make_selector():
    table = np.zeros((81, 2, ROWS, 256), np.float32)
    for tau in range(2):
        for r in range(ROWS):
            for f in range(4):
                a = tau + 2 - f
                if not 0 <= a <= 2:
                    continue
                for k in range(6):
                    b = r + 2 - k
                    if not 0 <= b <= 2:
                        continue
                    for c in range(3):
                        for o in range(3):
                            table[3 * (9 * a + 3 * b + c) + o, tau, r, 64 * f + slot_of(c, o, k)] = 1
    return table.reshape(81, 2048)


def make_pixel_order():
    table = np.zeros((768, 768), np.float32)
    for o in range(3):
        for pixel in range(256):
            table[256 * o + pixel, 3 * pixel + o] = 1
    return table


def make_key_spread():
    table = np.zeros((KP, HEAD), np.float32)
    table[np.arange(HEAD) % KP, np.arange(HEAD)] = 1
    return table


SELECTOR = make_selector().astype(ml_dtypes.bfloat16)
SELECTOR_T = np.ascontiguousarray(make_selector().T).astype(ml_dtypes.bfloat16)
PIXEL_ORDER = make_pixel_order().astype(ml_dtypes.bfloat16)
KEY_SPREAD = make_key_spread().astype(ml_dtypes.bfloat16)
MEAN_PAIR = (np.kron(np.eye(2), np.ones((CH, CH))) / CH).astype(ml_dtypes.bfloat16)


def dot(a, b):
    return jnp.dot(a, b, preferred_element_type=F32)


def dot_tn(a, b):
    return lax.dot_general(a, b, (((0,), (0,)), ((), ())), preferred_element_type=F32)


def dot_nt(a, b):
    return lax.dot_general(a, b, (((1,), (1,)), ((), ())), preferred_element_type=F32)


def roll(x, shift, axis):
    shift %= x.shape[axis]
    return pltpu.roll(x, shift, axis) if shift else x


def channel_means(values, mean_pair):
    rounded = [value.astype(BF16) for value in values]
    pairs = [jnp.concatenate(rounded[i : i + 2], axis=1) for i in range(0, len(values), 2)]
    means = dot(jnp.concatenate(pairs, axis=0), mean_pair)
    out = []
    for i in range(len(pairs)):
        rows = slice(COLS * i, COLS * i + COLS)
        out += [means[rows, :CH], means[rows, CH:]]
    return out


def lanes_of(shape):
    return lax.broadcasted_iota(jnp.int32, shape, len(shape) - 1)


def sublanes_of(shape):
    return lax.broadcasted_iota(jnp.int32, shape, len(shape) - 2)


def from_left(x):
    return jnp.where(lanes_of(x.shape) >= 1, roll(x, 1, x.ndim - 1), 0.0)


def from_right(x):
    return jnp.where(lanes_of(x.shape) < COLS - 1, roll(x, -1, x.ndim - 1), 0.0)


def activated_rows(feat_ref, frame, half_gain, mean_pair):
    xs = [feat_ref[frame, r].astype(F32) for r in range(ROWS)]
    acts = []
    for x, mean in zip(xs, channel_means([x * x for x in xs], mean_pair)):
        half = x * lax.rsqrt(mean + NORM_EPS) * half_gain
        acts.append((half + half * jnp.tanh(half)).astype(BF16))
    return acts


def frame_sums(taps, out_ref, frame):
    groups = [taps[8 * g : 8 * g + 8] for g in range(8)]
    row = sublanes_of((8, COLS))
    groups.append(
        jnp.where(
            row < 2,
            roll(groups[0], 2, 0),
            jnp.where(row < 4, roll(groups[1], 4, 0), roll(groups[2], 6, 0)),
        )
    )
    for o in range(3):
        out_ref[frame, o] = from_left(groups[o]) + groups[3 + o] + from_right(groups[6 + o])


def pair_sums(feat_ref, frame, half_gain, mean_pair, weight):
    acts = []
    for tau in range(2):
        acts += activated_rows(feat_ref, frame + tau, half_gain, mean_pair)
    return dot(jnp.concatenate(acts, axis=1), weight)


def tail_kernel(
    feat_hbm, gain_hbm, mean_hbm, conv_hbm, sel_hbm, sel_t_hbm,
    out_ref, feat_ref, weight_ref, weight_t_ref, mean_ref, gain_ref,
    conv_ref, sel_ref, sel_t_ref, sems,
):
    frames = feat_hbm.shape[0]
    last = pltpu.make_async_copy(feat_hbm.at[frames - 2 :], feat_ref.at[frames - 2 :], sems.at[0])
    rest = pltpu.make_async_copy(feat_hbm.at[: frames - 2], feat_ref.at[: frames - 2], sems.at[1])
    small = [
        pltpu.make_async_copy(src, dst, sems.at[2 + i])
        for i, (src, dst) in enumerate(
            (
                (conv_hbm, conv_ref),
                (sel_hbm, sel_ref),
                (sel_t_hbm, sel_t_ref),
                (gain_hbm, gain_ref),
                (mean_hbm, mean_ref),
            )
        )
    ]
    for copy in small:
        copy.start()
    last.start()
    rest.start()
    for copy in small:
        copy.wait()
    conv = conv_ref[...]
    for i in range(8):
        at = slice(CH * i, CH * i + CH)
        wide = slice(256 * i, 256 * i + 256)
        weight_ref[at, :] = dot_tn(conv, sel_ref[:, wide]).astype(BF16)
        weight_t_ref[:, at] = dot(sel_t_ref[wide, :], conv).astype(BF16)
    last.wait()
    sums = pair_sums(feat_ref, frames - 2, 0.5 * gain_ref[...], mean_ref[...], weight_ref[:, 128:])
    taps = sums.T
    for f in range(2):
        frame_sums(taps[64 * f : 64 * f + 64], out_ref, f)
    rest.wait()


def conv_kernel(
    feat_ref, gain_ref, mean_ref, weight_ref, up_hbm, down_hbm, out_ref, up_ref, down_ref, carry, sems
):
    copies = [
        pltpu.make_async_copy(up_hbm, up_ref, sems.at[0]),
        pltpu.make_async_copy(down_hbm, down_ref, sems.at[1]),
    ]
    for copy in copies:
        copy.start()
    carry[...] = jnp.zeros_like(carry)
    half_gain = 0.5 * gain_ref[...]
    mean_pair = mean_ref[...]

    @pl.loop(0, feat_ref.shape[0] // FORWARD_FRAMES)
    def _(step):
        for pair in range(FORWARD_FRAMES // 2):
            frame = step * FORWARD_FRAMES + 2 * pair
            sums = pair_sums(feat_ref, frame, half_gain, mean_pair, weight_ref[...])
            taps = (sums[:, :128] + carry[...]).T
            carry[...] = sums[:, 128:]
            for f in range(2):
                frame_sums(taps[64 * f : 64 * f + 64], out_ref, frame + f)

    for copy in copies:
        copy.wait()


VMEM = pl.BlockSpec(memory_space=pltpu.VMEM)
SMEM = pl.BlockSpec(memory_space=pltpu.SMEM)
ANYWHERE = pl.BlockSpec(memory_space=pl.ANY)


def megabytes(count):
    return pltpu.CompilerParams(vmem_limit_bytes=count * 1024 * 1024)


def conv_tail(features, *small):
    return pl.pallas_call(
        tail_kernel,
        in_specs=[ANYWHERE] * 6,
        out_specs=[VMEM] * 6,
        out_shape=[
            jax.ShapeDtypeStruct((2, 3, 8, COLS), F32),
            pltpu.VMEM(features.shape, BF16),
            pltpu.VMEM((1024, 256), BF16),
            pltpu.VMEM((256, 1024), BF16),
            pltpu.VMEM((256, 256), BF16),
            pltpu.VMEM((1, CH), F32),
        ],
        scratch_shapes=[
            pltpu.VMEM((81, CH), BF16),
            pltpu.VMEM((81, 2048), BF16),
            pltpu.VMEM((2048, 81), BF16),
            pltpu.SemaphoreType.DMA((7,)),
        ],
        compiler_params=megabytes(8),
        name="conv_tail",
    )(
        features, *small
    )


def conv_main(features, gain, mean_pair, weight, up, down):
    return pl.pallas_call(
        conv_kernel,
        in_specs=[VMEM] * 4 + [ANYWHERE] * 2,
        out_specs=[VMEM, ANYWHERE, ANYWHERE],
        out_shape=[
            jax.ShapeDtypeStruct((features.shape[0], 3, 8, COLS), F32),
            pltpu.VMEM(up.shape, BF16),
            pltpu.VMEM(down.shape, BF16),
        ],
        scratch_shapes=[pltpu.VMEM((COLS, 128), F32), pltpu.SemaphoreType.DMA((2,))],
        compiler_params=megabytes(12),
        cost_estimate=pl.CostEstimate(
            flops=2 * 16384 * 1024, bytes_accessed=20 * 1024 * 1024, transcendentals=2 * 2097152
        ),
        name="conv_main",
    )(features, gain, mean_pair, weight, up, down)


def lay_rows(groups):
    row = sublanes_of(groups[0].shape)
    both = jnp.where(row < 4, groups[0], roll(groups[1], 4, 1))
    return jnp.concatenate([both, groups[2]], axis=1)


def unless(is_edge, value):
    return jnp.where(is_edge, jnp.zeros_like(value), value)


def rim_kernel(place_ref, sums_ref, prior_ref, up_ref, down_ref):
    first_block = place_ref[1] == 0
    for o in range(3):
        for k, out_ref in ((0, up_ref), (5, down_ref)):
            out_ref[o] = sums_ref[:, o, k, :]
            out_ref[o, 0:2] = sums_ref[0:2, o, k, :] + unless(first_block, prior_ref[:, o, k, :])


def rims(place, sums, prior):
    shape = jax.ShapeDtypeStruct((3, sums.shape[0], COLS), F32)
    return pl.pallas_call(
        rim_kernel,
        in_specs=[SMEM] + [VMEM] * 2,
        out_specs=[VMEM] * 2,
        out_shape=[shape] * 2,
        compiler_params=megabytes(4),
        name="rims",
    )(place, sums, prior)


def colour_kernel(own_ref, bias_ref, sums_ref, prior_ref, above_ref, below_ref, *rest):
    out_refs, total = rest[:GROUP], rest[GROUP]
    total[...] = sums_ref[...]
    total[0:2] = sums_ref[0:2] + unless(own_ref[1] == 0, prior_ref[...])
    top, bottom = own_ref[0] == 0, own_ref[0] == own_ref[2] - 1
    row = sublanes_of((8, 8, COLS))
    me = lax.rem(own_ref[0], GROUP)
    for turn in range(GROUP):
        frames = pl.ds(pl.multiple_of(lax.rem(me + turn, GROUP) * 8, 8), 8)
        groups = []
        for o in range(3):
            value = total[frames, o]
            value += jnp.where(row == 1, unless(top, above_ref[o, frames, :])[:, None, :], 0.0)
            value += jnp.where(row == 4, unless(bottom, below_ref[o, frames, :])[:, None, :], 0.0)
            groups.append(roll(value, -1, 1) + bias_ref[o])
        out_refs[turn][...] = lay_rows(groups).astype(BF16)


def colours(own, bias, sums, prior, above, below):
    shape = jax.ShapeDtypeStruct((8, 16, COLS), BF16)
    return pl.pallas_call(
        colour_kernel,
        in_specs=[SMEM] * 2 + [VMEM] * 4,
        out_specs=[VMEM] * GROUP,
        out_shape=[shape] * GROUP,
        scratch_shapes=[pltpu.VMEM(sums.shape, F32)],
        compiler_params=megabytes(4),
        name="colours",
    )(own, bias, sums, prior, above, below)


def swap_turns(parts):
    count = lax.axis_size("tile")
    out = [parts[0]]
    for turn in range(1, GROUP):
        pairs = [(i, i - i % GROUP + (i + turn) % GROUP) for i in range(count)]
        out.append(lax.ppermute(parts[turn], "tile", pairs))
    return out


def to_neighbours(up, down):
    count = lax.axis_size("tile")
    above = lax.ppermute(down, "tile", [(i, (i + 1) % count) for i in range(count)])
    below = lax.ppermute(up, "tile", [((i + 1) % count, i) for i in range(count)])
    return above, below


def swap_blocks(x):
    row, group = sublanes_of(x.shape), lanes_of(x.shape) // 16
    for bit in (4, 2, 1):
        low = (row & bit) == 0
        same = low == ((group & bit) == 0)
        moved = jnp.where(
            low,
            roll(roll(x, -bit, 1), 16 * bit, 2),
            roll(roll(x, bit, 1), -16 * bit, 2),
        )
        x = jnp.where(same, x, moved)
    return x


def gather_patches(me, x_refs, strips):
    for turn in range(GROUP):
        strips[lax.rem(me + GROUP - turn, GROUP)] = x_refs[turn][...].astype(F32)
    first = sublanes_of((8, 8, COLS)) < 4
    pieces = [[], [], []]
    for half in range(2):
        even, odd = strips[2 * half], strips[2 * half + 1]
        pieces[0].append(jnp.where(first, even[:, :8], roll(odd[:, :8], 4, 1)))
        pieces[1].append(jnp.where(first, roll(even[:, :8], 4, 1), odd[:, :8]))
        pieces[2].append(jnp.where(first, even[:, 8:], roll(odd[:, 8:], 4, 1)))
    ordered = [swap_blocks(piece).reshape(64, 128) for group in pieces for piece in group]
    return jnp.concatenate(ordered, axis=1).astype(BF16)


def scatter_patches(me, grad, strips, out_refs):
    rows = [swap_blocks(grad[:, 128 * i : 128 * i + 128].reshape(8, 8, 128)) for i in range(6)]
    for half in range(2):
        groups = [rows[2 * o + half] for o in range(3)]
        strips[2 * half] = lay_rows(groups)
        strips[2 * half + 1] = lay_rows([roll(group, 4, 1) for group in groups])
    for turn in range(GROUP):
        out_refs[turn][...] = strips[lax.rem(me + turn, GROUP)].astype(BF16)


def normal_cdf(x):
    return 0.5 * (1.0 + lax.erf(x * 0.7071067811865476))


def pose_kernel(
    own_ref,
    x0_ref,
    x1_ref,
    x2_ref,
    x3_ref,
    frames_ref,
    counts_ref,
    key_rows_ref,
    key_cols_ref,
    key_vis_ref,
    key_spread_ref,
    gain_ref,
    up,
    down,
    order_hbm,
    patch_hbm,
    head_hbm,
    position_hbm,
    out0_ref,
    out1_ref,
    out2_ref,
    out3_ref,
    order,
    patch,
    head,
    position,
    strips,
    key_table,
    hidden_pre,
    hidden,
    pre_grad,
    sems,
):
    pairs = [(order_hbm, order), (patch_hbm, patch), (position_hbm, position), (head_hbm, head)]
    copies = [pltpu.make_async_copy(src, dst, sems.at[i]) for i, (src, dst) in enumerate(pairs)]
    for copy in copies:
        copy.start()
    token_row = own_ref[0] // GROUP
    me = lax.rem(own_ref[0], GROUP)
    first_frame = pl.multiple_of(me * 8, 8)

    frame = sublanes_of((8, 32)) + first_frame
    hit = jnp.zeros((8, 32), F32)
    for slot in range(3):
        used = frames_ref[slot] == frame
        hit = jnp.maximum(hit, jnp.where(used & (counts_ref[...] > slot), 1.0, 0.0))
    weight = jnp.max(hit, axis=1, keepdims=True)
    spread = key_spread_ref[...]

    def own_keys(ref):
        key_table[...] = dot_tn(ref[...].astype(F32).astype(BF16), spread)
        return key_table[pl.ds(first_frame, 8), :]

    def by_token(value):
        return jnp.broadcast_to(value[:, None, :], (8, 8, HEAD)).reshape(64, HEAD)

    token_column = sublanes_of((64, HEAD)) % 8
    column = lanes_of((64, HEAD))
    pixel_row = token_row * 4 + column // (4 * KP)
    pixel_col = token_column * 4 + (column // KP) % 4
    row_gap = pixel_row.astype(F32) - by_token(own_keys(key_rows_ref))
    col_gap = pixel_col.astype(F32) - by_token(own_keys(key_cols_ref))
    target = jnp.exp((row_gap * row_gap + col_gap * col_gap) * -0.125)
    mask = by_token(own_keys(key_vis_ref) * weight)

    raw = gather_patches(me, (x0_ref, x1_ref, x2_ref, x3_ref), strips)
    copies[0].wait()
    patches = dot(raw, order[...]).astype(BF16)
    copies[1].wait()
    copies[2].wait()
    pair_rows = pl.ds(pl.multiple_of(token_row // 2 * 16, 16), 16)
    two = position[pair_rows, :].astype(F32)
    places = jnp.where(lax.rem(token_row, 2) == 0, two[:8], two[8:])
    places = jnp.broadcast_to(places[None], (8, 8, DP)).reshape(64, DP)
    embedded = dot(patches, patch[...]) + places
    centred = embedded - jnp.mean(embedded, axis=-1, keepdims=True)
    inverse = lax.rsqrt(jnp.mean(centred * centred, axis=-1, keepdims=True) + NORM_EPS)
    unit_rows = centred * inverse
    gain = jnp.concatenate([gain_ref[i : i + 1] for i in range(DP // 128)], axis=1)
    normed_tokens = (unit_rows * gain).astype(BF16)

    for i in range(HID // 256):
        at = slice(256 * i, 256 * i + 256)
        value = dot(normed_tokens, up[:, at])
        hidden_pre[:, at] = value
        hidden[:, at] = (value * normal_cdf(value)).astype(BF16)

    block = dot(hidden[...], down[...])
    block_round = (embedded + block).astype(BF16)
    copies[3].wait()
    heatmap = dot_nt(block_round, head[...])
    heat_grad = ((heatmap - target) * mask).astype(BF16)
    out_grad = dot(heat_grad, head[...])
    out_round = out_grad.astype(BF16)

    for i in range(HID // 256):
        at = slice(256 * i, 256 * i + 256)
        grad = dot_nt(out_round, down[at, :])
        pre = hidden_pre[:, at]
        slope = normal_cdf(pre) + pre * jnp.exp(-0.5 * pre * pre) * 0.3989422804014327
        pre_grad[:, at] = (grad * slope).astype(BF16)

    normed_grad = dot_nt(pre_grad[...], up[...])
    unit_grad = normed_grad * gain
    embed_grad = out_grad + inverse * (
        unit_grad
        - jnp.mean(unit_grad, axis=-1, keepdims=True)
        - unit_rows * jnp.mean(unit_grad * unit_rows, axis=-1, keepdims=True)
    )
    colour_grad = dot_nt(embed_grad.astype(BF16), patch[...]).astype(BF16)
    outs = (out0_ref, out1_ref, out2_ref, out3_ref)
    scatter_patches(me, dot_nt(colour_grad, order[...]), strips, outs)


def pose(own, parts, frames, counts, key_rows, key_cols, key_vis, gain, up, down, patch, head, position):
    return pl.pallas_call(
        pose_kernel,
        in_specs=[SMEM] + [VMEM] * 13 + [ANYWHERE] * 4,
        out_specs=[VMEM] * GROUP,
        out_shape=[jax.ShapeDtypeStruct((8, 16, COLS), BF16)] * GROUP,
        scratch_shapes=[
            pltpu.VMEM((768, 768), BF16),
            pltpu.VMEM((768, DP), BF16),
            pltpu.VMEM((HEAD, DP), BF16),
            pltpu.VMEM((64, DP), BF16),
            pltpu.VMEM((GROUP, 8, 16, COLS), F32),
            pltpu.VMEM((32, HEAD), F32),
            pltpu.VMEM((64, HID), F32),
            pltpu.VMEM((64, HID), BF16),
            pltpu.VMEM((64, HID), BF16),
            pltpu.SemaphoreType.DMA((4,)),
        ],
        compiler_params=megabytes(20),
        cost_estimate=pl.CostEstimate(
            flops=2 * 64 * 15800000, bytes_accessed=17 * 1024 * 1024, transcendentals=64 * HID * 3
        ),
        name="pose",
    )(
        own,
        *parts,
        frames,
        counts,
        key_rows,
        key_cols,
        key_vis,
        jnp.asarray(KEY_SPREAD),
        gain,
        up,
        down,
        jnp.asarray(PIXEL_ORDER),
        patch,
        head,
        position,
    )


def strip_kernel(own_ref, x0_ref, x1_ref, x2_ref, x3_ref, out_ref, first_ref, last_ref):
    me = lax.rem(own_ref[0], GROUP)
    first = sublanes_of((8, 8, COLS)) < 4
    for turn, ref in enumerate((x0_ref, x1_ref, x2_ref, x3_ref)):
        frames = pl.ds(pl.multiple_of(lax.rem(me + GROUP - turn, GROUP) * 8, 8), 8)
        value = ref[...].astype(F32)
        groups = [value[:, :8], roll(value[:, :8], 4, 1), value[:, 8:]]
        for o in range(3):
            out_ref[frames, o] = roll(jnp.where(first, groups[o], 0.0), 1, 1)
    for o in range(3):
        first_ref[o] = out_ref[:, o, 1, :]
        last_ref[o] = out_ref[:, o, 4, :]


def strip_grads(own, parts):
    rim = jax.ShapeDtypeStruct((3, 32, COLS), F32)
    return pl.pallas_call(
        strip_kernel,
        in_specs=[SMEM] + [VMEM] * GROUP,
        out_specs=[VMEM] * 3,
        out_shape=[jax.ShapeDtypeStruct((32, 3, 8, COLS), F32), rim, rim],
        compiler_params=megabytes(4),
        name="strip_grads",
    )(own, *parts)


def whole_kernel(place_ref, x_ref, above_ref, below_ref, out_ref, first_ref):
    row = sublanes_of((32, 8, COLS))
    top, bottom = place_ref[0] == 0, place_ref[0] == place_ref[2] - 1
    for o in range(3):
        value = jnp.where(row == 0, unless(top, above_ref[o])[:, None, :], x_ref[:, o])
        value = jnp.where(row == 5, unless(bottom, below_ref[o])[:, None, :], value)
        out_ref[:, o] = value
        first_ref[:, o] = value[:2]


def whole_grads(place, x, above, below):
    return pl.pallas_call(
        whole_kernel,
        in_specs=[SMEM] + [VMEM] * 3,
        out_specs=[VMEM] * 2,
        out_shape=[
            jax.ShapeDtypeStruct(x.shape, F32),
            jax.ShapeDtypeStruct((2, 3, 8, COLS), F32),
        ],
        compiler_params=megabytes(4),
        name="whole_grads",
    )(place, x, above, below)


def frame_taps(groups):
    row = sublanes_of((8, COLS))
    taps = [from_right(g) for g in groups] + list(groups) + [from_left(g) for g in groups]
    last = taps.pop()
    for i in range(3):
        taps[i] = jnp.where(row >= 6, roll(last, 6 - 2 * i, 0), taps[i])
    return taps


def pair_taps(ref, frame):
    rows = []
    for f in range(2):
        rows += frame_taps([ref[frame + f, o] for o in range(3)])
    return jnp.concatenate(rows, axis=0).T


def back_pair(feat_ref, frame, taps, weight, half_gain, mean_pair, store):
    grads = dot(taps, weight)
    places = [(tau, r) for tau in range(2) for r in range(ROWS)]
    for part in range(0, len(places), BACK_ROWS):
        group = places[part : part + BACK_ROWS]
        xs = [feat_ref[frame + tau, r].astype(F32) for tau, r in group]
        means = channel_means([x * x for x in xs], mean_pair)
        kept = []
        for x, mean, (tau, r) in zip(xs, means, group):
            rescale = lax.rsqrt(mean + NORM_EPS)
            normed = x * rescale
            half_pre = normed * half_gain
            tanh = jnp.tanh(half_pre)
            slope = (1.0 + tanh) * (1.0 + half_pre * (1.0 - tanh)) * half_gain
            at = CH * (ROWS * tau + r)
            kept.append((rescale, normed, grads[:, at : at + CH] * slope))
        along = channel_means([scaled * normed for _, normed, scaled in kept], mean_pair)
        for (rescale, normed, scaled), mean, (tau, r) in zip(kept, along, group):
            store(tau, r, (rescale * (scaled - normed * mean)).astype(BF16))


def back_kernel(
    feat_ref, grad_ref, gain_ref, mean_ref, weight_ref, out_hbm, buffer, carry, sems
):
    half_gain = 0.5 * gain_ref[...]
    mean_pair = mean_ref[...]
    carry[...] = pair_taps(grad_ref, 0)
    steps = (feat_ref.shape[0] - 2) // BACK_FRAMES

    def copy_of(step, slot):
        rows = pl.ds(step * BACK_FRAMES, BACK_FRAMES)
        return pltpu.make_async_copy(buffer.at[slot], out_hbm.at[rows], sems.at[slot])

    @pl.loop(0, steps)
    def _(step):
        slot = lax.rem(step, 2)

        @pl.when(step >= 2)
        def _():
            copy_of(step - 2, slot).wait()

        for pair in range(BACK_FRAMES // 2):
            frame = step * BACK_FRAMES + 2 * pair
            now = carry[...]
            later = pair_taps(grad_ref, frame + 2)
            carry[...] = later
            taps = jnp.concatenate([now, later], axis=1).astype(BF16)

            def store(tau, r, value):
                buffer[slot, 2 * pair + tau, r] = value

            back_pair(feat_ref, frame, taps, weight_ref[...], half_gain, mean_pair, store)
        copy_of(step, slot).start()

    for step in range(max(steps - 2, 0), steps):
        copy_of(step, step % 2).wait()


def last_kernel(
    place_ref, feat_ref, grad_ref, next_ref, gain_ref, mean_ref, weight_ref, prior_hbm, out_hbm, buffer, sem
):
    del prior_hbm
    frame = feat_ref.shape[0] - 2
    last_block = place_ref[1] == place_ref[3] - 1
    later = unless(last_block, pair_taps(next_ref, 0))
    taps = jnp.concatenate([pair_taps(grad_ref, frame), later], axis=1).astype(BF16)

    def store(tau, r, value):
        buffer[tau, r] = value

    back_pair(feat_ref, frame, taps, weight_ref[...], 0.5 * gain_ref[...], mean_ref[...], store)
    copy = pltpu.make_async_copy(buffer, out_hbm.at[frame:], sem)
    copy.start()
    copy.wait()


def conv_backward(place, features, grads, later, gain, mean_pair, weight):
    out_shape = jax.ShapeDtypeStruct(features.shape, BF16)
    part = pl.pallas_call(
        back_kernel,
        in_specs=[VMEM] * 5,
        out_specs=ANYWHERE,
        out_shape=out_shape,
        scratch_shapes=[
            pltpu.VMEM((2, BACK_FRAMES, ROWS, COLS, CH), BF16),
            pltpu.VMEM((COLS, 128), F32),
            pltpu.SemaphoreType.DMA((2,)),
        ],
        compiler_params=megabytes(16),
        cost_estimate=pl.CostEstimate(
            flops=2 * 16384 * 1024, bytes_accessed=9 * 1024 * 1024, transcendentals=2 * 2097152
        ),
        name="conv_back",
    )(features, grads, gain, mean_pair, weight)
    return pl.pallas_call(
        last_kernel,
        in_specs=[SMEM] + [VMEM] * 6 + [ANYWHERE],
        out_specs=ANYWHERE,
        out_shape=out_shape,
        input_output_aliases={7: 0},
        scratch_shapes=[pltpu.VMEM((2, ROWS, COLS, CH), BF16), pltpu.SemaphoreType.DMA],
        compiler_params=megabytes(12),
        name="conv_last",
    )(place, features, grads, later, gain, mean_pair, weight, part)


def per_device(
    features,
    norm_gain,
    conv_weight,
    colour_bias,
    observed_frames,
    observed_counts,
    key_rows,
    key_columns,
    key_visible,
    position_table,
    patch_weight,
    layer_gain,
    up_weight,
    down_weight,
    head_weight,
):
    tm_count = lax.axis_size("tm")
    own = jnp.stack(
        [
            lax.axis_index("tile"),
            lax.axis_index("tm"),
            jnp.int32(lax.axis_size("tile")),
            jnp.int32(tm_count),
        ]
    )
    gain = norm_gain.reshape(1, CH)
    features, layer_gain, own = lax.optimization_barrier(
        (features, layer_gain.reshape(DP // 128, 128), own)
    )
    features = pltpu.with_memory_space_constraint(features, pltpu.HBM)
    up_weight = pltpu.with_memory_space_constraint(up_weight, pltpu.HBM)
    down_weight = pltpu.with_memory_space_constraint(down_weight, pltpu.HBM)
    gain = pltpu.with_memory_space_constraint(gain, pltpu.HBM)
    consts = [jnp.asarray(x) for x in (MEAN_PAIR, SELECTOR, SELECTOR_T)]
    mean_pair, sel, sel_t = [pltpu.with_memory_space_constraint(x, pltpu.HBM) for x in consts]
    conv_weight = pltpu.with_memory_space_constraint(conv_weight.T, pltpu.HBM)
    tail, features, weight, weight_t, mean_pair, gain = conv_tail(
        features, gain, mean_pair, conv_weight, sel, sel_t
    )
    prior = lax.ppermute(tail, "tm", [(i, (i + 1) % tm_count) for i in range(tm_count)])
    sums, up, down = conv_main(features, gain, mean_pair, weight, up_weight, down_weight)
    above, below = to_neighbours(*rims(own, sums, prior))
    parts = swap_turns(colours(own, colour_bias, sums, prior, above, below))
    parts = pose(
        own,
        parts,
        observed_frames.transpose(2, 0, 1),
        observed_counts,
        key_rows.T,
        key_columns.T,
        key_visible.T,
        layer_gain,
        up,
        down,
        patch_weight,
        head_weight.T,
        position_table,
    )
    grads, first, last = strip_grads(own, swap_turns(parts))
    above, below = to_neighbours(first, last)
    grads, first = whole_grads(own, grads, above, below)
    later = lax.ppermute(first, "tm", [((i + 1) % tm_count, i) for i in range(tm_count)])
    return conv_backward(own, features, grads, later, gain, mean_pair, weight_t)


def solution(mesh):
    in_specs = (
        P("tm", "tile", None, None),
        P(),
        P(),
        P(),
        P("tm", None, None),
        P("tm", None),
        P("tm", None),
        P("tm", None),
        P("tm", None),
        P(),
        P(),
        P(),
        P(),
        P(),
        P(),
    )
    return jax.shard_map(
        per_device,
        mesh=mesh,
        in_specs=in_specs,
        out_specs=P("tm", "tile", None, None),
        check_vma=False,
    )
```

```python
import functools

import jax
import jax.numpy as jnp
import ml_dtypes
import numpy as np
from jax import lax
from jax.experimental import pallas as pl
from jax.experimental.pallas import tpu as pltpu
from jax.sharding import PartitionSpec as P

CH = 128
DP = 1280
HID = 2560
PATCH = 16
KP = 17
HEAD = 272
COLS = 128
ROWS = 4
GROUP = 4
FORWARD_FRAMES = 8
BACK_FRAMES = 8
BACK_ROWS = 4
NORM_EPS = 1e-06
F32 = jnp.float32
BF16 = jnp.bfloat16


def slot_of(c, o, k):
    group = 3 * c + o
    if group < 8:
        return 8 * group + k
    return 8 * (k // 2) + 6 + k % 2


def make_selector():
    table = np.zeros((81, 2, ROWS, 256), np.float32)
    for tau in range(2):
        for r in range(ROWS):
            for f in range(4):
                a = tau + 2 - f
                if not 0 <= a <= 2:
                    continue
                for k in range(6):
                    b = r + 2 - k
                    if not 0 <= b <= 2:
                        continue
                    for c in range(3):
                        for o in range(3):
                            table[3 * (9 * a + 3 * b + c) + o, tau, r, 64 * f + slot_of(c, o, k)] = 1
    return table.reshape(81, 2048)


def make_pixel_order():
    table = np.zeros((768, 768), np.float32)
    for o in range(3):
        for pixel in range(256):
            table[256 * o + pixel, 3 * pixel + o] = 1
    return table


def make_key_spread():
    table = np.zeros((KP, HEAD), np.float32)
    table[np.arange(HEAD) % KP, np.arange(HEAD)] = 1
    return table


SELECTOR = make_selector().astype(ml_dtypes.bfloat16)
SELECTOR_T = np.ascontiguousarray(make_selector().T).astype(ml_dtypes.bfloat16)
PIXEL_ORDER = make_pixel_order().astype(ml_dtypes.bfloat16)
KEY_SPREAD = make_key_spread().astype(ml_dtypes.bfloat16)
MEAN_PAIR = (np.kron(np.eye(2), np.ones((CH, CH))) / CH).astype(ml_dtypes.bfloat16)


def dot(a, b):
    return jnp.dot(a, b, preferred_element_type=F32)


def dot_tn(a, b):
    return lax.dot_general(a, b, (((0,), (0,)), ((), ())), preferred_element_type=F32)


def dot_nt(a, b):
    return lax.dot_general(a, b, (((1,), (1,)), ((), ())), preferred_element_type=F32)


def roll(x, shift, axis):
    shift %= x.shape[axis]
    return pltpu.roll(x, shift, axis) if shift else x


def channel_means(values, mean_pair):
    rounded = [value.astype(BF16) for value in values]
    pairs = [jnp.concatenate(rounded[i : i + 2], axis=1) for i in range(0, len(values), 2)]
    means = dot(jnp.concatenate(pairs, axis=0), mean_pair)
    out = []
    for i in range(len(pairs)):
        rows = slice(COLS * i, COLS * i + COLS)
        out += [means[rows, :CH], means[rows, CH:]]
    return out


def lanes_of(shape):
    return lax.broadcasted_iota(jnp.int32, shape, len(shape) - 1)


def sublanes_of(shape):
    return lax.broadcasted_iota(jnp.int32, shape, len(shape) - 2)


def from_left(x):
    return jnp.where(lanes_of(x.shape) >= 1, roll(x, 1, x.ndim - 1), 0.0)


def from_right(x):
    return jnp.where(lanes_of(x.shape) < COLS - 1, roll(x, -1, x.ndim - 1), 0.0)


def activated_rows(feat_ref, frame, half_gain, mean_pair):
    xs = [feat_ref[frame, r].astype(F32) for r in range(ROWS)]
    acts = []
    for x, mean in zip(xs, channel_means([x * x for x in xs], mean_pair)):
        half = x * lax.rsqrt(mean + NORM_EPS) * half_gain
        acts.append((half + half * jnp.tanh(half)).astype(BF16))
    return acts


def frame_sums(taps, out_ref, frame):
    groups = [taps[8 * g : 8 * g + 8] for g in range(8)]
    row = sublanes_of((8, COLS))
    groups.append(
        jnp.where(
            row < 2,
            roll(groups[0], 2, 0),
            jnp.where(row < 4, roll(groups[1], 4, 0), roll(groups[2], 6, 0)),
        )
    )
    for o in range(3):
        out_ref[frame, o] = from_left(groups[o]) + groups[3 + o] + from_right(groups[6 + o])


def pair_sums(feat_ref, frame, half_gain, mean_pair, weight):
    acts = []
    for tau in range(2):
        acts += activated_rows(feat_ref, frame + tau, half_gain, mean_pair)
    return dot(jnp.concatenate(acts, axis=1), weight)


def tail_kernel(
    feat_hbm, gain_hbm, mean_hbm, conv_hbm, sel_hbm, sel_t_hbm,
    out_ref, feat_ref, weight_ref, weight_t_ref, mean_ref, gain_ref,
    conv_ref, sel_ref, sel_t_ref, sems,
):
    frames = feat_hbm.shape[0]
    last = pltpu.make_async_copy(feat_hbm.at[frames - 2 :], feat_ref.at[frames - 2 :], sems.at[0])
    rest = pltpu.make_async_copy(feat_hbm.at[: frames - 2], feat_ref.at[: frames - 2], sems.at[1])
    small = [
        pltpu.make_async_copy(src, dst, sems.at[2 + i])
        for i, (src, dst) in enumerate(
            (
                (conv_hbm, conv_ref),
                (sel_hbm, sel_ref),
                (sel_t_hbm, sel_t_ref),
                (gain_hbm, gain_ref),
                (mean_hbm, mean_ref),
            )
        )
    ]
    for copy in small:
        copy.start()
    last.start()
    rest.start()
    for copy in small:
        copy.wait()
    conv = conv_ref[...]
    for i in range(8):
        at = slice(CH * i, CH * i + CH)
        wide = slice(256 * i, 256 * i + 256)
        weight_ref[at, :] = dot_tn(conv, sel_ref[:, wide]).astype(BF16)
        weight_t_ref[:, at] = dot(sel_t_ref[wide, :], conv).astype(BF16)
    last.wait()
    sums = pair_sums(feat_ref, frames - 2, 0.5 * gain_ref[...], mean_ref[...], weight_ref[:, 128:])
    taps = sums.T
    for f in range(2):
        frame_sums(taps[64 * f : 64 * f + 64], out_ref, f)
    rest.wait()


def conv_kernel(
    feat_ref, gain_ref, mean_ref, weight_ref, up_hbm, down_hbm, out_ref, up_ref, down_ref, carry, sems
):
    copies = [
        pltpu.make_async_copy(up_hbm, up_ref, sems.at[0]),
        pltpu.make_async_copy(down_hbm, down_ref, sems.at[1]),
    ]
    for copy in copies:
        copy.start()
    carry[...] = jnp.zeros_like(carry)
    half_gain = 0.5 * gain_ref[...]
    mean_pair = mean_ref[...]

    @pl.loop(0, feat_ref.shape[0] // FORWARD_FRAMES)
    def _(step):
        for pair in range(FORWARD_FRAMES // 2):
            frame = step * FORWARD_FRAMES + 2 * pair
            sums = pair_sums(feat_ref, frame, half_gain, mean_pair, weight_ref[...])
            taps = (sums[:, :128] + carry[...]).T
            carry[...] = sums[:, 128:]
            for f in range(2):
                frame_sums(taps[64 * f : 64 * f + 64], out_ref, frame + f)

    for copy in copies:
        copy.wait()


VMEM = pl.BlockSpec(memory_space=pltpu.VMEM)
SMEM = pl.BlockSpec(memory_space=pltpu.SMEM)
ANYWHERE = pl.BlockSpec(memory_space=pl.ANY)


def megabytes(count):
    return pltpu.CompilerParams(vmem_limit_bytes=count * 1024 * 1024)


def conv_tail(features, *small):
    return pl.pallas_call(
        tail_kernel,
        in_specs=[ANYWHERE] * 6,
        out_specs=[VMEM] * 6,
        out_shape=[
            jax.ShapeDtypeStruct((2, 3, 8, COLS), F32),
            pltpu.VMEM(features.shape, BF16),
            pltpu.VMEM((1024, 256), BF16),
            pltpu.VMEM((256, 1024), BF16),
            pltpu.VMEM((256, 256), BF16),
            pltpu.VMEM((1, CH), F32),
        ],
        scratch_shapes=[
            pltpu.VMEM((81, CH), BF16),
            pltpu.VMEM((81, 2048), BF16),
            pltpu.VMEM((2048, 81), BF16),
            pltpu.SemaphoreType.DMA((7,)),
        ],
        compiler_params=megabytes(8),
        name="conv_tail",
    )(
        features, *small
    )


def conv_main(features, gain, mean_pair, weight, up, down):
    return pl.pallas_call(
        conv_kernel,
        in_specs=[VMEM] * 4 + [ANYWHERE] * 2,
        out_specs=[VMEM, ANYWHERE, ANYWHERE],
        out_shape=[
            jax.ShapeDtypeStruct((features.shape[0], 3, 8, COLS), F32),
            pltpu.VMEM(up.shape, BF16),
            pltpu.VMEM(down.shape, BF16),
        ],
        scratch_shapes=[pltpu.VMEM((COLS, 128), F32), pltpu.SemaphoreType.DMA((2,))],
        compiler_params=megabytes(12),
        cost_estimate=pl.CostEstimate(
            flops=2 * 16384 * 1024, bytes_accessed=20 * 1024 * 1024, transcendentals=2 * 2097152
        ),
        name="conv_main",
    )(features, gain, mean_pair, weight, up, down)


def lay_rows(groups):
    row = sublanes_of(groups[0].shape)
    both = jnp.where(row < 4, groups[0], roll(groups[1], 4, 1))
    return jnp.concatenate([both, groups[2]], axis=1)


def unless(is_edge, value):
    return jnp.where(is_edge, jnp.zeros_like(value), value)


def is_even(place_ref):
    return lax.rem(place_ref[0], 2) == 0


def rim_kernel(place_ref, sums_ref, prior_ref, inside_ref, across_ref, up, down):
    first_block = place_ref[1] == 0
    for o in range(3):
        for k, out_ref in ((0, up), (5, down)):
            out_ref[o] = sums_ref[:, o, k, :]
            out_ref[o, 0:2] = sums_ref[0:2, o, k, :] + unless(first_block, prior_ref[:, o, k, :])
    even = is_even(place_ref)
    inside_ref[...] = jnp.where(even, down[...], up[...])
    across_ref[...] = jnp.where(even, up[...], down[...])


def rims(place, sums, prior):
    shape = jax.ShapeDtypeStruct((3, sums.shape[0], COLS), F32)
    return pl.pallas_call(
        rim_kernel,
        in_specs=[SMEM] + [VMEM] * 2,
        out_specs=[VMEM] * 2,
        out_shape=[shape] * 2,
        scratch_shapes=[pltpu.VMEM(shape.shape, F32)] * 2,
        compiler_params=megabytes(4),
        name="rims",
    )(place, sums, prior)


def colour_kernel(own_ref, bias_ref, sums_ref, prior_ref, inside_ref, across_ref, *rest):
    out_refs, total = rest[:GROUP], rest[GROUP]
    total[...] = sums_ref[...]
    total[0:2] = sums_ref[0:2] + unless(own_ref[1] == 0, prior_ref[...])
    top, bottom = own_ref[0] == 0, own_ref[0] == own_ref[2] - 1
    row = sublanes_of((8, 8, COLS))
    me = lax.rem(own_ref[0], GROUP)
    even = is_even(own_ref)
    for turn in range(GROUP):
        frames = pl.ds(pl.multiple_of(lax.rem(me + turn, GROUP) * 8, 8), 8)
        groups = []
        for o in range(3):
            value = total[frames, o]
            inside, across = inside_ref[o, frames, :], across_ref[o, frames, :]
            above = unless(top, jnp.where(even, across, inside))
            below = unless(bottom, jnp.where(even, inside, across))
            value += jnp.where(row == 1, above[:, None, :], 0.0)
            value += jnp.where(row == 4, below[:, None, :], 0.0)
            groups.append(roll(value, -1, 1) + bias_ref[o])
        out_refs[turn][...] = lay_rows(groups).astype(BF16)


def colours(own, bias, sums, prior, inside, across):
    shape = jax.ShapeDtypeStruct((8, 16, COLS), BF16)
    return pl.pallas_call(
        colour_kernel,
        in_specs=[SMEM] * 2 + [VMEM] * 4,
        out_specs=[VMEM] * GROUP,
        out_shape=[shape] * GROUP,
        scratch_shapes=[pltpu.VMEM(sums.shape, F32)],
        compiler_params=megabytes(4),
        name="colours",
    )(own, bias, sums, prior, inside, across)


def swap_turns(parts):
    count = lax.axis_size("tile")
    out = [parts[0]]
    for turn in range(1, GROUP):
        pairs = [(i, i - i % GROUP + (i + turn) % GROUP) for i in range(count)]
        out.append(lax.ppermute(parts[turn], "tile", pairs))
    return out


def swap_rims(inside, across):
    count = lax.axis_size("tile")
    pairs = [(i, i + 1 - 2 * (i % 2)) for i in range(count)]
    others = [(i, min(max(i - 1 + 2 * (i % 2), 0), count - 1)) for i in range(count)]
    return lax.ppermute(inside, "tile", pairs), lax.ppermute(across, "tile", others)


def swap_blocks(x):
    row, group = sublanes_of(x.shape), lanes_of(x.shape) // 16
    for bit in (4, 2, 1):
        low = (row & bit) == 0
        same = low == ((group & bit) == 0)
        moved = jnp.where(
            low,
            roll(roll(x, -bit, 1), 16 * bit, 2),
            roll(roll(x, bit, 1), -16 * bit, 2),
        )
        x = jnp.where(same, x, moved)
    return x


def gather_patches(me, x_refs, strips):
    for turn in range(GROUP):
        strips[lax.rem(me + GROUP - turn, GROUP)] = x_refs[turn][...].astype(F32)
    first = sublanes_of((8, 8, COLS)) < 4
    pieces = [[], [], []]
    for half in range(2):
        even, odd = strips[2 * half], strips[2 * half + 1]
        pieces[0].append(jnp.where(first, even[:, :8], roll(odd[:, :8], 4, 1)))
        pieces[1].append(jnp.where(first, roll(even[:, :8], 4, 1), odd[:, :8]))
        pieces[2].append(jnp.where(first, even[:, 8:], roll(odd[:, 8:], 4, 1)))
    ordered = [swap_blocks(piece).reshape(64, 128) for group in pieces for piece in group]
    return jnp.concatenate(ordered, axis=1).astype(BF16)


def scatter_patches(me, grad, strips, out_refs):
    rows = [swap_blocks(grad[:, 128 * i : 128 * i + 128].reshape(8, 8, 128)) for i in range(6)]
    for half in range(2):
        groups = [rows[2 * o + half] for o in range(3)]
        strips[2 * half] = lay_rows(groups)
        strips[2 * half + 1] = lay_rows([roll(group, 4, 1) for group in groups])
    for turn in range(GROUP):
        out_refs[turn][...] = strips[lax.rem(me + turn, GROUP)].astype(BF16)


def normal_cdf(x):
    return 0.5 * (1.0 + lax.erf(x * 0.7071067811865476))


def pose_kernel(
    own_ref,
    x0_ref,
    x1_ref,
    x2_ref,
    x3_ref,
    frames_ref,
    counts_ref,
    key_rows_ref,
    key_cols_ref,
    key_vis_ref,
    key_spread_ref,
    gain_ref,
    up,
    down,
    order_hbm,
    patch_hbm,
    head_hbm,
    position_hbm,
    out0_ref,
    out1_ref,
    out2_ref,
    out3_ref,
    order,
    patch,
    head,
    position,
    strips,
    key_table,
    hidden_pre,
    hidden,
    pre_grad,
    sems,
):
    pairs = [(order_hbm, order), (patch_hbm, patch), (position_hbm, position), (head_hbm, head)]
    copies = [pltpu.make_async_copy(src, dst, sems.at[i]) for i, (src, dst) in enumerate(pairs)]
    for copy in copies:
        copy.start()
    token_row = own_ref[0] // GROUP
    me = lax.rem(own_ref[0], GROUP)
    first_frame = pl.multiple_of(me * 8, 8)

    frame = sublanes_of((8, 32)) + first_frame
    hit = jnp.zeros((8, 32), F32)
    for slot in range(3):
        used = frames_ref[slot] == frame
        hit = jnp.maximum(hit, jnp.where(used & (counts_ref[...] > slot), 1.0, 0.0))
    weight = jnp.max(hit, axis=1, keepdims=True)
    spread = key_spread_ref[...]

    def own_keys(ref):
        key_table[...] = dot_tn(ref[...].astype(F32).astype(BF16), spread)
        return key_table[pl.ds(first_frame, 8), :]

    def by_token(value):
        return jnp.broadcast_to(value[:, None, :], (8, 8, HEAD)).reshape(64, HEAD)

    token_column = sublanes_of((64, HEAD)) % 8
    column = lanes_of((64, HEAD))
    pixel_row = token_row * 4 + column // (4 * KP)
    pixel_col = token_column * 4 + (column // KP) % 4
    row_gap = pixel_row.astype(F32) - by_token(own_keys(key_rows_ref))
    col_gap = pixel_col.astype(F32) - by_token(own_keys(key_cols_ref))
    target = jnp.exp((row_gap * row_gap + col_gap * col_gap) * -0.125)
    mask = by_token(own_keys(key_vis_ref) * weight)

    raw = gather_patches(me, (x0_ref, x1_ref, x2_ref, x3_ref), strips)
    copies[0].wait()
    patches = dot(raw, order[...]).astype(BF16)
    copies[1].wait()
    copies[2].wait()
    pair_rows = pl.ds(pl.multiple_of(token_row // 2 * 16, 16), 16)
    two = position[pair_rows, :].astype(F32)
    places = jnp.where(lax.rem(token_row, 2) == 0, two[:8], two[8:])
    places = jnp.broadcast_to(places[None], (8, 8, DP)).reshape(64, DP)
    embedded = dot(patches, patch[...]) + places
    centred = embedded - jnp.mean(embedded, axis=-1, keepdims=True)
    inverse = lax.rsqrt(jnp.mean(centred * centred, axis=-1, keepdims=True) + NORM_EPS)
    unit_rows = centred * inverse
    gain = jnp.concatenate([gain_ref[i : i + 1] for i in range(DP // 128)], axis=1)
    normed_tokens = (unit_rows * gain).astype(BF16)

    for i in range(HID // 256):
        at = slice(256 * i, 256 * i + 256)
        value = dot(normed_tokens, up[:, at])
        hidden_pre[:, at] = value
        hidden[:, at] = (value * normal_cdf(value)).astype(BF16)

    block = dot(hidden[...], down[...])
    block_round = (embedded + block).astype(BF16)
    copies[3].wait()
    heatmap = dot_nt(block_round, head[...])
    heat_grad = ((heatmap - target) * mask).astype(BF16)
    out_grad = dot(heat_grad, head[...])
    out_round = out_grad.astype(BF16)

    for i in range(HID // 256):
        at = slice(256 * i, 256 * i + 256)
        grad = dot_nt(out_round, down[at, :])
        pre = hidden_pre[:, at]
        slope = normal_cdf(pre) + pre * jnp.exp(-0.5 * pre * pre) * 0.3989422804014327
        pre_grad[:, at] = (grad * slope).astype(BF16)

    normed_grad = dot_nt(pre_grad[...], up[...])
    unit_grad = normed_grad * gain
    embed_grad = out_grad + inverse * (
        unit_grad
        - jnp.mean(unit_grad, axis=-1, keepdims=True)
        - unit_rows * jnp.mean(unit_grad * unit_rows, axis=-1, keepdims=True)
    )
    colour_grad = dot_nt(embed_grad.astype(BF16), patch[...]).astype(BF16)
    outs = (out0_ref, out1_ref, out2_ref, out3_ref)
    scatter_patches(me, dot_nt(colour_grad, order[...]), strips, outs)


def pose(own, parts, frames, counts, key_rows, key_cols, key_vis, gain, up, down, patch, head, position):
    return pl.pallas_call(
        pose_kernel,
        in_specs=[SMEM] + [VMEM] * 13 + [ANYWHERE] * 4,
        out_specs=[VMEM] * GROUP,
        out_shape=[jax.ShapeDtypeStruct((8, 16, COLS), BF16)] * GROUP,
        scratch_shapes=[
            pltpu.VMEM((768, 768), BF16),
            pltpu.VMEM((768, DP), BF16),
            pltpu.VMEM((HEAD, DP), BF16),
            pltpu.VMEM((64, DP), BF16),
            pltpu.VMEM((GROUP, 8, 16, COLS), F32),
            pltpu.VMEM((32, HEAD), F32),
            pltpu.VMEM((64, HID), F32),
            pltpu.VMEM((64, HID), BF16),
            pltpu.VMEM((64, HID), BF16),
            pltpu.SemaphoreType.DMA((4,)),
        ],
        compiler_params=megabytes(20),
        cost_estimate=pl.CostEstimate(
            flops=2 * 64 * 15800000, bytes_accessed=17 * 1024 * 1024, transcendentals=64 * HID * 3
        ),
        name="pose",
    )(
        own,
        *parts,
        frames,
        counts,
        key_rows,
        key_cols,
        key_vis,
        jnp.asarray(KEY_SPREAD),
        gain,
        up,
        down,
        jnp.asarray(PIXEL_ORDER),
        patch,
        head,
        position,
    )


def strip_kernel(own_ref, x0_ref, x1_ref, x2_ref, x3_ref, out_ref, inside_ref, across_ref):
    me = lax.rem(own_ref[0], GROUP)
    first = sublanes_of((8, 8, COLS)) < 4
    for turn, ref in enumerate((x0_ref, x1_ref, x2_ref, x3_ref)):
        frames = pl.ds(pl.multiple_of(lax.rem(me + GROUP - turn, GROUP) * 8, 8), 8)
        value = ref[...].astype(F32)
        groups = [value[:, :8], roll(value[:, :8], 4, 1), value[:, 8:]]
        for o in range(3):
            out_ref[frames, o] = roll(jnp.where(first, groups[o], 0.0), 1, 1)
    even = is_even(own_ref)
    for o in range(3):
        upper, lower = out_ref[:, o, 1, :], out_ref[:, o, 4, :]
        inside_ref[o] = jnp.where(even, lower, upper)
        across_ref[o] = jnp.where(even, upper, lower)


def strip_grads(own, parts):
    rim = jax.ShapeDtypeStruct((3, 32, COLS), F32)
    return pl.pallas_call(
        strip_kernel,
        in_specs=[SMEM] + [VMEM] * GROUP,
        out_specs=[VMEM] * 3,
        out_shape=[jax.ShapeDtypeStruct((32, 3, 8, COLS), F32), rim, rim],
        compiler_params=megabytes(4),
        name="strip_grads",
    )(own, *parts)


def whole_kernel(place_ref, x_ref, inside_ref, across_ref, out_ref, first_ref):
    row = sublanes_of((32, 8, COLS))
    top, bottom = place_ref[0] == 0, place_ref[0] == place_ref[2] - 1
    even = is_even(place_ref)
    for o in range(3):
        above = unless(top, jnp.where(even, across_ref[o], inside_ref[o]))
        below = unless(bottom, jnp.where(even, inside_ref[o], across_ref[o]))
        value = jnp.where(row == 0, above[:, None, :], x_ref[:, o])
        value = jnp.where(row == 5, below[:, None, :], value)
        out_ref[:, o] = value
        first_ref[:, o] = value[:2]


def whole_grads(place, x, inside, across):
    return pl.pallas_call(
        whole_kernel,
        in_specs=[SMEM] + [VMEM] * 3,
        out_specs=[VMEM] * 2,
        out_shape=[
            jax.ShapeDtypeStruct(x.shape, F32),
            jax.ShapeDtypeStruct((2, 3, 8, COLS), F32),
        ],
        compiler_params=megabytes(4),
        name="whole_grads",
    )(place, x, inside, across)


def frame_taps(groups):
    row = sublanes_of((8, COLS))
    taps = [from_right(g) for g in groups] + list(groups) + [from_left(g) for g in groups]
    last = taps.pop()
    for i in range(3):
        taps[i] = jnp.where(row >= 6, roll(last, 6 - 2 * i, 0), taps[i])
    return taps


def pair_taps(ref, frame):
    rows = []
    for f in range(2):
        rows += frame_taps([ref[frame + f, o] for o in range(3)])
    return jnp.concatenate(rows, axis=0).T


def prepare_kernel(start, feat_ref, gain_ref, mean_ref, slope_ref, normed_ref):
    half_gain = 0.5 * gain_ref[...]
    mean_pair = mean_ref[...]
    places = [(tau, r) for tau in range(2) for r in range(ROWS)]

    @pl.loop(0, slope_ref.shape[0] // 2)
    def _(pair):
        xs = [feat_ref[start + 2 * pair + tau, r].astype(F32) for tau, r in places]
        means = channel_means([x * x for x in xs], mean_pair)
        for x, mean, (tau, r) in zip(xs, means, places):
            rescale = lax.rsqrt(mean + NORM_EPS)
            normed = x * rescale
            half_pre = normed * half_gain
            tanh = jnp.tanh(half_pre)
            slope = (1.0 + tanh) * (1.0 + half_pre * (1.0 - tanh)) * half_gain
            slope_ref[2 * pair + tau, r] = (slope * rescale).astype(BF16)
            normed_ref[2 * pair + tau, r] = normed.astype(BF16)


def prepare(start, count, features, gain, mean_pair):
    kept = pltpu.VMEM((count, ROWS, COLS, CH), BF16)
    return pl.pallas_call(
        functools.partial(prepare_kernel, start),
        in_specs=[VMEM] * 3,
        out_specs=[VMEM] * 2,
        out_shape=[kept] * 2,
        compiler_params=megabytes(8),
        cost_estimate=pl.CostEstimate(
            flops=10**9, bytes_accessed=10**5 * count, transcendentals=65536 * count
        ),
        name="prepare_%d" % start,
    )(features, gain, mean_pair)


def back_pair(kept, frame, taps, weight, mean_pair, store):
    slope_ref, normed_ref = kept
    grads = dot(taps, weight)
    places = [(tau, r) for tau in range(2) for r in range(ROWS)]
    for part in range(0, len(places), BACK_ROWS):
        group = places[part : part + BACK_ROWS]
        pairs = []
        for i, (tau, r) in enumerate(group):
            at = CH * (part + i)
            scaled = grads[:, at : at + CH] * slope_ref[frame + tau, r].astype(F32)
            pairs.append((scaled, normed_ref[frame + tau, r].astype(F32)))
        along = channel_means([scaled * normed for scaled, normed in pairs], mean_pair)
        for (scaled, normed), mean, (tau, r) in zip(pairs, along, group):
            store(tau, r, (scaled - normed * mean).astype(BF16))


def back_kernel(*refs):
    kept = refs[:-7]
    grad_ref, mean_ref, weight_ref, out_hbm, buffer, carry, sems = refs[-7:]
    mean_pair = mean_ref[...]
    carry[...] = pair_taps(grad_ref, 0)
    last_pair = grad_ref.shape[0] - 2
    copies = []
    for step in range(len(kept) // 2):
        base = step * BACK_FRAMES
        count = min(BACK_FRAMES, last_pair - base)
        slot = step % 2
        if step >= 2:
            copies[step - 2].wait()
        for pair in range(count // 2):
            now = carry[...]
            later = pair_taps(grad_ref, base + 2 * pair + 2)
            carry[...] = later
            taps = jnp.concatenate([now, later], axis=1).astype(BF16)

            def store(tau, r, value):
                buffer[slot, 2 * pair + tau, r] = value

            back_pair(kept[2 * step : 2 * step + 2], 2 * pair, taps, weight_ref[...], mean_pair, store)
        copies.append(
            pltpu.make_async_copy(
                buffer.at[slot, :count], out_hbm.at[base : base + count], sems.at[slot]
            )
        )
        copies[-1].start()
    for copy in copies[-2:]:
        copy.wait()


def last_kernel(
    place_ref, slope_ref, normed_ref, grad_ref, next_ref, mean_ref, weight_ref, prior_hbm,
    out_hbm, buffer, sem,
):
    del prior_hbm
    frame = grad_ref.shape[0] - 2
    last_block = place_ref[1] == place_ref[3] - 1
    later = unless(last_block, pair_taps(next_ref, 0))
    taps = jnp.concatenate([pair_taps(grad_ref, frame), later], axis=1).astype(BF16)

    def store(tau, r, value):
        buffer[tau, r] = value

    kept = (slope_ref, normed_ref)
    back_pair(kept, BACK_FRAMES - 2, taps, weight_ref[...], mean_ref[...], store)
    copy = pltpu.make_async_copy(buffer, out_hbm.at[frame:], sem)
    copy.start()
    copy.wait()


def conv_backward(place, kept, grads, later, mean_pair, weight):
    out_shape = jax.ShapeDtypeStruct((grads.shape[0], ROWS, COLS, CH), BF16)
    part = pl.pallas_call(
        back_kernel,
        in_specs=[VMEM] * (len(kept) * 2 + 3),
        out_specs=ANYWHERE,
        out_shape=out_shape,
        scratch_shapes=[
            pltpu.VMEM((2, BACK_FRAMES, ROWS, COLS, CH), BF16),
            pltpu.VMEM((COLS, 128), F32),
            pltpu.SemaphoreType.DMA((2,)),
        ],
        compiler_params=megabytes(16),
        cost_estimate=pl.CostEstimate(
            flops=2 * 16384 * 1024, bytes_accessed=9 * 1024 * 1024, transcendentals=2 * 2097152
        ),
        name="conv_back",
    )(*[x for pair in kept for x in pair], grads, mean_pair, weight)
    return pl.pallas_call(
        last_kernel,
        in_specs=[SMEM] + [VMEM] * 6 + [ANYWHERE],
        out_specs=ANYWHERE,
        out_shape=out_shape,
        input_output_aliases={7: 0},
        scratch_shapes=[pltpu.VMEM((2, ROWS, COLS, CH), BF16), pltpu.SemaphoreType.DMA],
        compiler_params=megabytes(12),
        name="conv_last",
    )(place, *kept[-1], grads, later, mean_pair, weight, part)


def per_device(
    features,
    norm_gain,
    conv_weight,
    colour_bias,
    observed_frames,
    observed_counts,
    key_rows,
    key_columns,
    key_visible,
    position_table,
    patch_weight,
    layer_gain,
    up_weight,
    down_weight,
    head_weight,
):
    tm_count = lax.axis_size("tm")
    own = jnp.stack(
        [
            lax.axis_index("tile"),
            lax.axis_index("tm"),
            jnp.int32(lax.axis_size("tile")),
            jnp.int32(tm_count),
        ]
    )
    gain = norm_gain.reshape(1, CH)
    features, layer_gain, own = lax.optimization_barrier(
        (features, layer_gain.reshape(DP // 128, 128), own)
    )
    features = pltpu.with_memory_space_constraint(features, pltpu.HBM)
    up_weight = pltpu.with_memory_space_constraint(up_weight, pltpu.HBM)
    down_weight = pltpu.with_memory_space_constraint(down_weight, pltpu.HBM)
    gain = pltpu.with_memory_space_constraint(gain, pltpu.HBM)
    consts = [jnp.asarray(x) for x in (MEAN_PAIR, SELECTOR, SELECTOR_T)]
    mean_pair, sel, sel_t = [pltpu.with_memory_space_constraint(x, pltpu.HBM) for x in consts]
    conv_weight = pltpu.with_memory_space_constraint(conv_weight.T, pltpu.HBM)
    tail, features, weight, weight_t, mean_pair, gain = conv_tail(
        features, gain, mean_pair, conv_weight, sel, sel_t
    )
    prior = lax.ppermute(tail, "tm", [(i, (i + 1) % tm_count) for i in range(tm_count)])
    sums, up, down = conv_main(features, gain, mean_pair, weight, up_weight, down_weight)
    def prepare_beside(chunk, *moving):
        kept.append(prepare(chunk * BACK_FRAMES, BACK_FRAMES, features, gain, mean_pair))
        *moving, kept[-1] = lax.optimization_barrier((*moving, kept[-1]))
        return moving

    kept = []
    rim_sums = prepare_beside(0, *swap_rims(*rims(own, sums, prior)))
    parts = swap_turns(colours(own, colour_bias, sums, prior, *rim_sums))
    parts = prepare_beside(1, *parts)
    parts = pose(
        own,
        parts,
        observed_frames.transpose(2, 0, 1),
        observed_counts,
        key_rows.T,
        key_columns.T,
        key_visible.T,
        layer_gain,
        up,
        down,
        patch_weight,
        head_weight.T,
        position_table,
    )
    grads, inside, across = strip_grads(own, prepare_beside(2, *swap_turns(parts)))
    rim_grads = prepare_beside(3, *swap_rims(inside, across))
    grads, first = whole_grads(own, grads, *rim_grads)
    later = lax.ppermute(first, "tm", [((i + 1) % tm_count, i) for i in range(tm_count)])
    return conv_backward(own, kept, grads, later, mean_pair, weight_t)


def solution(mesh):
    in_specs = (
        P("tm", "tile", None, None),
        P(),
        P(),
        P(),
        P("tm", None, None),
        P("tm", None),
        P("tm", None),
        P("tm", None),
        P("tm", None),
        P(),
        P(),
        P(),
        P(),
        P(),
        P(),
    )
    return jax.shard_map(
        per_device,
        mesh=mesh,
        in_specs=in_specs,
        out_specs=P("tm", "tile", None, None),
        check_vma=False,
    )
```

```python
import functools

import jax
import jax.numpy as jnp
import ml_dtypes
import numpy as np
from jax import lax
from jax.experimental import pallas as pl
from jax.experimental.pallas import tpu as pltpu
from jax.sharding import PartitionSpec as P

CH = 128
DP = 1280
HID = 2560
PATCH = 16
KP = 17
HEAD = 272
COLS = 128
ROWS = 4
GROUP = 4
FORWARD_FRAMES = 8
BACK_FRAMES = 8
BACK_ROWS = 4
NORM_EPS = 1e-06
F32 = jnp.float32
BF16 = jnp.bfloat16


def slot_of(c, o, k):
    group = 3 * c + o
    if group < 8:
        return 8 * group + k
    return 8 * (k // 2) + 6 + k % 2


def make_selector():
    table = np.zeros((81, 2, ROWS, 256), np.float32)
    for tau in range(2):
        for r in range(ROWS):
            for f in range(4):
                a = tau + 2 - f
                if not 0 <= a <= 2:
                    continue
                for k in range(6):
                    b = r + 2 - k
                    if not 0 <= b <= 2:
                        continue
                    for c in range(3):
                        for o in range(3):
                            table[3 * (9 * a + 3 * b + c) + o, tau, r, 64 * f + slot_of(c, o, k)] = 1
    return table.reshape(81, 2048)


def make_pixel_order():
    table = np.zeros((768, 768), np.float32)
    for o in range(3):
        for pixel in range(256):
            table[256 * o + pixel, 3 * pixel + o] = 1
    return table


def make_key_spread():
    table = np.zeros((KP, HEAD), np.float32)
    table[np.arange(HEAD) % KP, np.arange(HEAD)] = 1
    return table


SELECTOR = make_selector().astype(ml_dtypes.bfloat16)
SELECTOR_T = np.ascontiguousarray(make_selector().T).astype(ml_dtypes.bfloat16)
PIXEL_ORDER = make_pixel_order().astype(ml_dtypes.bfloat16)
KEY_SPREAD = make_key_spread().astype(ml_dtypes.bfloat16)
MEAN_PAIR = (np.kron(np.eye(2), np.ones((CH, CH))) / CH).astype(ml_dtypes.bfloat16)


def dot(a, b):
    return jnp.dot(a, b, preferred_element_type=F32)


def dot_tn(a, b):
    return lax.dot_general(a, b, (((0,), (0,)), ((), ())), preferred_element_type=F32)


def dot_nt(a, b):
    return lax.dot_general(a, b, (((1,), (1,)), ((), ())), preferred_element_type=F32)


def roll(x, shift, axis):
    shift %= x.shape[axis]
    return pltpu.roll(x, shift, axis) if shift else x


def channel_means(values, mean_pair):
    rounded = [value.astype(BF16) for value in values]
    pairs = [jnp.concatenate(rounded[i : i + 2], axis=1) for i in range(0, len(values), 2)]
    means = dot(jnp.concatenate(pairs, axis=0), mean_pair)
    out = []
    for i in range(len(pairs)):
        rows = slice(COLS * i, COLS * i + COLS)
        out += [means[rows, :CH], means[rows, CH:]]
    return out


def lanes_of(shape):
    return lax.broadcasted_iota(jnp.int32, shape, len(shape) - 1)


def sublanes_of(shape):
    return lax.broadcasted_iota(jnp.int32, shape, len(shape) - 2)


def from_left(x):
    return jnp.where(lanes_of(x.shape) >= 1, roll(x, 1, x.ndim - 1), 0.0)


def from_right(x):
    return jnp.where(lanes_of(x.shape) < COLS - 1, roll(x, -1, x.ndim - 1), 0.0)


def activated_rows(feat_ref, frame, half_gain, mean_pair):
    xs = [feat_ref[frame, r].astype(F32) for r in range(ROWS)]
    acts = []
    for x, mean in zip(xs, channel_means([x * x for x in xs], mean_pair)):
        half = x * lax.rsqrt(mean + NORM_EPS) * half_gain
        acts.append((half + half * jnp.tanh(half)).astype(BF16))
    return acts


def frame_sums(taps, out_ref, frame):
    groups = [taps[8 * g : 8 * g + 8] for g in range(8)]
    row = sublanes_of((8, COLS))
    groups.append(
        jnp.where(
            row < 2,
            roll(groups[0], 2, 0),
            jnp.where(row < 4, roll(groups[1], 4, 0), roll(groups[2], 6, 0)),
        )
    )
    for o in range(3):
        out_ref[frame, o] = from_left(groups[o]) + groups[3 + o] + from_right(groups[6 + o])


def pair_sums(feat_ref, frame, half_gain, mean_pair, weight):
    acts = []
    for tau in range(2):
        acts += activated_rows(feat_ref, frame + tau, half_gain, mean_pair)
    return dot(jnp.concatenate(acts, axis=1), weight)


def tail_kernel(
    feat_hbm, gain_hbm, mean_hbm, conv_hbm, sel_hbm, sel_t_hbm,
    out_ref, feat_ref, weight_ref, weight_t_ref, mean_ref, gain_ref,
    conv_ref, sel_ref, sel_t_ref, sems,
):
    frames = feat_hbm.shape[0]
    last = pltpu.make_async_copy(feat_hbm.at[frames - 2 :], feat_ref.at[frames - 2 :], sems.at[0])
    rest = pltpu.make_async_copy(feat_hbm.at[: frames - 2], feat_ref.at[: frames - 2], sems.at[1])
    small = [
        pltpu.make_async_copy(src, dst, sems.at[2 + i])
        for i, (src, dst) in enumerate(
            (
                (conv_hbm, conv_ref),
                (sel_hbm, sel_ref),
                (sel_t_hbm, sel_t_ref),
                (gain_hbm, gain_ref),
                (mean_hbm, mean_ref),
            )
        )
    ]
    for copy in small:
        copy.start()
    last.start()
    rest.start()
    for copy in small:
        copy.wait()
    conv = conv_ref[...]
    for i in range(8):
        at = slice(CH * i, CH * i + CH)
        wide = slice(256 * i, 256 * i + 256)
        weight_ref[at, :] = dot_tn(conv, sel_ref[:, wide]).astype(BF16)
        weight_t_ref[:, at] = dot(sel_t_ref[wide, :], conv).astype(BF16)
    last.wait()
    sums = pair_sums(feat_ref, frames - 2, 0.5 * gain_ref[...], mean_ref[...], weight_ref[:, 128:])
    taps = sums.T
    for f in range(2):
        frame_sums(taps[64 * f : 64 * f + 64], out_ref, f)
    rest.wait()


def conv_kernel(
    feat_ref, gain_ref, mean_ref, weight_ref, up_hbm, down_hbm, out_ref, up_ref, down_ref, carry, sems
):
    copies = [
        pltpu.make_async_copy(up_hbm, up_ref, sems.at[0]),
        pltpu.make_async_copy(down_hbm, down_ref, sems.at[1]),
    ]
    for copy in copies:
        copy.start()
    carry[...] = jnp.zeros_like(carry)
    half_gain = 0.5 * gain_ref[...]
    mean_pair = mean_ref[...]

    @pl.loop(0, feat_ref.shape[0] // FORWARD_FRAMES)
    def _(step):
        for pair in range(FORWARD_FRAMES // 2):
            frame = step * FORWARD_FRAMES + 2 * pair
            sums = pair_sums(feat_ref, frame, half_gain, mean_pair, weight_ref[...])
            taps = (sums[:, :128] + carry[...]).T
            carry[...] = sums[:, 128:]
            for f in range(2):
                frame_sums(taps[64 * f : 64 * f + 64], out_ref, frame + f)

    for copy in copies:
        copy.wait()


VMEM = pl.BlockSpec(memory_space=pltpu.VMEM)
SMEM = pl.BlockSpec(memory_space=pltpu.SMEM)
ANYWHERE = pl.BlockSpec(memory_space=pl.ANY)


def megabytes(count):
    return pltpu.CompilerParams(vmem_limit_bytes=count * 1024 * 1024)


def conv_tail(features, *small):
    return pl.pallas_call(
        tail_kernel,
        in_specs=[ANYWHERE] * 6,
        out_specs=[VMEM] * 6,
        out_shape=[
            jax.ShapeDtypeStruct((2, 3, 8, COLS), F32),
            pltpu.VMEM(features.shape, BF16),
            pltpu.VMEM((1024, 256), BF16),
            pltpu.VMEM((256, 1024), BF16),
            pltpu.VMEM((256, 256), BF16),
            pltpu.VMEM((1, CH), F32),
        ],
        scratch_shapes=[
            pltpu.VMEM((81, CH), BF16),
            pltpu.VMEM((81, 2048), BF16),
            pltpu.VMEM((2048, 81), BF16),
            pltpu.SemaphoreType.DMA((7,)),
        ],
        compiler_params=megabytes(8),
        name="conv_tail",
    )(
        features, *small
    )


def conv_main(features, gain, mean_pair, weight, up, down):
    return pl.pallas_call(
        conv_kernel,
        in_specs=[VMEM] * 4 + [ANYWHERE] * 2,
        out_specs=[VMEM, ANYWHERE, ANYWHERE],
        out_shape=[
            jax.ShapeDtypeStruct((features.shape[0], 3, 8, COLS), F32),
            pltpu.VMEM(up.shape, BF16),
            pltpu.VMEM(down.shape, BF16),
        ],
        scratch_shapes=[pltpu.VMEM((COLS, 128), F32), pltpu.SemaphoreType.DMA((2,))],
        compiler_params=megabytes(12),
        cost_estimate=pl.CostEstimate(
            flops=2 * 16384 * 1024, bytes_accessed=20 * 1024 * 1024, transcendentals=2 * 2097152
        ),
        name="conv_main",
    )(features, gain, mean_pair, weight, up, down)


def lay_rows(groups):
    row = sublanes_of(groups[0].shape)
    both = jnp.where(row < 4, groups[0], roll(groups[1], 4, 1))
    return jnp.concatenate([both, groups[2]], axis=1)


def unless(is_edge, value):
    return jnp.where(is_edge, jnp.zeros_like(value), value)


def is_even(place_ref):
    return lax.rem(place_ref[0], 2) == 0


def rim_kernel(place_ref, sums_ref, prior_ref, inside_ref, across_ref, up, down):
    first_block = place_ref[1] == 0
    for o in range(3):
        for k, out_ref in ((0, up), (5, down)):
            out_ref[o] = sums_ref[:, o, k, :]
            out_ref[o, 0:2] = sums_ref[0:2, o, k, :] + unless(first_block, prior_ref[:, o, k, :])
    even = is_even(place_ref)
    inside_ref[...] = jnp.where(even, down[...], up[...]).astype(BF16)
    across_ref[...] = jnp.where(even, up[...], down[...]).astype(BF16)


def rims(place, sums, prior):
    shape = jax.ShapeDtypeStruct((3, sums.shape[0], COLS), BF16)
    return pl.pallas_call(
        rim_kernel,
        in_specs=[SMEM] + [VMEM] * 2,
        out_specs=[VMEM] * 2,
        out_shape=[shape] * 2,
        scratch_shapes=[pltpu.VMEM(shape.shape, F32)] * 2,
        compiler_params=megabytes(4),
        name="rims",
    )(place, sums, prior)


def colour_kernel(own_ref, bias_ref, sums_ref, prior_ref, inside_ref, across_ref, *rest):
    out_refs, (total, above_rim, below_rim) = rest[:GROUP], rest[GROUP:]
    total[...] = sums_ref[...]
    total[0:2] = sums_ref[0:2] + unless(own_ref[1] == 0, prior_ref[...])
    top, bottom = own_ref[0] == 0, own_ref[0] == own_ref[2] - 1
    row = sublanes_of((8, 8, COLS))
    me = lax.rem(own_ref[0], GROUP)
    even = is_even(own_ref)
    inside, across = inside_ref[...].astype(F32), across_ref[...].astype(F32)
    above_rim[...] = unless(top, jnp.where(even, across, inside))
    below_rim[...] = unless(bottom, jnp.where(even, inside, across))
    for turn in range(GROUP):
        frames = pl.ds(pl.multiple_of(lax.rem(me + turn, GROUP) * 8, 8), 8)
        groups = []
        for o in range(3):
            value = total[frames, o]
            value += jnp.where(row == 1, above_rim[o, frames, :][:, None, :], 0.0)
            value += jnp.where(row == 4, below_rim[o, frames, :][:, None, :], 0.0)
            groups.append(roll(value, -1, 1) + bias_ref[o])
        out_refs[turn][...] = lay_rows(groups).astype(BF16)


def colours(own, bias, sums, prior, inside, across):
    shape = jax.ShapeDtypeStruct((8, 16, COLS), BF16)
    return pl.pallas_call(
        colour_kernel,
        in_specs=[SMEM] * 2 + [VMEM] * 4,
        out_specs=[VMEM] * GROUP,
        out_shape=[shape] * GROUP,
        scratch_shapes=[pltpu.VMEM(sums.shape, F32)]
        + [pltpu.VMEM((3, sums.shape[0], COLS), F32)] * 2,
        compiler_params=megabytes(4),
        name="colours",
    )(own, bias, sums, prior, inside, across)


def swap_turns(parts):
    count = lax.axis_size("tile")
    out = [parts[0]]
    for turn in range(1, GROUP):
        pairs = [(i, i - i % GROUP + (i + turn) % GROUP) for i in range(count)]
        out.append(lax.ppermute(parts[turn], "tile", pairs))
    return out


def swap_rims(inside, across):
    count = lax.axis_size("tile")
    pairs = [(i, i + 1 - 2 * (i % 2)) for i in range(count)]
    others = [(i, min(max(i - 1 + 2 * (i % 2), 0), count - 1)) for i in range(count)]
    return lax.ppermute(inside, "tile", pairs), lax.ppermute(across, "tile", others)


def swap_blocks(x):
    row, group = sublanes_of(x.shape), lanes_of(x.shape) // 16
    for bit in (4, 2, 1):
        low = (row & bit) == 0
        same = low == ((group & bit) == 0)
        moved = jnp.where(
            low,
            roll(roll(x, -bit, 1), 16 * bit, 2),
            roll(roll(x, bit, 1), -16 * bit, 2),
        )
        x = jnp.where(same, x, moved)
    return x


def gather_patches(me, x_refs, strips):
    for turn in range(GROUP):
        strips[lax.rem(me + GROUP - turn, GROUP)] = x_refs[turn][...].astype(F32)
    first = sublanes_of((8, 8, COLS)) < 4
    pieces = [[], [], []]
    for half in range(2):
        even, odd = strips[2 * half], strips[2 * half + 1]
        pieces[0].append(jnp.where(first, even[:, :8], roll(odd[:, :8], 4, 1)))
        pieces[1].append(jnp.where(first, roll(even[:, :8], 4, 1), odd[:, :8]))
        pieces[2].append(jnp.where(first, even[:, 8:], roll(odd[:, 8:], 4, 1)))
    ordered = [swap_blocks(piece).reshape(64, 128) for group in pieces for piece in group]
    return jnp.concatenate(ordered, axis=1).astype(BF16)


def scatter_patches(me, grad, strips, out_refs):
    rows = [swap_blocks(grad[:, 128 * i : 128 * i + 128].reshape(8, 8, 128)) for i in range(6)]
    for half in range(2):
        groups = [rows[2 * o + half] for o in range(3)]
        strips[2 * half] = lay_rows(groups)
        strips[2 * half + 1] = lay_rows([roll(group, 4, 1) for group in groups])
    for turn in range(GROUP):
        out_refs[turn][...] = strips[lax.rem(me + turn, GROUP)].astype(BF16)


def normal_cdf(x):
    return 0.5 * (1.0 + lax.erf(x * 0.7071067811865476))


def pose_kernel(
    own_ref,
    x0_ref,
    x1_ref,
    x2_ref,
    x3_ref,
    frames_ref,
    counts_ref,
    key_rows_ref,
    key_cols_ref,
    key_vis_ref,
    key_spread_ref,
    gain_ref,
    up,
    down,
    order_hbm,
    patch_hbm,
    head_hbm,
    position_hbm,
    out0_ref,
    out1_ref,
    out2_ref,
    out3_ref,
    order,
    patch,
    head,
    position,
    strips,
    key_table,
    hidden_pre,
    hidden,
    pre_grad,
    sems,
):
    pairs = [(order_hbm, order), (patch_hbm, patch), (position_hbm, position), (head_hbm, head)]
    copies = [pltpu.make_async_copy(src, dst, sems.at[i]) for i, (src, dst) in enumerate(pairs)]
    for copy in copies:
        copy.start()
    token_row = own_ref[0] // GROUP
    me = lax.rem(own_ref[0], GROUP)
    first_frame = pl.multiple_of(me * 8, 8)

    frame = sublanes_of((8, 32)) + first_frame
    hit = jnp.zeros((8, 32), F32)
    for slot in range(3):
        used = frames_ref[slot] == frame
        hit = jnp.maximum(hit, jnp.where(used & (counts_ref[...] > slot), 1.0, 0.0))
    weight = jnp.max(hit, axis=1, keepdims=True)
    spread = key_spread_ref[...]

    def own_keys(ref):
        key_table[...] = dot_tn(ref[...].astype(F32).astype(BF16), spread)
        return key_table[pl.ds(first_frame, 8), :]

    def by_token(value):
        return jnp.broadcast_to(value[:, None, :], (8, 8, HEAD)).reshape(64, HEAD)

    token_column = sublanes_of((64, HEAD)) % 8
    column = lanes_of((64, HEAD))
    pixel_row = token_row * 4 + column // (4 * KP)
    pixel_col = token_column * 4 + (column // KP) % 4
    row_gap = pixel_row.astype(F32) - by_token(own_keys(key_rows_ref))
    col_gap = pixel_col.astype(F32) - by_token(own_keys(key_cols_ref))
    target = jnp.exp((row_gap * row_gap + col_gap * col_gap) * -0.125)
    mask = by_token(own_keys(key_vis_ref) * weight)

    raw = gather_patches(me, (x0_ref, x1_ref, x2_ref, x3_ref), strips)
    copies[0].wait()
    patches = dot(raw, order[...]).astype(BF16)
    copies[1].wait()
    copies[2].wait()
    pair_rows = pl.ds(pl.multiple_of(token_row // 2 * 16, 16), 16)
    two = position[pair_rows, :].astype(F32)
    places = jnp.where(lax.rem(token_row, 2) == 0, two[:8], two[8:])
    places = jnp.broadcast_to(places[None], (8, 8, DP)).reshape(64, DP)
    embedded = dot(patches, patch[...]) + places
    centred = embedded - jnp.mean(embedded, axis=-1, keepdims=True)
    inverse = lax.rsqrt(jnp.mean(centred * centred, axis=-1, keepdims=True) + NORM_EPS)
    unit_rows = centred * inverse
    gain = jnp.concatenate([gain_ref[i : i + 1] for i in range(DP // 128)], axis=1)
    normed_tokens = (unit_rows * gain).astype(BF16)

    for i in range(HID // 256):
        at = slice(256 * i, 256 * i + 256)
        value = dot(normed_tokens, up[:, at])
        hidden_pre[:, at] = value
        hidden[:, at] = (value * normal_cdf(value)).astype(BF16)

    block = dot(hidden[...], down[...])
    block_round = (embedded + block).astype(BF16)
    copies[3].wait()
    heatmap = dot_nt(block_round, head[...])
    heat_grad = ((heatmap - target) * mask).astype(BF16)
    out_grad = dot(heat_grad, head[...])
    out_round = out_grad.astype(BF16)

    for i in range(HID // 256):
        at = slice(256 * i, 256 * i + 256)
        grad = dot_nt(out_round, down[at, :])
        pre = hidden_pre[:, at]
        slope = normal_cdf(pre) + pre * jnp.exp(-0.5 * pre * pre) * 0.3989422804014327
        pre_grad[:, at] = (grad * slope).astype(BF16)

    normed_grad = dot_nt(pre_grad[...], up[...])
    unit_grad = normed_grad * gain
    embed_grad = out_grad + inverse * (
        unit_grad
        - jnp.mean(unit_grad, axis=-1, keepdims=True)
        - unit_rows * jnp.mean(unit_grad * unit_rows, axis=-1, keepdims=True)
    )
    colour_grad = dot_nt(embed_grad.astype(BF16), patch[...]).astype(BF16)
    outs = (out0_ref, out1_ref, out2_ref, out3_ref)
    scatter_patches(me, dot_nt(colour_grad, order[...]), strips, outs)


def pose(own, parts, frames, counts, key_rows, key_cols, key_vis, gain, up, down, patch, head, position):
    return pl.pallas_call(
        pose_kernel,
        in_specs=[SMEM] + [VMEM] * 13 + [ANYWHERE] * 4,
        out_specs=[VMEM] * GROUP,
        out_shape=[jax.ShapeDtypeStruct((8, 16, COLS), BF16)] * GROUP,
        scratch_shapes=[
            pltpu.VMEM((768, 768), BF16),
            pltpu.VMEM((768, DP), BF16),
            pltpu.VMEM((HEAD, DP), BF16),
            pltpu.VMEM((64, DP), BF16),
            pltpu.VMEM((GROUP, 8, 16, COLS), F32),
            pltpu.VMEM((32, HEAD), F32),
            pltpu.VMEM((64, HID), F32),
            pltpu.VMEM((64, HID), BF16),
            pltpu.VMEM((64, HID), BF16),
            pltpu.SemaphoreType.DMA((4,)),
        ],
        compiler_params=megabytes(20),
        cost_estimate=pl.CostEstimate(
            flops=2 * 64 * 15800000, bytes_accessed=17 * 1024 * 1024, transcendentals=64 * HID * 3
        ),
        name="pose",
    )(
        own,
        *parts,
        frames,
        counts,
        key_rows,
        key_cols,
        key_vis,
        jnp.asarray(KEY_SPREAD),
        gain,
        up,
        down,
        jnp.asarray(PIXEL_ORDER),
        patch,
        head,
        position,
    )


def strip_kernel(own_ref, x0_ref, x1_ref, x2_ref, x3_ref, out_ref, inside_ref, across_ref):
    me = lax.rem(own_ref[0], GROUP)
    first = sublanes_of((8, 8, COLS)) < 4
    for turn, ref in enumerate((x0_ref, x1_ref, x2_ref, x3_ref)):
        frames = pl.ds(pl.multiple_of(lax.rem(me + GROUP - turn, GROUP) * 8, 8), 8)
        value = ref[...].astype(F32)
        groups = [value[:, :8], roll(value[:, :8], 4, 1), value[:, 8:]]
        for o in range(3):
            out_ref[frames, o] = roll(jnp.where(first, groups[o], 0.0), 1, 1)
    even = is_even(own_ref)
    for o in range(3):
        upper, lower = out_ref[:, o, 1, :], out_ref[:, o, 4, :]
        inside_ref[o] = jnp.where(even, lower, upper).astype(BF16)
        across_ref[o] = jnp.where(even, upper, lower).astype(BF16)


def strip_grads(own, parts):
    rim = jax.ShapeDtypeStruct((3, 32, COLS), BF16)
    return pl.pallas_call(
        strip_kernel,
        in_specs=[SMEM] + [VMEM] * GROUP,
        out_specs=[VMEM] * 3,
        out_shape=[jax.ShapeDtypeStruct((32, 3, 8, COLS), F32), rim, rim],
        compiler_params=megabytes(4),
        name="strip_grads",
    )(own, *parts)


def whole_kernel(place_ref, x_ref, inside_ref, across_ref, out_ref, first_ref):
    row = sublanes_of((32, 8, COLS))
    top, bottom = place_ref[0] == 0, place_ref[0] == place_ref[2] - 1
    even = is_even(place_ref)
    for o in range(3):
        inside, across = inside_ref[o].astype(F32), across_ref[o].astype(F32)
        above = unless(top, jnp.where(even, across, inside))
        below = unless(bottom, jnp.where(even, inside, across))
        value = jnp.where(row == 0, above[:, None, :], x_ref[:, o])
        value = jnp.where(row == 5, below[:, None, :], value)
        out_ref[:, o] = value
        first_ref[:, o] = value[:2]


def whole_grads(place, x, inside, across):
    return pl.pallas_call(
        whole_kernel,
        in_specs=[SMEM] + [VMEM] * 3,
        out_specs=[VMEM] * 2,
        out_shape=[
            jax.ShapeDtypeStruct(x.shape, F32),
            jax.ShapeDtypeStruct((2, 3, 8, COLS), F32),
        ],
        compiler_params=megabytes(4),
        name="whole_grads",
    )(place, x, inside, across)


def frame_taps(groups):
    row = sublanes_of((8, COLS))
    taps = [from_right(g) for g in groups] + list(groups) + [from_left(g) for g in groups]
    last = taps.pop()
    for i in range(3):
        taps[i] = jnp.where(row >= 6, roll(last, 6 - 2 * i, 0), taps[i])
    return taps


def pair_taps(ref, frame):
    rows = []
    for f in range(2):
        rows += frame_taps([ref[frame + f, o] for o in range(3)])
    return jnp.concatenate(rows, axis=0).T


def prepare_kernel(start, feat_ref, gain_ref, mean_ref, slope_ref, normed_ref):
    half_gain = 0.5 * gain_ref[...]
    mean_pair = mean_ref[...]
    places = [(tau, r) for tau in range(2) for r in range(ROWS)]

    @pl.loop(0, slope_ref.shape[0] // 2)
    def _(pair):
        xs = [feat_ref[start + 2 * pair + tau, r].astype(F32) for tau, r in places]
        means = channel_means([x * x for x in xs], mean_pair)
        for x, mean, (tau, r) in zip(xs, means, places):
            rescale = lax.rsqrt(mean + NORM_EPS)
            normed = x * rescale
            half_pre = normed * half_gain
            tanh = jnp.tanh(half_pre)
            slope = (1.0 + tanh) * (1.0 + half_pre * (1.0 - tanh)) * half_gain
            slope_ref[2 * pair + tau, r] = (slope * rescale).astype(BF16)
            normed_ref[2 * pair + tau, r] = normed.astype(BF16)


def prepare(start, count, features, gain, mean_pair):
    kept = pltpu.VMEM((count, ROWS, COLS, CH), BF16)
    return pl.pallas_call(
        functools.partial(prepare_kernel, start),
        in_specs=[VMEM] * 3,
        out_specs=[VMEM] * 2,
        out_shape=[kept] * 2,
        compiler_params=megabytes(8),
        cost_estimate=pl.CostEstimate(
            flops=10**9, bytes_accessed=10**5 * count, transcendentals=65536 * count
        ),
        name="prepare_%d" % start,
    )(features, gain, mean_pair)


def back_pair(kept, frame, taps, weight, mean_pair, store):
    slope_ref, normed_ref = kept
    grads = dot(taps, weight)
    places = [(tau, r) for tau in range(2) for r in range(ROWS)]
    for part in range(0, len(places), BACK_ROWS):
        group = places[part : part + BACK_ROWS]
        pairs = []
        for i, (tau, r) in enumerate(group):
            at = CH * (part + i)
            scaled = grads[:, at : at + CH] * slope_ref[frame + tau, r].astype(F32)
            pairs.append((scaled, normed_ref[frame + tau, r].astype(F32)))
        along = channel_means([scaled * normed for scaled, normed in pairs], mean_pair)
        for (scaled, normed), mean, (tau, r) in zip(pairs, along, group):
            store(tau, r, (scaled - normed * mean).astype(BF16))


def back_kernel(*refs):
    kept = refs[:-7]
    grad_ref, mean_ref, weight_ref, out_hbm, buffer, carry, sems = refs[-7:]
    mean_pair = mean_ref[...]
    carry[...] = pair_taps(grad_ref, 0)
    last_pair = grad_ref.shape[0] - 2
    copies = []
    for step in range(len(kept) // 2):
        base = step * BACK_FRAMES
        count = min(BACK_FRAMES, last_pair - base)
        slot = step % 2
        if step >= 2:
            copies[step - 2].wait()
        for pair in range(count // 2):
            now = carry[...]
            later = pair_taps(grad_ref, base + 2 * pair + 2)
            carry[...] = later
            taps = jnp.concatenate([now, later], axis=1).astype(BF16)

            def store(tau, r, value):
                buffer[slot, 2 * pair + tau, r] = value

            back_pair(kept[2 * step : 2 * step + 2], 2 * pair, taps, weight_ref[...], mean_pair, store)
        copies.append(
            pltpu.make_async_copy(
                buffer.at[slot, :count], out_hbm.at[base : base + count], sems.at[slot]
            )
        )
        copies[-1].start()
    for copy in copies[-2:]:
        copy.wait()


def last_kernel(
    place_ref, slope_ref, normed_ref, grad_ref, next_ref, mean_ref, weight_ref, prior_hbm,
    out_hbm, buffer, sem,
):
    del prior_hbm
    frame = grad_ref.shape[0] - 2
    last_block = place_ref[1] == place_ref[3] - 1
    later = unless(last_block, pair_taps(next_ref, 0))
    taps = jnp.concatenate([pair_taps(grad_ref, frame), later], axis=1).astype(BF16)

    def store(tau, r, value):
        buffer[tau, r] = value

    kept = (slope_ref, normed_ref)
    back_pair(kept, BACK_FRAMES - 2, taps, weight_ref[...], mean_ref[...], store)
    copy = pltpu.make_async_copy(buffer, out_hbm.at[frame:], sem)
    copy.start()
    copy.wait()


def conv_backward(place, kept, grads, later, mean_pair, weight):
    out_shape = jax.ShapeDtypeStruct((grads.shape[0], ROWS, COLS, CH), BF16)
    part = pl.pallas_call(
        back_kernel,
        in_specs=[VMEM] * (len(kept) * 2 + 3),
        out_specs=ANYWHERE,
        out_shape=out_shape,
        scratch_shapes=[
            pltpu.VMEM((2, BACK_FRAMES, ROWS, COLS, CH), BF16),
            pltpu.VMEM((COLS, 128), F32),
            pltpu.SemaphoreType.DMA((2,)),
        ],
        compiler_params=megabytes(16),
        cost_estimate=pl.CostEstimate(
            flops=2 * 16384 * 1024, bytes_accessed=9 * 1024 * 1024, transcendentals=2 * 2097152
        ),
        name="conv_back",
    )(*[x for pair in kept for x in pair], grads, mean_pair, weight)
    return pl.pallas_call(
        last_kernel,
        in_specs=[SMEM] + [VMEM] * 6 + [ANYWHERE],
        out_specs=ANYWHERE,
        out_shape=out_shape,
        input_output_aliases={7: 0},
        scratch_shapes=[pltpu.VMEM((2, ROWS, COLS, CH), BF16), pltpu.SemaphoreType.DMA],
        compiler_params=megabytes(12),
        name="conv_last",
    )(place, *kept[-1], grads, later, mean_pair, weight, part)


def per_device(
    features,
    norm_gain,
    conv_weight,
    colour_bias,
    observed_frames,
    observed_counts,
    key_rows,
    key_columns,
    key_visible,
    position_table,
    patch_weight,
    layer_gain,
    up_weight,
    down_weight,
    head_weight,
):
    tm_count = lax.axis_size("tm")
    own = jnp.stack(
        [
            lax.axis_index("tile"),
            lax.axis_index("tm"),
            jnp.int32(lax.axis_size("tile")),
            jnp.int32(tm_count),
        ]
    )
    gain = norm_gain.reshape(1, CH)
    features, layer_gain, own = lax.optimization_barrier(
        (features, layer_gain.reshape(DP // 128, 128), own)
    )
    features = pltpu.with_memory_space_constraint(features, pltpu.HBM)
    up_weight = pltpu.with_memory_space_constraint(up_weight, pltpu.HBM)
    down_weight = pltpu.with_memory_space_constraint(down_weight, pltpu.HBM)
    gain = pltpu.with_memory_space_constraint(gain, pltpu.HBM)
    consts = [jnp.asarray(x) for x in (MEAN_PAIR, SELECTOR, SELECTOR_T)]
    mean_pair, sel, sel_t = [pltpu.with_memory_space_constraint(x, pltpu.HBM) for x in consts]
    conv_weight = pltpu.with_memory_space_constraint(conv_weight.T, pltpu.HBM)
    tail, features, weight, weight_t, mean_pair, gain = conv_tail(
        features, gain, mean_pair, conv_weight, sel, sel_t
    )
    prior = lax.ppermute(tail, "tm", [(i, (i + 1) % tm_count) for i in range(tm_count)])
    sums, up, down = conv_main(features, gain, mean_pair, weight, up_weight, down_weight)
    def prepare_beside(chunk, *moving):
        kept.append(prepare(chunk * BACK_FRAMES, BACK_FRAMES, features, gain, mean_pair))
        *moving, kept[-1] = lax.optimization_barrier((*moving, kept[-1]))
        return moving

    kept = []
    rim_sums = prepare_beside(0, *swap_rims(*rims(own, sums, prior)))
    parts = swap_turns(colours(own, colour_bias, sums, prior, *rim_sums))
    parts = prepare_beside(1, *parts)
    parts = pose(
        own,
        parts,
        observed_frames.transpose(2, 0, 1),
        observed_counts,
        key_rows.T,
        key_columns.T,
        key_visible.T,
        layer_gain,
        up,
        down,
        patch_weight,
        head_weight.T,
        position_table,
    )
    grads, inside, across = strip_grads(own, prepare_beside(2, *swap_turns(parts)))
    rim_grads = prepare_beside(3, *swap_rims(inside, across))
    grads, first = whole_grads(own, grads, *rim_grads)
    later = lax.ppermute(first, "tm", [((i + 1) % tm_count, i) for i in range(tm_count)])
    return conv_backward(own, kept, grads, later, mean_pair, weight_t)


def solution(mesh):
    in_specs = (
        P("tm", "tile", None, None),
        P(),
        P(),
        P(),
        P("tm", None, None),
        P("tm", None),
        P("tm", None),
        P("tm", None),
        P("tm", None),
        P(),
        P(),
        P(),
        P(),
        P(),
        P(),
    )
    return jax.shard_map(
        per_device,
        mesh=mesh,
        in_specs=in_specs,
        out_specs=P("tm", "tile", None, None),
        check_vma=False,
    )
```

```python
import functools

import jax
import jax.numpy as jnp
import ml_dtypes
import numpy as np
from jax import lax
from jax.experimental import pallas as pl
from jax.experimental.pallas import tpu as pltpu
from jax.sharding import PartitionSpec as P

CH = 128
DP = 1280
HID = 2560
PATCH = 16
KP = 17
HEAD = 272
COLS = 128
ROWS = 4
GROUP = 4
FORWARD_FRAMES = 16
BACK_FRAMES = 8
BACK_ROWS = 4
NORM_EPS = 1e-06
F32 = jnp.float32
BF16 = jnp.bfloat16


def slot_of(c, o, k):
    group = 3 * c + o
    if group < 8:
        return 8 * group + k
    return 8 * (k // 2) + 6 + k % 2


def make_selector():
    table = np.zeros((81, 2, ROWS, 256), np.float32)
    for tau in range(2):
        for r in range(ROWS):
            for f in range(4):
                a = tau + 2 - f
                if not 0 <= a <= 2:
                    continue
                for k in range(6):
                    b = r + 2 - k
                    if not 0 <= b <= 2:
                        continue
                    for c in range(3):
                        for o in range(3):
                            table[3 * (9 * a + 3 * b + c) + o, tau, r, 64 * f + slot_of(c, o, k)] = 1
    return table.reshape(81, 2048)


def make_pixel_order():
    table = np.zeros((768, 768), np.float32)
    for o in range(3):
        for pixel in range(256):
            table[256 * o + pixel, 3 * pixel + o] = 1
    return table


def make_key_spread():
    table = np.zeros((KP, HEAD), np.float32)
    table[np.arange(HEAD) % KP, np.arange(HEAD)] = 1
    return table


SELECTOR = make_selector().astype(ml_dtypes.bfloat16)
SELECTOR_T = np.ascontiguousarray(make_selector().T).astype(ml_dtypes.bfloat16)
PIXEL_ORDER = make_pixel_order().astype(ml_dtypes.bfloat16)
PIXEL_ORDER_T = np.ascontiguousarray(make_pixel_order().T).astype(ml_dtypes.bfloat16)
KEY_SPREAD = make_key_spread().astype(ml_dtypes.bfloat16)
MEAN_PAIR = (np.kron(np.eye(2), np.ones((CH, CH))) / CH).astype(ml_dtypes.bfloat16)


def dot(a, b):
    return jnp.dot(a, b, preferred_element_type=F32)


def dot_tn(a, b):
    return lax.dot_general(a, b, (((0,), (0,)), ((), ())), preferred_element_type=F32)


def dot_nt(a, b):
    return lax.dot_general(a, b, (((1,), (1,)), ((), ())), preferred_element_type=F32)


def roll(x, shift, axis):
    shift %= x.shape[axis]
    return pltpu.roll(x, shift, axis) if shift else x


def channel_means(values, mean_pair):
    rounded = [value.astype(BF16) for value in values]
    pairs = [jnp.concatenate(rounded[i : i + 2], axis=1) for i in range(0, len(values), 2)]
    means = dot(jnp.concatenate(pairs, axis=0), mean_pair)
    out = []
    for i in range(len(pairs)):
        rows = slice(COLS * i, COLS * i + COLS)
        out += [means[rows, :CH], means[rows, CH:]]
    return out


def lanes_of(shape):
    return lax.broadcasted_iota(jnp.int32, shape, len(shape) - 1)


def sublanes_of(shape):
    return lax.broadcasted_iota(jnp.int32, shape, len(shape) - 2)


def from_left(x):
    return jnp.where(lanes_of(x.shape) >= 1, roll(x, 1, x.ndim - 1), 0.0)


def from_right(x):
    return jnp.where(lanes_of(x.shape) < COLS - 1, roll(x, -1, x.ndim - 1), 0.0)


def activated_rows(feat_ref, frame, half_gain, mean_pair):
    xs = [feat_ref[frame, r].astype(F32) for r in range(ROWS)]
    acts = []
    for x, mean in zip(xs, channel_means([x * x for x in xs], mean_pair)):
        half = x * lax.rsqrt(mean + NORM_EPS) * half_gain
        acts.append((half + half * jnp.tanh(half)).astype(BF16))
    return acts


def frame_sums(taps, out_ref, frame):
    groups = [taps[8 * g : 8 * g + 8] for g in range(8)]
    row = sublanes_of((8, COLS))
    groups.append(
        jnp.where(
            row < 2,
            roll(groups[0], 2, 0),
            jnp.where(row < 4, roll(groups[1], 4, 0), roll(groups[2], 6, 0)),
        )
    )
    for o in range(3):
        out_ref[frame, o] = from_left(groups[o]) + groups[3 + o] + from_right(groups[6 + o])


def pair_sums(feat_ref, frame, half_gain, mean_pair, weight):
    acts = []
    for tau in range(2):
        acts += activated_rows(feat_ref, frame + tau, half_gain, mean_pair)
    return dot(jnp.concatenate(acts, axis=1), weight)


def tail_kernel(
    feat_hbm, gain_hbm, mean_hbm, conv_hbm, sel_hbm, sel_t_hbm,
    out_ref, feat_ref, weight_ref, weight_t_ref, mean_ref, gain_ref,
    conv_ref, sel_ref, sel_t_ref, sems,
):
    frames = feat_hbm.shape[0]
    last = pltpu.make_async_copy(feat_hbm.at[frames - 2 :], feat_ref.at[frames - 2 :], sems.at[0])
    rest = pltpu.make_async_copy(feat_hbm.at[: frames - 2], feat_ref.at[: frames - 2], sems.at[1])
    small = [
        pltpu.make_async_copy(src, dst, sems.at[2 + i])
        for i, (src, dst) in enumerate(
            (
                (conv_hbm, conv_ref),
                (sel_hbm, sel_ref),
                (sel_t_hbm, sel_t_ref),
                (gain_hbm, gain_ref),
                (mean_hbm, mean_ref),
            )
        )
    ]
    for copy in small:
        copy.start()
    last.start()
    rest.start()
    for copy in small:
        copy.wait()
    conv = conv_ref[...]
    for i in range(8):
        at = slice(CH * i, CH * i + CH)
        wide = slice(256 * i, 256 * i + 256)
        weight_ref[at, :] = dot_tn(conv, sel_ref[:, wide]).astype(BF16)
        weight_t_ref[:, at] = dot(sel_t_ref[wide, :], conv).astype(BF16)
    last.wait()
    sums = pair_sums(feat_ref, frames - 2, 0.5 * gain_ref[...], mean_ref[...], weight_ref[:, 128:])
    taps = sums.T
    for f in range(2):
        frame_sums(taps[64 * f : 64 * f + 64], out_ref, f)
    rest.wait()


def conv_kernel(
    feat_ref, gain_ref, mean_ref, weight_ref, up_hbm, down_hbm, out_ref, up_ref, down_ref, carry, sems
):
    copies = [
        pltpu.make_async_copy(up_hbm, up_ref, sems.at[0]),
        pltpu.make_async_copy(down_hbm, down_ref, sems.at[1]),
    ]
    for copy in copies:
        copy.start()
    carry[...] = jnp.zeros_like(carry)
    half_gain = 0.5 * gain_ref[...]
    mean_pair = mean_ref[...]

    @pl.loop(0, feat_ref.shape[0] // FORWARD_FRAMES)
    def _(step):
        for pair in range(FORWARD_FRAMES // 2):
            frame = step * FORWARD_FRAMES + 2 * pair
            sums = pair_sums(feat_ref, frame, half_gain, mean_pair, weight_ref[...])
            taps = (sums[:, :128] + carry[...]).T
            carry[...] = sums[:, 128:]
            for f in range(2):
                frame_sums(taps[64 * f : 64 * f + 64], out_ref, frame + f)

    for copy in copies:
        copy.wait()


VMEM = pl.BlockSpec(memory_space=pltpu.VMEM)
SMEM = pl.BlockSpec(memory_space=pltpu.SMEM)
ANYWHERE = pl.BlockSpec(memory_space=pl.ANY)


def megabytes(count):
    return pltpu.CompilerParams(vmem_limit_bytes=count * 1024 * 1024)


def conv_tail(features, *small):
    return pl.pallas_call(
        tail_kernel,
        in_specs=[ANYWHERE] * 6,
        out_specs=[VMEM] * 6,
        out_shape=[
            jax.ShapeDtypeStruct((2, 3, 8, COLS), F32),
            pltpu.VMEM(features.shape, BF16),
            pltpu.VMEM((1024, 256), BF16),
            pltpu.VMEM((256, 1024), BF16),
            pltpu.VMEM((256, 256), BF16),
            pltpu.VMEM((1, CH), F32),
        ],
        scratch_shapes=[
            pltpu.VMEM((81, CH), BF16),
            pltpu.VMEM((81, 2048), BF16),
            pltpu.VMEM((2048, 81), BF16),
            pltpu.SemaphoreType.DMA((7,)),
        ],
        compiler_params=megabytes(8),
        name="conv_tail",
    )(
        features, *small
    )


def conv_main(features, gain, mean_pair, weight, up, down):
    return pl.pallas_call(
        conv_kernel,
        in_specs=[VMEM] * 4 + [ANYWHERE] * 2,
        out_specs=[VMEM, ANYWHERE, ANYWHERE],
        out_shape=[
            jax.ShapeDtypeStruct((features.shape[0], 3, 8, COLS), F32),
            pltpu.VMEM(up.shape, BF16),
            pltpu.VMEM(down.shape, BF16),
        ],
        scratch_shapes=[pltpu.VMEM((COLS, 128), F32), pltpu.SemaphoreType.DMA((2,))],
        compiler_params=megabytes(12),
        cost_estimate=pl.CostEstimate(
            flops=2 * 16384 * 1024, bytes_accessed=20 * 1024 * 1024, transcendentals=2 * 2097152
        ),
        name="conv_main",
    )(features, gain, mean_pair, weight, up, down)


def lay_rows(groups):
    row = sublanes_of(groups[0].shape)
    both = jnp.where(row < 4, groups[0], roll(groups[1], 4, 1))
    return jnp.concatenate([both, groups[2]], axis=1)


def unless(is_edge, value):
    return jnp.where(is_edge, jnp.zeros_like(value), value)


def is_even(place_ref):
    return lax.rem(place_ref[0], 2) == 0


def rim_kernel(place_ref, sums_ref, prior_ref, inside_ref, across_ref, up, down):
    first_block = place_ref[1] == 0
    for o in range(3):
        for k, out_ref in ((0, up), (5, down)):
            out_ref[o] = sums_ref[:, o, k, :]
            out_ref[o, 0:2] = sums_ref[0:2, o, k, :] + unless(first_block, prior_ref[:, o, k, :])
    even = is_even(place_ref)
    inside_ref[...] = jnp.where(even, down[...], up[...]).astype(BF16)
    across_ref[...] = jnp.where(even, up[...], down[...]).astype(BF16)


def rims(place, sums, prior):
    shape = jax.ShapeDtypeStruct((3, sums.shape[0], COLS), BF16)
    return pl.pallas_call(
        rim_kernel,
        in_specs=[SMEM] + [VMEM] * 2,
        out_specs=[VMEM] * 2,
        out_shape=[shape] * 2,
        scratch_shapes=[pltpu.VMEM(shape.shape, F32)] * 2,
        compiler_params=megabytes(4),
        name="rims",
    )(place, sums, prior)


def colour_kernel(own_ref, bias_ref, sums_ref, prior_ref, inside_ref, across_ref, *rest):
    out_refs, (total, above_rim, below_rim) = rest[:GROUP], rest[GROUP:]
    total[...] = sums_ref[...]
    total[0:2] = sums_ref[0:2] + unless(own_ref[1] == 0, prior_ref[...])
    top, bottom = own_ref[0] == 0, own_ref[0] == own_ref[2] - 1
    row = sublanes_of((8, 8, COLS))
    me = lax.rem(own_ref[0], GROUP)
    even = is_even(own_ref)
    inside, across = inside_ref[...].astype(F32), across_ref[...].astype(F32)
    above_rim[...] = unless(top, jnp.where(even, across, inside))
    below_rim[...] = unless(bottom, jnp.where(even, inside, across))
    for turn in range(GROUP):
        frames = pl.ds(pl.multiple_of(lax.rem(me + turn, GROUP) * 8, 8), 8)
        groups = []
        for o in range(3):
            value = total[frames, o]
            value += jnp.where(row == 1, above_rim[o, frames, :][:, None, :], 0.0)
            value += jnp.where(row == 4, below_rim[o, frames, :][:, None, :], 0.0)
            groups.append(roll(value, -1, 1) + bias_ref[o])
        out_refs[turn][...] = lay_rows(groups).astype(BF16)


def colours(own, bias, sums, prior, inside, across):
    shape = jax.ShapeDtypeStruct((8, 16, COLS), BF16)
    return pl.pallas_call(
        colour_kernel,
        in_specs=[SMEM] * 2 + [VMEM] * 4,
        out_specs=[VMEM] * GROUP,
        out_shape=[shape] * GROUP,
        scratch_shapes=[pltpu.VMEM(sums.shape, F32)]
        + [pltpu.VMEM((3, sums.shape[0], COLS), F32)] * 2,
        compiler_params=megabytes(4),
        name="colours",
    )(own, bias, sums, prior, inside, across)


def swap_turns(parts):
    count = lax.axis_size("tile")
    out = [parts[0]]
    for turn in range(1, GROUP):
        pairs = [(i, i - i % GROUP + (i + turn) % GROUP) for i in range(count)]
        out.append(lax.ppermute(parts[turn], "tile", pairs))
    return out


def swap_rims(inside, across):
    count = lax.axis_size("tile")
    pairs = [(i, i + 1 - 2 * (i % 2)) for i in range(count)]
    others = [(i, min(max(i - 1 + 2 * (i % 2), 0), count - 1)) for i in range(count)]
    return lax.ppermute(inside, "tile", pairs), lax.ppermute(across, "tile", others)


def swap_blocks(x):
    row, group = sublanes_of(x.shape), lanes_of(x.shape) // 16
    for bit in (4, 2, 1):
        low = (row & bit) == 0
        same = low == ((group & bit) == 0)
        moved = jnp.where(
            low,
            roll(roll(x, -bit, 1), 16 * bit, 2),
            roll(roll(x, bit, 1), -16 * bit, 2),
        )
        x = jnp.where(same, x, moved)
    return x


def gather_patches(me, x_refs, strips):
    for turn in range(GROUP):
        strips[lax.rem(me + GROUP - turn, GROUP)] = x_refs[turn][...].astype(F32)
    first = sublanes_of((8, 8, COLS)) < 4
    pieces = [[], [], []]
    for half in range(2):
        even, odd = strips[2 * half], strips[2 * half + 1]
        pieces[0].append(jnp.where(first, even[:, :8], roll(odd[:, :8], 4, 1)))
        pieces[1].append(jnp.where(first, roll(even[:, :8], 4, 1), odd[:, :8]))
        pieces[2].append(jnp.where(first, even[:, 8:], roll(odd[:, 8:], 4, 1)))
    ordered = [swap_blocks(piece).reshape(64, 128) for group in pieces for piece in group]
    return jnp.concatenate(ordered, axis=1).astype(BF16)


def scatter_patches(me, grad, strips, out_refs):
    rows = [swap_blocks(grad[:, 128 * i : 128 * i + 128].reshape(8, 8, 128)) for i in range(6)]
    for half in range(2):
        groups = [rows[2 * o + half] for o in range(3)]
        strips[2 * half] = lay_rows(groups)
        strips[2 * half + 1] = lay_rows([roll(group, 4, 1) for group in groups])
    for turn in range(GROUP):
        out_refs[turn][...] = strips[lax.rem(me + turn, GROUP)].astype(BF16)


def normal_cdf(x):
    return 0.5 * (1.0 + lax.erf(x * 0.7071067811865476))


def pose_kernel(
    own_ref,
    x0_ref,
    x1_ref,
    x2_ref,
    x3_ref,
    frames_ref,
    counts_ref,
    key_rows_ref,
    key_cols_ref,
    key_vis_ref,
    key_spread_ref,
    gain_ref,
    up,
    down,
    order,
    patch,
    head,
    position,
    order_t,
    out0_ref,
    out1_ref,
    out2_ref,
    out3_ref,
    strips,
    key_table,
    hidden_pre,
    hidden,
    pre_grad,
):
    token_row = own_ref[0] // GROUP
    me = lax.rem(own_ref[0], GROUP)
    first_frame = pl.multiple_of(me * 8, 8)

    frame = sublanes_of((8, 32)) + first_frame
    hit = jnp.zeros((8, 32), F32)
    for slot in range(3):
        used = frames_ref[slot] == frame
        hit = jnp.maximum(hit, jnp.where(used & (counts_ref[...] > slot), 1.0, 0.0))
    weight = jnp.max(hit, axis=1, keepdims=True)
    spread = key_spread_ref[...]

    def own_keys(ref):
        key_table[...] = dot_tn(ref[...].astype(F32).astype(BF16), spread)
        return key_table[pl.ds(first_frame, 8), :]

    def by_token(value):
        return jnp.broadcast_to(value[:, None, :], (8, 8, HEAD)).reshape(64, HEAD)

    token_column = sublanes_of((64, HEAD)) % 8
    column = lanes_of((64, HEAD))
    pixel_row = token_row * 4 + column // (4 * KP)
    pixel_col = token_column * 4 + (column // KP) % 4
    row_gap = pixel_row.astype(F32) - by_token(own_keys(key_rows_ref))
    col_gap = pixel_col.astype(F32) - by_token(own_keys(key_cols_ref))
    target = jnp.exp((row_gap * row_gap + col_gap * col_gap) * -0.125)
    mask = by_token(own_keys(key_vis_ref) * weight)

    raw = gather_patches(me, (x0_ref, x1_ref, x2_ref, x3_ref), strips)
    patches = dot(raw, order[...]).astype(BF16)
    pair_rows = pl.ds(pl.multiple_of(token_row // 2 * 16, 16), 16)
    two = position[pair_rows, :].astype(F32)
    places = jnp.where(lax.rem(token_row, 2) == 0, two[:8], two[8:])
    places = jnp.broadcast_to(places[None], (8, 8, DP)).reshape(64, DP)
    embedded = dot(patches, patch[...]) + places
    centred = embedded - jnp.mean(embedded, axis=-1, keepdims=True)
    inverse = lax.rsqrt(jnp.mean(centred * centred, axis=-1, keepdims=True) + NORM_EPS)
    unit_rows = centred * inverse
    gain = jnp.concatenate([gain_ref[i : i + 1] for i in range(DP // 128)], axis=1)
    normed_tokens = (unit_rows * gain).astype(BF16)

    for i in range(HID // 256):
        at = slice(256 * i, 256 * i + 256)
        value = dot(normed_tokens, up[:, at])
        hidden_pre[:, at] = value
        hidden[:, at] = (value * normal_cdf(value)).astype(BF16)

    block = dot(hidden[...], down[...])
    block_round = (embedded + block).astype(BF16)
    heatmap = dot_nt(block_round, head[...])
    heat_grad = ((heatmap - target) * mask).astype(BF16)
    out_grad = dot(heat_grad, head[...])
    out_round = out_grad.astype(BF16)

    for i in range(HID // 256):
        at = slice(256 * i, 256 * i + 256)
        grad = dot_nt(out_round, down[at, :])
        pre = hidden_pre[:, at]
        slope = normal_cdf(pre) + pre * jnp.exp(-0.5 * pre * pre) * 0.3989422804014327
        pre_grad[:, at] = (grad * slope).astype(BF16)

    normed_grad = dot_nt(pre_grad[...], up[...])
    unit_grad = normed_grad * gain
    embed_grad = out_grad + inverse * (
        unit_grad
        - jnp.mean(unit_grad, axis=-1, keepdims=True)
        - unit_rows * jnp.mean(unit_grad * unit_rows, axis=-1, keepdims=True)
    )
    colour_grad = dot_nt(embed_grad.astype(BF16), patch[...]).astype(BF16)
    outs = (out0_ref, out1_ref, out2_ref, out3_ref)
    scatter_patches(me, dot(colour_grad, order_t[...]), strips, outs)


def pose(own, parts, frames, counts, key_rows, key_cols, key_vis, gain, up, down, patch, head, position):
    return pl.pallas_call(
        pose_kernel,
        in_specs=[SMEM] + [VMEM] * 18,
        out_specs=[VMEM] * GROUP,
        out_shape=[jax.ShapeDtypeStruct((8, 16, COLS), BF16)] * GROUP,
        scratch_shapes=[
            pltpu.VMEM((GROUP, 8, 16, COLS), F32),
            pltpu.VMEM((32, HEAD), F32),
            pltpu.VMEM((64, HID), F32),
            pltpu.VMEM((64, HID), BF16),
            pltpu.VMEM((64, HID), BF16),
        ],
        compiler_params=megabytes(20),
        cost_estimate=pl.CostEstimate(
            flops=2 * 64 * 15800000, bytes_accessed=17 * 1024 * 1024, transcendentals=64 * HID * 3
        ),
        name="pose",
    )(
        own,
        *parts,
        frames,
        counts,
        key_rows,
        key_cols,
        key_vis,
        jnp.asarray(KEY_SPREAD),
        gain,
        up,
        down,
        jnp.asarray(PIXEL_ORDER),
        patch,
        head,
        position,
        jnp.asarray(PIXEL_ORDER_T),
    )


def strip_kernel(own_ref, x0_ref, x1_ref, x2_ref, x3_ref, out_ref, inside_ref, across_ref):
    me = lax.rem(own_ref[0], GROUP)
    first = sublanes_of((8, 8, COLS)) < 4
    for turn, ref in enumerate((x0_ref, x1_ref, x2_ref, x3_ref)):
        frames = pl.ds(pl.multiple_of(lax.rem(me + GROUP - turn, GROUP) * 8, 8), 8)
        value = ref[...].astype(F32)
        groups = [value[:, :8], roll(value[:, :8], 4, 1), value[:, 8:]]
        for o in range(3):
            out_ref[frames, o] = roll(jnp.where(first, groups[o], 0.0), 1, 1)
    even = is_even(own_ref)
    for o in range(3):
        upper, lower = out_ref[:, o, 1, :], out_ref[:, o, 4, :]
        inside_ref[o] = jnp.where(even, lower, upper).astype(BF16)
        across_ref[o] = jnp.where(even, upper, lower).astype(BF16)


def strip_grads(own, parts):
    rim = jax.ShapeDtypeStruct((3, 32, COLS), BF16)
    return pl.pallas_call(
        strip_kernel,
        in_specs=[SMEM] + [VMEM] * GROUP,
        out_specs=[VMEM] * 3,
        out_shape=[jax.ShapeDtypeStruct((32, 3, 8, COLS), F32), rim, rim],
        compiler_params=megabytes(4),
        name="strip_grads",
    )(own, *parts)


def whole_kernel(place_ref, x_ref, inside_ref, across_ref, out_ref, first_ref):
    row = sublanes_of((32, 8, COLS))
    top, bottom = place_ref[0] == 0, place_ref[0] == place_ref[2] - 1
    even = is_even(place_ref)
    for o in range(3):
        inside, across = inside_ref[o].astype(F32), across_ref[o].astype(F32)
        above = unless(top, jnp.where(even, across, inside))
        below = unless(bottom, jnp.where(even, inside, across))
        value = jnp.where(row == 0, above[:, None, :], x_ref[:, o])
        value = jnp.where(row == 5, below[:, None, :], value)
        out_ref[:, o] = value
        first_ref[:, o] = value[:2]


def whole_grads(place, x, inside, across):
    return pl.pallas_call(
        whole_kernel,
        in_specs=[SMEM] + [VMEM] * 3,
        out_specs=[VMEM] * 2,
        out_shape=[
            jax.ShapeDtypeStruct(x.shape, F32),
            jax.ShapeDtypeStruct((2, 3, 8, COLS), F32),
        ],
        compiler_params=megabytes(4),
        name="whole_grads",
    )(place, x, inside, across)


def frame_taps(groups):
    row = sublanes_of((8, COLS))
    taps = [from_right(g) for g in groups] + list(groups) + [from_left(g) for g in groups]
    last = taps.pop()
    for i in range(3):
        taps[i] = jnp.where(row >= 6, roll(last, 6 - 2 * i, 0), taps[i])
    return taps


def pair_taps(ref, frame):
    rows = []
    for f in range(2):
        rows += frame_taps([ref[frame + f, o] for o in range(3)])
    return jnp.concatenate(rows, axis=0).T


def prepare_kernel(start, feat_ref, gain_ref, mean_ref, slope_ref, normed_ref):
    half_gain = 0.5 * gain_ref[...]
    mean_pair = mean_ref[...]
    places = [(tau, r) for tau in range(2) for r in range(ROWS)]

    for pair in range(slope_ref.shape[0] // 2):
        xs = [feat_ref[start + 2 * pair + tau, r].astype(F32) for tau, r in places]
        means = channel_means([x * x for x in xs], mean_pair)
        for x, mean, (tau, r) in zip(xs, means, places):
            rescale = lax.rsqrt(mean + NORM_EPS)
            normed = x * rescale
            half_pre = normed * half_gain
            tanh = jnp.tanh(half_pre)
            slope = (1.0 + tanh) * (1.0 + half_pre * (1.0 - tanh)) * half_gain
            slope_ref[2 * pair + tau, r] = (slope * rescale).astype(BF16)
            normed_ref[2 * pair + tau, r] = normed.astype(BF16)


def prepare(start, count, features, gain, mean_pair):
    kept = pltpu.VMEM((count, ROWS, COLS, CH), BF16)
    return pl.pallas_call(
        functools.partial(prepare_kernel, start),
        in_specs=[VMEM] * 3,
        out_specs=[VMEM] * 2,
        out_shape=[kept] * 2,
        compiler_params=megabytes(8),
        cost_estimate=pl.CostEstimate(
            flops=10**9, bytes_accessed=10**5 * count, transcendentals=65536 * count
        ),
        name="prepare_%d" % start,
    )(features, gain, mean_pair)


def back_pair(kept, frame, taps, weight, mean_pair, store):
    slope_ref, normed_ref = kept
    grads = dot(taps, weight)
    places = [(tau, r) for tau in range(2) for r in range(ROWS)]
    for part in range(0, len(places), BACK_ROWS):
        group = places[part : part + BACK_ROWS]
        pairs = []
        for i, (tau, r) in enumerate(group):
            at = CH * (part + i)
            scaled = grads[:, at : at + CH] * slope_ref[frame + tau, r].astype(F32)
            pairs.append((scaled, normed_ref[frame + tau, r].astype(F32)))
        along = channel_means([scaled * normed for scaled, normed in pairs], mean_pair)
        for (scaled, normed), mean, (tau, r) in zip(pairs, along, group):
            store(tau, r, (scaled - normed * mean).astype(BF16))


def back_kernel(*refs):
    kept = refs[:-7]
    grad_ref, mean_ref, weight_ref, out_hbm, buffer, carry, sems = refs[-7:]
    mean_pair = mean_ref[...]
    carry[...] = pair_taps(grad_ref, 0)
    last_pair = grad_ref.shape[0] - 2
    copies = []
    for step in range(len(kept) // 2):
        base = step * BACK_FRAMES
        count = min(BACK_FRAMES, last_pair - base)
        slot = step % 2
        if step >= 2:
            copies[step - 2].wait()
        for pair in range(count // 2):
            now = carry[...]
            later = pair_taps(grad_ref, base + 2 * pair + 2)
            carry[...] = later
            taps = jnp.concatenate([now, later], axis=1).astype(BF16)

            def store(tau, r, value):
                buffer[slot, 2 * pair + tau, r] = value

            back_pair(kept[2 * step : 2 * step + 2], 2 * pair, taps, weight_ref[...], mean_pair, store)
        copies.append(
            pltpu.make_async_copy(
                buffer.at[slot, :count], out_hbm.at[base : base + count], sems.at[slot]
            )
        )
        copies[-1].start()
    for copy in copies[-2:]:
        copy.wait()


def last_kernel(
    place_ref, slope_ref, normed_ref, grad_ref, next_ref, mean_ref, weight_ref, prior_hbm,
    out_hbm, buffer, sem,
):
    del prior_hbm
    frame = grad_ref.shape[0] - 2
    last_block = place_ref[1] == place_ref[3] - 1
    later = unless(last_block, pair_taps(next_ref, 0))
    taps = jnp.concatenate([pair_taps(grad_ref, frame), later], axis=1).astype(BF16)

    def store(tau, r, value):
        buffer[tau, r] = value

    kept = (slope_ref, normed_ref)
    back_pair(kept, BACK_FRAMES - 2, taps, weight_ref[...], mean_ref[...], store)
    copy = pltpu.make_async_copy(buffer, out_hbm.at[frame:], sem)
    copy.start()
    copy.wait()


def conv_backward(place, kept, grads, later, mean_pair, weight):
    out_shape = jax.ShapeDtypeStruct((grads.shape[0], ROWS, COLS, CH), BF16)
    part = pl.pallas_call(
        back_kernel,
        in_specs=[VMEM] * (len(kept) * 2 + 3),
        out_specs=ANYWHERE,
        out_shape=out_shape,
        scratch_shapes=[
            pltpu.VMEM((2, BACK_FRAMES, ROWS, COLS, CH), BF16),
            pltpu.VMEM((COLS, 128), F32),
            pltpu.SemaphoreType.DMA((2,)),
        ],
        compiler_params=megabytes(16),
        cost_estimate=pl.CostEstimate(
            flops=2 * 16384 * 1024, bytes_accessed=9 * 1024 * 1024, transcendentals=2 * 2097152
        ),
        name="conv_back",
    )(*[x for pair in kept for x in pair], grads, mean_pair, weight)
    return pl.pallas_call(
        last_kernel,
        in_specs=[SMEM] + [VMEM] * 6 + [ANYWHERE],
        out_specs=ANYWHERE,
        out_shape=out_shape,
        input_output_aliases={7: 0},
        scratch_shapes=[pltpu.VMEM((2, ROWS, COLS, CH), BF16), pltpu.SemaphoreType.DMA],
        compiler_params=megabytes(12),
        name="conv_last",
    )(place, *kept[-1], grads, later, mean_pair, weight, part)


def per_device(
    features,
    norm_gain,
    conv_weight,
    colour_bias,
    observed_frames,
    observed_counts,
    key_rows,
    key_columns,
    key_visible,
    position_table,
    patch_weight,
    layer_gain,
    up_weight,
    down_weight,
    head_weight,
):
    tm_count = lax.axis_size("tm")
    own = jnp.stack(
        [
            lax.axis_index("tile"),
            lax.axis_index("tm"),
            jnp.int32(lax.axis_size("tile")),
            jnp.int32(tm_count),
        ]
    )
    gain = norm_gain.reshape(1, CH)
    features, layer_gain, own = lax.optimization_barrier(
        (features, layer_gain.reshape(DP // 128, 128), own)
    )
    features = pltpu.with_memory_space_constraint(features, pltpu.HBM)
    up_weight = pltpu.with_memory_space_constraint(up_weight, pltpu.HBM)
    down_weight = pltpu.with_memory_space_constraint(down_weight, pltpu.HBM)
    gain = pltpu.with_memory_space_constraint(gain, pltpu.HBM)
    consts = [jnp.asarray(x) for x in (MEAN_PAIR, SELECTOR, SELECTOR_T)]
    mean_pair, sel, sel_t = [pltpu.with_memory_space_constraint(x, pltpu.HBM) for x in consts]
    conv_weight = pltpu.with_memory_space_constraint(conv_weight.T, pltpu.HBM)
    tail, features, weight, weight_t, mean_pair, gain = conv_tail(
        features, gain, mean_pair, conv_weight, sel, sel_t
    )
    prior = lax.ppermute(tail, "tm", [(i, (i + 1) % tm_count) for i in range(tm_count)])
    sums, up, down = conv_main(features, gain, mean_pair, weight, up_weight, down_weight)
    def prepare_beside(chunk, *moving):
        kept.append(prepare(chunk * BACK_FRAMES, BACK_FRAMES, features, gain, mean_pair))
        *moving, kept[-1] = lax.optimization_barrier((*moving, kept[-1]))
        return moving

    kept = []
    rim_sums = prepare_beside(0, *swap_rims(*rims(own, sums, prior)))
    parts = swap_turns(colours(own, colour_bias, sums, prior, *rim_sums))
    parts = prepare_beside(1, *parts)
    parts = pose(
        own,
        parts,
        observed_frames.transpose(2, 0, 1),
        observed_counts,
        key_rows.T,
        key_columns.T,
        key_visible.T,
        layer_gain,
        up,
        down,
        patch_weight,
        head_weight.T,
        position_table,
    )
    grads, inside, across = strip_grads(own, prepare_beside(2, *swap_turns(parts)))
    rim_grads = prepare_beside(3, *swap_rims(inside, across))
    grads, first = whole_grads(own, grads, *rim_grads)
    later = lax.ppermute(first, "tm", [((i + 1) % tm_count, i) for i in range(tm_count)])
    return conv_backward(own, kept, grads, later, mean_pair, weight_t)


def solution(mesh):
    in_specs = (
        P("tm", "tile", None, None),
        P(),
        P(),
        P(),
        P("tm", None, None),
        P("tm", None),
        P("tm", None),
        P("tm", None),
        P("tm", None),
        P(),
        P(),
        P(),
        P(),
        P(),
        P(),
    )
    return jax.shard_map(
        per_device,
        mesh=mesh,
        in_specs=in_specs,
        out_specs=P("tm", "tile", None, None),
        check_vma=False,
    )
```

```python
import functools

import jax
import jax.numpy as jnp
import ml_dtypes
import numpy as np
from jax import lax
from jax.experimental import pallas as pl
from jax.experimental.pallas import tpu as pltpu
from jax.sharding import PartitionSpec as P

CH = 128
DP = 1280
HID = 2560
PATCH = 16
KP = 17
HEAD = 272
COLS = 128
ROWS = 4
GROUP = 4
FORWARD_FRAMES = 16
BACK_FRAMES = 8
BACK_ROWS = 8
NORM_EPS = 1e-06
F32 = jnp.float32
BF16 = jnp.bfloat16


def slot_of(c, o, k):
    group = 3 * c + o
    if group < 8:
        return 8 * group + k
    return 8 * (k // 2) + 6 + k % 2


def make_selector():
    table = np.zeros((81, 2, ROWS, 256), np.float32)
    for tau in range(2):
        for r in range(ROWS):
            for f in range(4):
                a = tau + 2 - f
                if not 0 <= a <= 2:
                    continue
                for k in range(6):
                    b = r + 2 - k
                    if not 0 <= b <= 2:
                        continue
                    for c in range(3):
                        for o in range(3):
                            table[3 * (9 * a + 3 * b + c) + o, tau, r, 64 * f + slot_of(c, o, k)] = 1
    return table.reshape(81, 2048)


def make_pixel_order():
    table = np.zeros((768, 768), np.float32)
    for o in range(3):
        for pixel in range(256):
            table[256 * o + pixel, 3 * pixel + o] = 1
    return table


def make_key_spread():
    table = np.zeros((KP, HEAD), np.float32)
    table[np.arange(HEAD) % KP, np.arange(HEAD)] = 1
    return table


SELECTOR = make_selector().astype(ml_dtypes.bfloat16)
SELECTOR_T = np.ascontiguousarray(make_selector().T).astype(ml_dtypes.bfloat16)
PIXEL_ORDER = make_pixel_order().astype(ml_dtypes.bfloat16)
PIXEL_ORDER_T = np.ascontiguousarray(make_pixel_order().T).astype(ml_dtypes.bfloat16)
KEY_SPREAD = make_key_spread().astype(ml_dtypes.bfloat16)
MEAN_PAIR = (np.kron(np.eye(2), np.ones((CH, CH))) / CH).astype(ml_dtypes.bfloat16)


def dot(a, b):
    return jnp.dot(a, b, preferred_element_type=F32)


def dot_tn(a, b):
    return lax.dot_general(a, b, (((0,), (0,)), ((), ())), preferred_element_type=F32)


def dot_nt(a, b):
    return lax.dot_general(a, b, (((1,), (1,)), ((), ())), preferred_element_type=F32)


def roll(x, shift, axis):
    shift %= x.shape[axis]
    return pltpu.roll(x, shift, axis) if shift else x


def channel_means(values, mean_pair):
    rounded = [value.astype(BF16) for value in values]
    pairs = [jnp.concatenate(rounded[i : i + 2], axis=1) for i in range(0, len(values), 2)]
    means = dot(jnp.concatenate(pairs, axis=0), mean_pair)
    out = []
    for i in range(len(pairs)):
        rows = slice(COLS * i, COLS * i + COLS)
        out += [means[rows, :CH], means[rows, CH:]]
    return out


def lanes_of(shape):
    return lax.broadcasted_iota(jnp.int32, shape, len(shape) - 1)


def sublanes_of(shape):
    return lax.broadcasted_iota(jnp.int32, shape, len(shape) - 2)


def from_left(x):
    return jnp.where(lanes_of(x.shape) >= 1, roll(x, 1, x.ndim - 1), 0.0)


def from_right(x):
    return jnp.where(lanes_of(x.shape) < COLS - 1, roll(x, -1, x.ndim - 1), 0.0)


def activated_rows(feat_ref, frame, half_gain, mean_pair):
    xs = [feat_ref[frame, r].astype(F32) for r in range(ROWS)]
    acts = []
    for x, mean in zip(xs, channel_means([x * x for x in xs], mean_pair)):
        half = x * lax.rsqrt(mean + NORM_EPS) * half_gain
        acts.append((half + half * jnp.tanh(half)).astype(BF16))
    return acts


def frame_sums(taps, out_ref, frame):
    groups = [taps[8 * g : 8 * g + 8] for g in range(8)]
    row = sublanes_of((8, COLS))
    groups.append(
        jnp.where(
            row < 2,
            roll(groups[0], 2, 0),
            jnp.where(row < 4, roll(groups[1], 4, 0), roll(groups[2], 6, 0)),
        )
    )
    for o in range(3):
        out_ref[frame, o] = from_left(groups[o]) + groups[3 + o] + from_right(groups[6 + o])


def pair_sums(feat_ref, frame, half_gain, mean_pair, weight):
    acts = []
    for tau in range(2):
        acts += activated_rows(feat_ref, frame + tau, half_gain, mean_pair)
    return dot(jnp.concatenate(acts, axis=1), weight)


def tail_kernel(
    feat_hbm, gain_hbm, mean_hbm, conv_hbm, sel_hbm, sel_t_hbm,
    out_ref, feat_ref, weight_ref, weight_t_ref, mean_ref, gain_ref,
    conv_ref, sel_ref, sel_t_ref, sems,
):
    frames = feat_hbm.shape[0]
    last = pltpu.make_async_copy(feat_hbm.at[frames - 2 :], feat_ref.at[frames - 2 :], sems.at[0])
    rest = pltpu.make_async_copy(feat_hbm.at[: frames - 2], feat_ref.at[: frames - 2], sems.at[1])
    small = [
        pltpu.make_async_copy(src, dst, sems.at[2 + i])
        for i, (src, dst) in enumerate(
            (
                (conv_hbm, conv_ref),
                (sel_hbm, sel_ref),
                (sel_t_hbm, sel_t_ref),
                (gain_hbm, gain_ref),
                (mean_hbm, mean_ref),
            )
        )
    ]
    for copy in small:
        copy.start()
    last.start()
    rest.start()
    for copy in small:
        copy.wait()
    conv = conv_ref[...]
    for i in range(8):
        at = slice(CH * i, CH * i + CH)
        wide = slice(256 * i, 256 * i + 256)
        weight_ref[at, :] = dot_tn(conv, sel_ref[:, wide]).astype(BF16)
        weight_t_ref[:, at] = dot(sel_t_ref[wide, :], conv).astype(BF16)
    last.wait()
    sums = pair_sums(feat_ref, frames - 2, 0.5 * gain_ref[...], mean_ref[...], weight_ref[:, 128:])
    taps = sums.T
    for f in range(2):
        frame_sums(taps[64 * f : 64 * f + 64], out_ref, f)
    rest.wait()


def conv_kernel(
    feat_ref, gain_ref, mean_ref, weight_ref, up_hbm, down_hbm, out_ref, up_ref, down_ref, carry, sems
):
    copies = [
        pltpu.make_async_copy(up_hbm, up_ref, sems.at[0]),
        pltpu.make_async_copy(down_hbm, down_ref, sems.at[1]),
    ]
    for copy in copies:
        copy.start()
    carry[...] = jnp.zeros_like(carry)
    half_gain = 0.5 * gain_ref[...]
    mean_pair = mean_ref[...]

    @pl.loop(0, feat_ref.shape[0] // FORWARD_FRAMES)
    def _(step):
        for pair in range(FORWARD_FRAMES // 2):
            frame = step * FORWARD_FRAMES + 2 * pair
            sums = pair_sums(feat_ref, frame, half_gain, mean_pair, weight_ref[...])
            taps = (sums[:, :128] + carry[...]).T
            carry[...] = sums[:, 128:]
            for f in range(2):
                frame_sums(taps[64 * f : 64 * f + 64], out_ref, frame + f)

    for copy in copies:
        copy.wait()


VMEM = pl.BlockSpec(memory_space=pltpu.VMEM)
SMEM = pl.BlockSpec(memory_space=pltpu.SMEM)
ANYWHERE = pl.BlockSpec(memory_space=pl.ANY)


def megabytes(count):
    return pltpu.CompilerParams(vmem_limit_bytes=count * 1024 * 1024)


def conv_tail(features, *small):
    return pl.pallas_call(
        tail_kernel,
        in_specs=[ANYWHERE] * 6,
        out_specs=[VMEM] * 6,
        out_shape=[
            jax.ShapeDtypeStruct((2, 3, 8, COLS), F32),
            pltpu.VMEM(features.shape, BF16),
            pltpu.VMEM((1024, 256), BF16),
            pltpu.VMEM((256, 1024), BF16),
            pltpu.VMEM((256, 256), BF16),
            pltpu.VMEM((1, CH), F32),
        ],
        scratch_shapes=[
            pltpu.VMEM((81, CH), BF16),
            pltpu.VMEM((81, 2048), BF16),
            pltpu.VMEM((2048, 81), BF16),
            pltpu.SemaphoreType.DMA((7,)),
        ],
        compiler_params=megabytes(8),
        name="conv_tail",
    )(
        features, *small
    )


def conv_main(features, gain, mean_pair, weight, up, down):
    return pl.pallas_call(
        conv_kernel,
        in_specs=[VMEM] * 4 + [ANYWHERE] * 2,
        out_specs=[VMEM, ANYWHERE, ANYWHERE],
        out_shape=[
            jax.ShapeDtypeStruct((features.shape[0], 3, 8, COLS), F32),
            pltpu.VMEM(up.shape, BF16),
            pltpu.VMEM(down.shape, BF16),
        ],
        scratch_shapes=[pltpu.VMEM((COLS, 128), F32), pltpu.SemaphoreType.DMA((2,))],
        compiler_params=megabytes(12),
        cost_estimate=pl.CostEstimate(
            flops=2 * 16384 * 1024, bytes_accessed=20 * 1024 * 1024, transcendentals=2 * 2097152
        ),
        name="conv_main",
    )(features, gain, mean_pair, weight, up, down)


def lay_rows(groups):
    row = sublanes_of(groups[0].shape)
    both = jnp.where(row < 4, groups[0], roll(groups[1], 4, 1))
    return jnp.concatenate([both, groups[2]], axis=1)


def unless(is_edge, value):
    return jnp.where(is_edge, jnp.zeros_like(value), value)


def is_even(place_ref):
    return lax.rem(place_ref[0], 2) == 0


def rim_kernel(place_ref, sums_ref, prior_ref, inside_ref, across_ref, up, down):
    first_block = place_ref[1] == 0
    for o in range(3):
        for k, out_ref in ((0, up), (5, down)):
            out_ref[o] = sums_ref[:, o, k, :]
            out_ref[o, 0:2] = sums_ref[0:2, o, k, :] + unless(first_block, prior_ref[:, o, k, :])
    even = is_even(place_ref)
    inside_ref[...] = jnp.where(even, down[...], up[...]).astype(BF16)
    across_ref[...] = jnp.where(even, up[...], down[...]).astype(BF16)


def rims(place, sums, prior):
    shape = jax.ShapeDtypeStruct((3, sums.shape[0], COLS), BF16)
    return pl.pallas_call(
        rim_kernel,
        in_specs=[SMEM] + [VMEM] * 2,
        out_specs=[VMEM] * 2,
        out_shape=[shape] * 2,
        scratch_shapes=[pltpu.VMEM(shape.shape, F32)] * 2,
        compiler_params=megabytes(4),
        name="rims",
    )(place, sums, prior)


def colour_kernel(own_ref, bias_ref, sums_ref, prior_ref, inside_ref, across_ref, *rest):
    out_refs, (total, above_rim, below_rim) = rest[:GROUP], rest[GROUP:]
    total[...] = sums_ref[...]
    total[0:2] = sums_ref[0:2] + unless(own_ref[1] == 0, prior_ref[...])
    top, bottom = own_ref[0] == 0, own_ref[0] == own_ref[2] - 1
    row = sublanes_of((8, 8, COLS))
    me = lax.rem(own_ref[0], GROUP)
    even = is_even(own_ref)
    inside, across = inside_ref[...].astype(F32), across_ref[...].astype(F32)
    above_rim[...] = unless(top, jnp.where(even, across, inside))
    below_rim[...] = unless(bottom, jnp.where(even, inside, across))
    for turn in range(GROUP):
        frames = pl.ds(pl.multiple_of(lax.rem(me + turn, GROUP) * 8, 8), 8)
        groups = []
        for o in range(3):
            value = total[frames, o]
            value += jnp.where(row == 1, above_rim[o, frames, :][:, None, :], 0.0)
            value += jnp.where(row == 4, below_rim[o, frames, :][:, None, :], 0.0)
            groups.append(roll(value, -1, 1) + bias_ref[o])
        out_refs[turn][...] = lay_rows(groups).astype(BF16)


def colours(own, bias, sums, prior, inside, across):
    shape = jax.ShapeDtypeStruct((8, 16, COLS), BF16)
    return pl.pallas_call(
        colour_kernel,
        in_specs=[SMEM] * 2 + [VMEM] * 4,
        out_specs=[VMEM] * GROUP,
        out_shape=[shape] * GROUP,
        scratch_shapes=[pltpu.VMEM(sums.shape, F32)]
        + [pltpu.VMEM((3, sums.shape[0], COLS), F32)] * 2,
        compiler_params=megabytes(4),
        name="colours",
    )(own, bias, sums, prior, inside, across)


def swap_turns(parts):
    count = lax.axis_size("tile")
    out = [parts[0]]
    for turn in range(1, GROUP):
        pairs = [(i, i - i % GROUP + (i + turn) % GROUP) for i in range(count)]
        out.append(lax.ppermute(parts[turn], "tile", pairs))
    return out


def swap_rims(inside, across):
    count = lax.axis_size("tile")
    pairs = [(i, i + 1 - 2 * (i % 2)) for i in range(count)]
    others = [(i, min(max(i - 1 + 2 * (i % 2), 0), count - 1)) for i in range(count)]
    return lax.ppermute(inside, "tile", pairs), lax.ppermute(across, "tile", others)


def swap_blocks(x):
    row, group = sublanes_of(x.shape), lanes_of(x.shape) // 16
    for bit in (4, 2, 1):
        low = (row & bit) == 0
        same = low == ((group & bit) == 0)
        moved = jnp.where(
            low,
            roll(roll(x, -bit, 1), 16 * bit, 2),
            roll(roll(x, bit, 1), -16 * bit, 2),
        )
        x = jnp.where(same, x, moved)
    return x


def gather_patches(me, x_refs, strips):
    for turn in range(GROUP):
        strips[lax.rem(me + GROUP - turn, GROUP)] = x_refs[turn][...].astype(F32)
    first = sublanes_of((8, 8, COLS)) < 4
    pieces = [[], [], []]
    for half in range(2):
        even, odd = strips[2 * half], strips[2 * half + 1]
        pieces[0].append(jnp.where(first, even[:, :8], roll(odd[:, :8], 4, 1)))
        pieces[1].append(jnp.where(first, roll(even[:, :8], 4, 1), odd[:, :8]))
        pieces[2].append(jnp.where(first, even[:, 8:], roll(odd[:, 8:], 4, 1)))
    ordered = [swap_blocks(piece).reshape(64, 128) for group in pieces for piece in group]
    return jnp.concatenate(ordered, axis=1).astype(BF16)


def scatter_patches(me, grad, strips, out_refs):
    rows = [swap_blocks(grad[:, 128 * i : 128 * i + 128].reshape(8, 8, 128)) for i in range(6)]
    for half in range(2):
        groups = [rows[2 * o + half] for o in range(3)]
        strips[2 * half] = lay_rows(groups)
        strips[2 * half + 1] = lay_rows([roll(group, 4, 1) for group in groups])
    for turn in range(GROUP):
        out_refs[turn][...] = strips[lax.rem(me + turn, GROUP)].astype(BF16)


def normal_cdf(x):
    return 0.5 * (1.0 + lax.erf(x * 0.7071067811865476))


def pose_kernel(
    own_ref,
    x0_ref,
    x1_ref,
    x2_ref,
    x3_ref,
    frames_ref,
    counts_ref,
    key_rows_ref,
    key_cols_ref,
    key_vis_ref,
    key_spread_ref,
    gain_ref,
    up,
    down,
    order,
    patch,
    head,
    position,
    order_t,
    out0_ref,
    out1_ref,
    out2_ref,
    out3_ref,
    strips,
    key_table,
    hidden_pre,
    hidden,
    pre_grad,
):
    token_row = own_ref[0] // GROUP
    me = lax.rem(own_ref[0], GROUP)
    first_frame = pl.multiple_of(me * 8, 8)

    frame = sublanes_of((8, 32)) + first_frame
    hit = jnp.zeros((8, 32), F32)
    for slot in range(3):
        used = frames_ref[slot] == frame
        hit = jnp.maximum(hit, jnp.where(used & (counts_ref[...] > slot), 1.0, 0.0))
    weight = jnp.max(hit, axis=1, keepdims=True)
    spread = key_spread_ref[...]

    def own_keys(ref):
        key_table[...] = dot_tn(ref[...].astype(F32).astype(BF16), spread)
        return key_table[pl.ds(first_frame, 8), :]

    def by_token(value):
        return jnp.broadcast_to(value[:, None, :], (8, 8, HEAD)).reshape(64, HEAD)

    token_column = sublanes_of((64, HEAD)) % 8
    column = lanes_of((64, HEAD))
    pixel_row = token_row * 4 + column // (4 * KP)
    pixel_col = token_column * 4 + (column // KP) % 4
    row_gap = pixel_row.astype(F32) - by_token(own_keys(key_rows_ref))
    col_gap = pixel_col.astype(F32) - by_token(own_keys(key_cols_ref))
    target = jnp.exp((row_gap * row_gap + col_gap * col_gap) * -0.125)
    mask = by_token(own_keys(key_vis_ref) * weight)

    raw = gather_patches(me, (x0_ref, x1_ref, x2_ref, x3_ref), strips)
    patches = dot(raw, order[...]).astype(BF16)
    pair_rows = pl.ds(pl.multiple_of(token_row // 2 * 16, 16), 16)
    two = position[pair_rows, :].astype(F32)
    places = jnp.where(lax.rem(token_row, 2) == 0, two[:8], two[8:])
    places = jnp.broadcast_to(places[None], (8, 8, DP)).reshape(64, DP)
    embedded = dot(patches, patch[...]) + places
    centred = embedded - jnp.mean(embedded, axis=-1, keepdims=True)
    inverse = lax.rsqrt(jnp.mean(centred * centred, axis=-1, keepdims=True) + NORM_EPS)
    unit_rows = centred * inverse
    gain = jnp.concatenate([gain_ref[i : i + 1] for i in range(DP // 128)], axis=1)
    normed_tokens = (unit_rows * gain).astype(BF16)

    for i in range(HID // 256):
        at = slice(256 * i, 256 * i + 256)
        value = dot(normed_tokens, up[:, at])
        hidden_pre[:, at] = value
        hidden[:, at] = (value * normal_cdf(value)).astype(BF16)

    block = dot(hidden[...], down[...])
    block_round = (embedded + block).astype(BF16)
    heatmap = dot_nt(block_round, head[...])
    heat_grad = ((heatmap - target) * mask).astype(BF16)
    out_grad = dot(heat_grad, head[...])
    out_round = out_grad.astype(BF16)

    for i in range(HID // 256):
        at = slice(256 * i, 256 * i + 256)
        grad = dot_nt(out_round, down[at, :])
        pre = hidden_pre[:, at]
        slope = normal_cdf(pre) + pre * jnp.exp(-0.5 * pre * pre) * 0.3989422804014327
        pre_grad[:, at] = (grad * slope).astype(BF16)

    normed_grad = dot_nt(pre_grad[...], up[...])
    unit_grad = normed_grad * gain
    embed_grad = out_grad + inverse * (
        unit_grad
        - jnp.mean(unit_grad, axis=-1, keepdims=True)
        - unit_rows * jnp.mean(unit_grad * unit_rows, axis=-1, keepdims=True)
    )
    colour_grad = dot_nt(embed_grad.astype(BF16), patch[...]).astype(BF16)
    outs = (out0_ref, out1_ref, out2_ref, out3_ref)
    scatter_patches(me, dot(colour_grad, order_t[...]), strips, outs)


def pose(own, parts, frames, counts, key_rows, key_cols, key_vis, gain, up, down, patch, head, position):
    return pl.pallas_call(
        pose_kernel,
        in_specs=[SMEM] + [VMEM] * 18,
        out_specs=[VMEM] * GROUP,
        out_shape=[jax.ShapeDtypeStruct((8, 16, COLS), BF16)] * GROUP,
        scratch_shapes=[
            pltpu.VMEM((GROUP, 8, 16, COLS), F32),
            pltpu.VMEM((32, HEAD), F32),
            pltpu.VMEM((64, HID), F32),
            pltpu.VMEM((64, HID), BF16),
            pltpu.VMEM((64, HID), BF16),
        ],
        compiler_params=megabytes(20),
        cost_estimate=pl.CostEstimate(
            flops=2 * 64 * 15800000, bytes_accessed=17 * 1024 * 1024, transcendentals=64 * HID * 3
        ),
        name="pose",
    )(
        own,
        *parts,
        frames,
        counts,
        key_rows,
        key_cols,
        key_vis,
        jnp.asarray(KEY_SPREAD),
        gain,
        up,
        down,
        jnp.asarray(PIXEL_ORDER),
        patch,
        head,
        position,
        jnp.asarray(PIXEL_ORDER_T),
    )


def strip_kernel(own_ref, x0_ref, x1_ref, x2_ref, x3_ref, out_ref, inside_ref, across_ref):
    me = lax.rem(own_ref[0], GROUP)
    first = sublanes_of((8, 8, COLS)) < 4
    for turn, ref in enumerate((x0_ref, x1_ref, x2_ref, x3_ref)):
        frames = pl.ds(pl.multiple_of(lax.rem(me + GROUP - turn, GROUP) * 8, 8), 8)
        value = ref[...].astype(F32)
        groups = [value[:, :8], roll(value[:, :8], 4, 1), value[:, 8:]]
        for o in range(3):
            out_ref[frames, o] = roll(jnp.where(first, groups[o], 0.0), 1, 1)
    even = is_even(own_ref)
    for o in range(3):
        upper, lower = out_ref[:, o, 1, :], out_ref[:, o, 4, :]
        inside_ref[o] = jnp.where(even, lower, upper).astype(BF16)
        across_ref[o] = jnp.where(even, upper, lower).astype(BF16)


def strip_grads(own, parts):
    rim = jax.ShapeDtypeStruct((3, 32, COLS), BF16)
    return pl.pallas_call(
        strip_kernel,
        in_specs=[SMEM] + [VMEM] * GROUP,
        out_specs=[VMEM] * 3,
        out_shape=[jax.ShapeDtypeStruct((32, 3, 8, COLS), F32), rim, rim],
        compiler_params=megabytes(4),
        name="strip_grads",
    )(own, *parts)


def whole_kernel(place_ref, x_ref, inside_ref, across_ref, out_ref, first_ref):
    row = sublanes_of((32, 8, COLS))
    top, bottom = place_ref[0] == 0, place_ref[0] == place_ref[2] - 1
    even = is_even(place_ref)
    for o in range(3):
        inside, across = inside_ref[o].astype(F32), across_ref[o].astype(F32)
        above = unless(top, jnp.where(even, across, inside))
        below = unless(bottom, jnp.where(even, inside, across))
        value = jnp.where(row == 0, above[:, None, :], x_ref[:, o])
        value = jnp.where(row == 5, below[:, None, :], value)
        out_ref[:, o] = value
        first_ref[:, o] = value[:2]


def whole_grads(place, x, inside, across):
    return pl.pallas_call(
        whole_kernel,
        in_specs=[SMEM] + [VMEM] * 3,
        out_specs=[VMEM] * 2,
        out_shape=[
            jax.ShapeDtypeStruct(x.shape, F32),
            jax.ShapeDtypeStruct((2, 3, 8, COLS), F32),
        ],
        compiler_params=megabytes(4),
        name="whole_grads",
    )(place, x, inside, across)


def frame_taps(groups):
    row = sublanes_of((8, COLS))
    taps = [from_right(g) for g in groups] + list(groups) + [from_left(g) for g in groups]
    last = taps.pop()
    for i in range(3):
        taps[i] = jnp.where(row >= 6, roll(last, 6 - 2 * i, 0), taps[i])
    return taps


def pair_taps(ref, frame):
    rows = []
    for f in range(2):
        rows += frame_taps([ref[frame + f, o] for o in range(3)])
    return jnp.concatenate(rows, axis=0).T


def prepare_kernel(start, feat_ref, gain_ref, mean_ref, slope_ref, normed_ref):
    half_gain = 0.5 * gain_ref[...]
    mean_pair = mean_ref[...]
    places = [(tau, r) for tau in range(2) for r in range(ROWS)]

    for pair in range(slope_ref.shape[0] // 2):
        xs = [feat_ref[start + 2 * pair + tau, r].astype(F32) for tau, r in places]
        means = channel_means([x * x for x in xs], mean_pair)
        for x, mean, (tau, r) in zip(xs, means, places):
            rescale = lax.rsqrt(mean + NORM_EPS)
            normed = x * rescale
            half_pre = normed * half_gain
            tanh = jnp.tanh(half_pre)
            slope = (1.0 + tanh) * (1.0 + half_pre * (1.0 - tanh)) * half_gain
            slope_ref[2 * pair + tau, r] = (slope * rescale).astype(BF16)
            normed_ref[2 * pair + tau, r] = normed.astype(BF16)


def prepare(start, count, features, gain, mean_pair):
    kept = pltpu.VMEM((count, ROWS, COLS, CH), BF16)
    return pl.pallas_call(
        functools.partial(prepare_kernel, start),
        in_specs=[VMEM] * 3,
        out_specs=[VMEM] * 2,
        out_shape=[kept] * 2,
        compiler_params=megabytes(8),
        cost_estimate=pl.CostEstimate(
            flops=10**9, bytes_accessed=10**5 * count, transcendentals=65536 * count
        ),
        name="prepare_%d" % start,
    )(features, gain, mean_pair)


def back_pair(kept, frame, taps, weight, mean_pair, store):
    slope_ref, normed_ref = kept
    grads = dot(taps, weight)
    places = [(tau, r) for tau in range(2) for r in range(ROWS)]
    for part in range(0, len(places), BACK_ROWS):
        group = places[part : part + BACK_ROWS]
        pairs = []
        for i, (tau, r) in enumerate(group):
            at = CH * (part + i)
            scaled = grads[:, at : at + CH] * slope_ref[frame + tau, r].astype(F32)
            pairs.append((scaled, normed_ref[frame + tau, r].astype(F32)))
        along = channel_means([scaled * normed for scaled, normed in pairs], mean_pair)
        for (scaled, normed), mean, (tau, r) in zip(pairs, along, group):
            store(tau, r, (scaled - normed * mean).astype(BF16))


def back_kernel(*refs):
    kept = refs[:-7]
    grad_ref, mean_ref, weight_ref, out_hbm, buffer, carry, sems = refs[-7:]
    mean_pair = mean_ref[...]
    carry[...] = pair_taps(grad_ref, 0)
    last_pair = grad_ref.shape[0] - 2
    copies = []
    for step in range(len(kept) // 2):
        base = step * BACK_FRAMES
        count = min(BACK_FRAMES, last_pair - base)
        slot = step % 2
        if step >= 2:
            copies[step - 2].wait()
        for pair in range(count // 2):
            now = carry[...]
            later = pair_taps(grad_ref, base + 2 * pair + 2)
            carry[...] = later
            taps = jnp.concatenate([now, later], axis=1).astype(BF16)

            def store(tau, r, value):
                buffer[slot, 2 * pair + tau, r] = value

            back_pair(kept[2 * step : 2 * step + 2], 2 * pair, taps, weight_ref[...], mean_pair, store)
        copies.append(
            pltpu.make_async_copy(
                buffer.at[slot, :count], out_hbm.at[base : base + count], sems.at[slot]
            )
        )
        copies[-1].start()
    for copy in copies[-2:]:
        copy.wait()


def last_kernel(
    place_ref, slope_ref, normed_ref, grad_ref, next_ref, mean_ref, weight_ref, prior_hbm,
    out_hbm, buffer, sem,
):
    del prior_hbm
    frame = grad_ref.shape[0] - 2
    last_block = place_ref[1] == place_ref[3] - 1
    later = unless(last_block, pair_taps(next_ref, 0))
    taps = jnp.concatenate([pair_taps(grad_ref, frame), later], axis=1).astype(BF16)

    def store(tau, r, value):
        buffer[tau, r] = value

    kept = (slope_ref, normed_ref)
    back_pair(kept, BACK_FRAMES - 2, taps, weight_ref[...], mean_ref[...], store)
    copy = pltpu.make_async_copy(buffer, out_hbm.at[frame:], sem)
    copy.start()
    copy.wait()


def conv_backward(place, kept, grads, later, mean_pair, weight):
    out_shape = jax.ShapeDtypeStruct((grads.shape[0], ROWS, COLS, CH), BF16)
    part = pl.pallas_call(
        back_kernel,
        in_specs=[VMEM] * (len(kept) * 2 + 3),
        out_specs=ANYWHERE,
        out_shape=out_shape,
        scratch_shapes=[
            pltpu.VMEM((2, BACK_FRAMES, ROWS, COLS, CH), BF16),
            pltpu.VMEM((COLS, 128), F32),
            pltpu.SemaphoreType.DMA((2,)),
        ],
        compiler_params=megabytes(16),
        cost_estimate=pl.CostEstimate(
            flops=2 * 16384 * 1024, bytes_accessed=9 * 1024 * 1024, transcendentals=2 * 2097152
        ),
        name="conv_back",
    )(*[x for pair in kept for x in pair], grads, mean_pair, weight)
    return pl.pallas_call(
        last_kernel,
        in_specs=[SMEM] + [VMEM] * 6 + [ANYWHERE],
        out_specs=ANYWHERE,
        out_shape=out_shape,
        input_output_aliases={7: 0},
        scratch_shapes=[pltpu.VMEM((2, ROWS, COLS, CH), BF16), pltpu.SemaphoreType.DMA],
        compiler_params=megabytes(12),
        name="conv_last",
    )(place, *kept[-1], grads, later, mean_pair, weight, part)


def per_device(
    features,
    norm_gain,
    conv_weight,
    colour_bias,
    observed_frames,
    observed_counts,
    key_rows,
    key_columns,
    key_visible,
    position_table,
    patch_weight,
    layer_gain,
    up_weight,
    down_weight,
    head_weight,
):
    tm_count = lax.axis_size("tm")
    own = jnp.stack(
        [
            lax.axis_index("tile"),
            lax.axis_index("tm"),
            jnp.int32(lax.axis_size("tile")),
            jnp.int32(tm_count),
        ]
    )
    gain = norm_gain.reshape(1, CH)
    features, layer_gain, own = lax.optimization_barrier(
        (features, layer_gain.reshape(DP // 128, 128), own)
    )
    features = pltpu.with_memory_space_constraint(features, pltpu.HBM)
    up_weight = pltpu.with_memory_space_constraint(up_weight, pltpu.HBM)
    down_weight = pltpu.with_memory_space_constraint(down_weight, pltpu.HBM)
    gain = pltpu.with_memory_space_constraint(gain, pltpu.HBM)
    consts = [jnp.asarray(x) for x in (MEAN_PAIR, SELECTOR, SELECTOR_T)]
    mean_pair, sel, sel_t = [pltpu.with_memory_space_constraint(x, pltpu.HBM) for x in consts]
    conv_weight = pltpu.with_memory_space_constraint(conv_weight.T, pltpu.HBM)
    tail, features, weight, weight_t, mean_pair, gain = conv_tail(
        features, gain, mean_pair, conv_weight, sel, sel_t
    )
    prior = lax.ppermute(tail, "tm", [(i, (i + 1) % tm_count) for i in range(tm_count)])
    sums, up, down = conv_main(features, gain, mean_pair, weight, up_weight, down_weight)
    def prepare_beside(chunk, *moving):
        kept.append(prepare(chunk * BACK_FRAMES, BACK_FRAMES, features, gain, mean_pair))
        *moving, kept[-1] = lax.optimization_barrier((*moving, kept[-1]))
        return moving

    kept = []
    rim_sums = prepare_beside(0, *swap_rims(*rims(own, sums, prior)))
    parts = swap_turns(colours(own, colour_bias, sums, prior, *rim_sums))
    parts = prepare_beside(1, *parts)
    parts = pose(
        own,
        parts,
        observed_frames.transpose(2, 0, 1),
        observed_counts,
        key_rows.T,
        key_columns.T,
        key_visible.T,
        layer_gain,
        up,
        down,
        patch_weight,
        head_weight.T,
        position_table,
    )
    grads, inside, across = strip_grads(own, prepare_beside(2, *swap_turns(parts)))
    rim_grads = prepare_beside(3, *swap_rims(inside, across))
    grads, first = whole_grads(own, grads, *rim_grads)
    later = lax.ppermute(first, "tm", [((i + 1) % tm_count, i) for i in range(tm_count)])
    return conv_backward(own, kept, grads, later, mean_pair, weight_t)


def solution(mesh):
    in_specs = (
        P("tm", "tile", None, None),
        P(),
        P(),
        P(),
        P("tm", None, None),
        P("tm", None),
        P("tm", None),
        P("tm", None),
        P("tm", None),
        P(),
        P(),
        P(),
        P(),
        P(),
        P(),
    )
    return jax.shard_map(
        per_device,
        mesh=mesh,
        in_specs=in_specs,
        out_specs=P("tm", "tile", None, None),
        check_vma=False,
    )
```
